32 devices in a mesh: dp: 4 (over z), tensor: 8 (over y, x, core).
Axes of the slice: x: 2, y: 2, z: 4, core: 2. Of those that a mesh axis runs over, the one named last changes fastest.
Arguments:
- tokens: bfloat16 [1024, 4096], P('dp', 'tensor'), may hold values from -0.25 to 0.25
- small_weights: bfloat16 [2, 3328, 8960], P(None, ('dp', 'tensor')), may hold values from -6 to 6
- ffn_growth: bfloat16 [11008, 8960], P('tensor'), may hold values from -0.0625 to 0.0625
- width_growth: bfloat16 [4096, 3328], P('dp'), may hold values from -0.109375 to 0.109375
Outputs:
- grown_weights: bfloat16 [2, 4096, 11008], P(None, 'dp', 'tensor')
- hidden: bfloat16 [1024, 11008], P('dp', 'tensor')
The draws below stay inside these ranges and needn't reach their ends.
All inputs are finite; a program needn't handle non-finite values.
Results may differ from the reference program's by a relative error of at most 0.0071.
Values may be sent and summed in bfloat16 or wider, within the bound.
No kernel may reach another device: no remote copies, remote signals or barrier semaphores. Data moves between devices by JAX's collectives and lax.ppermute only.
A program may use at most 128 MiB of HBM per device.

```python
import jax
import jax.numpy as jnp
from jax import lax

DS = 3328
FS = 8960
DL = 4096
FL = 11008
TOKENS = 1024


def level_of(own_key, extent, cuts, smallest, largest):
    factor_of = 1.0
    for dim, shards_of in cuts:
        draws = jax.random.uniform(jax.random.fold_in(jax.random.fold_in(own_key, 6), dim), (shards_of,), jnp.float32, smallest / len(cuts), largest / len(cuts))
        factor_of = factor_of * jnp.repeat(jnp.exp(draws), extent[dim] // shards_of).reshape((-1,) + (1,) * (len(extent) - 1 - dim))
    return factor_of


def noise(rng, dims, width, most, shards=(), dtype=jnp.bfloat16):
    array = width * jax.random.normal(rng, dims, jnp.float32)
    if shards:
        array = array * level_of(rng, dims, shards, -0.22, 0.18)
    return jnp.clip(array, -most, most).astype(dtype)


def setup_inputs(seed: int = 0) -> dict:
    arg_keys = jax.random.split(jax.random.key(seed), 5)
    tokens = noise(arg_keys[0], (TOKENS, DL), (DL ** -0.5), 0.25, ((0, 4), (1, 8)))
    small_weights = noise(arg_keys[1], (2, DS, FS), 1.0, 6.0, ((1, 32),))
    ffn_growth = noise(arg_keys[2], (FL, FS), FS ** -0.5, 0.0625, ((0, 8),))
    width_growth = noise(arg_keys[3], (DL, DS), DS ** -0.5, 0.109375, ((0, 4),))
    return dict(tokens=tokens, small_weights=small_weights, ffn_growth=ffn_growth, width_growth=width_growth)


def reference(tokens, small_weights, ffn_growth, width_growth):
    def grow_one(single):
        panels = jnp.dot(single, ffn_growth.T, preferred_element_type=jnp.float32).astype(jnp.bfloat16)
        return jnp.dot(width_growth, panels, preferred_element_type=jnp.float32).astype(jnp.bfloat16)

    grown_weights = lax.map(grow_one, small_weights)
    pre_gate = jnp.dot(tokens, grown_weights[0], preferred_element_type=jnp.float32)
    pre_up = jnp.dot(tokens, grown_weights[1], preferred_element_type=jnp.float32)
    hidden = (jax.nn.silu(pre_gate) * pre_up).astype(jnp.bfloat16)
    return grown_weights, hidden
```

```python
import jax
import jax.numpy as jnp
from jax import lax
from jax.sharding import PartitionSpec as P

BF16, F32 = jnp.bfloat16, jnp.float32


def pieces(extent, width):
    starts = list(range(0, extent, width))
    return [(start, min(width, extent - start)) for start in starts]


def token_rows(tokens, width_growth):
    by_rows = lax.all_to_all(tokens, "tensor", 0, 1, tiled=True)
    by_features = lax.all_to_all(by_rows, "dp", 1, 0, tiled=True)
    part = jnp.dot(by_features, width_growth, preferred_element_type=F32)
    own = lax.psum_scatter(part, "dp", scatter_dimension=0, tiled=True).astype(BF16)
    return lax.all_gather(own, "tensor", axis=0, tiled=True)


def on_device(tokens, small_weights, ffn_growth, width_growth):
    columns = ffn_growth.shape[0]
    small = [lax.all_gather(small_weights[m], "tensor", axis=0, tiled=True) for m in range(2)]
    token_growth = token_rows(tokens, width_growth)
    grown, pre = [], []
    for m in range(2):
        grown_parts, pre_parts = [], []
        for start, width in pieces(columns, 512):
            panel = jnp.einsum(
                "sf,cf->sc", small[m], ffn_growth[start:start + width], preferred_element_type=F32
            ).astype(BF16)
            panels = lax.all_gather(panel, "dp", axis=0, tiled=True)
            grown_parts.append(jnp.dot(width_growth, panels, preferred_element_type=F32).astype(BF16))
            pre_parts.append(jnp.dot(token_growth, panels, preferred_element_type=F32))
        grown.append(jnp.concatenate(grown_parts, axis=1))
        pre.append(jnp.concatenate(pre_parts, axis=1))
    hidden = (jax.nn.silu(pre[0]) * pre[1]).astype(BF16)
    return (jnp.stack(grown), hidden)


def solution(mesh):
    placed = (P("dp", "tensor"), P(None, ("dp", "tensor"), None), P("tensor", None), P("dp", None))
    return jax.shard_map(
        on_device,
        mesh=mesh,
        in_specs=placed,
        out_specs=(P(None, "dp", "tensor"), P("dp", "tensor")),
        check_vma=False,
    )
```

```python
import jax
import jax.numpy as jnp
from jax import lax
from jax.sharding import PartitionSpec as P

BF16, F32 = jnp.bfloat16, jnp.float32
WIDTH = 512


def pieces(extent, width):
    starts = list(range(0, extent, width))
    return [(start, min(width, extent - start)) for start in starts]


def token_rows(tokens, width_growth):
    nd, nt = lax.axis_size("dp"), lax.axis_size("tensor")
    by_rows = lax.all_to_all(tokens, "tensor", 0, 1, tiled=True)
    by_features = lax.all_to_all(by_rows, "dp", 1, 0, tiled=True)
    part = jnp.dot(by_features, width_growth, preferred_element_type=F32).astype(BF16)
    parts = lax.all_to_all(part, "dp", 0, 0, tiled=True)
    own = jnp.sum(parts.reshape(nd, -1, parts.shape[1]).astype(F32), axis=0).astype(BF16)
    copies = jnp.broadcast_to(own[None], (nt,) + own.shape).reshape(-1, own.shape[1])
    return lax.all_to_all(copies, "tensor", 0, 0, tiled=True)


def panel_of(small, growth):
    return jnp.einsum("sf,cf->sc", small, growth, preferred_element_type=F32).astype(BF16)


def after(array, *made):
    return lax.optimization_barrier((array,) + made)[0]


def gathered_form(tokens, small_weights, ffn_growth, width_growth):
    columns = ffn_growth.shape[0]
    small = [lax.all_gather(small_weights[m], "tensor", axis=0, tiled=True) for m in range(2)]
    token_growth = token_rows(tokens, width_growth)
    grown, pre = [], []
    for m in range(2):
        grown_parts, pre_parts = [], []
        for start, width in pieces(columns, WIDTH):
            panel = panel_of(small[m], ffn_growth[start:start + width])
            panels = lax.all_gather(panel, "dp", axis=0, tiled=True)
            grown_parts.append(jnp.dot(width_growth, panels, preferred_element_type=F32).astype(BF16))
            pre_parts.append(jnp.dot(token_growth, panels, preferred_element_type=F32))
        grown.append(jnp.concatenate(grown_parts, axis=1))
        pre.append(jnp.concatenate(pre_parts, axis=1))
    hidden = (jax.nn.silu(pre[0]) * pre[1]).astype(BF16)
    return (jnp.stack(grown), hidden)


SWAP_INNER = [(1, 2), (2, 1)]
TO_INNER = [(0, 1), (3, 2)]
TO_OUTER = [(1, 0), (2, 3)]
ORDER = [[0, 1, 2, 3], [1, 2, 3, 0], [2, 1, 0, 3], [3, 2, 1, 0]]


def ordered_columns(array, block):
    order = jnp.array(ORDER, jnp.int32)[lax.axis_index("dp")]
    rows = array.shape[0]
    return jnp.concatenate(
        [lax.dynamic_slice(array, (0, order[b] * block), (rows, block)) for b in range(4)], axis=1
    )


def rows_of_outer(rows, block):
    nt = lax.axis_size("tensor")
    half = rows.shape[0] // 2
    core = lax.rem(lax.axis_index("tensor"), 2)
    mine = lax.dynamic_slice(rows, (core * half, block), (half, 3 * block))
    got = lax.ppermute(mine, "dp", TO_INNER)
    other = lax.ppermute(got, "tensor", [(j, j ^ 1) for j in range(nt)])
    first = jnp.where(core == 0, got, other)
    second = jnp.where(core == 0, other, got)
    return jnp.concatenate([first, second], axis=0)


def line_form(tokens, small_weights, ffn_growth, width_growth):
    columns = ffn_growth.shape[0]
    block = width_growth.shape[1] // 4
    own_rows = width_growth.shape[0]
    small = [lax.all_gather(small_weights[m], "tensor", axis=0, tiled=True) for m in range(2)]
    growth = ordered_columns(width_growth, block)
    growth_out = rows_of_outer(growth, block)
    token_growth = ordered_columns(token_rows(tokens, width_growth), block)
    token_growth_out = rows_of_outer(token_growth, block)
    rows = jnp.concatenate([growth, token_growth], axis=0)
    rows_out = jnp.concatenate([growth_out, token_growth_out], axis=0)

    work = [(m, start, width) for m in range(2) for start, width in pieces(columns, WIDTH)]
    count = len(work)
    own, outer, mate, far, out, received = ({} for _ in range(6))
    grown, pre = [[], []], [[], []]

    def send_panel(k):
        m, start, width = work[k]
        made = [own[k - 1]] if k else []
        made += [out[k - 3]] if k >= 3 else []
        own[k] = panel_of(after(small[m], *made), ffn_growth[start:start + width])
        sent = after(own[k], outer[k - 2]) if k >= 2 else own[k]
        outer[k] = lax.ppermute(sent, "dp", TO_INNER)
        mate[k] = lax.ppermute(sent, "dp", SWAP_INNER)

    def finish(k):
        m = work[k][0]
        panels = jnp.concatenate([own[k], mate[k], far[k], outer[k]], axis=0)
        sums = jnp.dot(after(rows, out[min(k + 1, count - 1)]), panels, preferred_element_type=F32)
        if k == count - 1:
            sums = lax.optimization_barrier(sums)
        sums = sums + received[k].astype(F32)
        grown[m].append(sums[:own_rows].astype(BF16))
        pre[m].append(sums[own_rows:])

    send_panel(0)
    send_panel(1)
    for k in range(count):
        far[k] = lax.ppermute(outer[k], "dp", SWAP_INNER)
        if k + 2 < count:
            send_panel(k + 2)
        panels = jnp.concatenate([own[k], mate[k], far[k]], axis=0)
        out[k] = jnp.dot(
            after(rows_out, own[min(k + 2, count - 1)]), panels, preferred_element_type=F32
        ).astype(BF16)
        received[k] = lax.ppermute(out[k], "dp", TO_OUTER)
        if k:
            finish(k - 1)
    finish(count - 1)
    pre = [jnp.concatenate(parts, axis=1) for parts in pre]
    hidden = (jax.nn.silu(pre[0]) * pre[1]).astype(BF16)
    return (jnp.stack([jnp.concatenate(parts, axis=1) for parts in grown]), hidden)


def solution(mesh):
    placed = (P("dp", "tensor"), P(None, ("dp", "tensor"), None), P("tensor", None), P("dp", None))
    return jax.shard_map(
        line_form if mesh.shape["dp"] == 4 else gathered_form,
        mesh=mesh,
        in_specs=placed,
        out_specs=(P(None, "dp", "tensor"), P("dp", "tensor")),
        check_vma=False,
    )
```

```python
import functools

import jax
import jax.numpy as jnp
from jax import lax
from jax.experimental import pallas as pl
from jax.experimental.pallas import tpu as pltpu
from jax.sharding import PartitionSpec as P

BF16, F32 = jnp.bfloat16, jnp.float32
WIDTH = 512
VMEM_LIMIT = 56 * 1024 * 1024
ANY = pl.BlockSpec(memory_space=pl.ANY)


def pieces(extent, width):
    starts = list(range(0, extent, width))
    return [(start, min(width, extent - start)) for start in starts]


def after(array, *made):
    return lax.optimization_barrier((array,) + made)[0]


def token_rows(tokens, width_growth):
    nd, nt = lax.axis_size("dp"), lax.axis_size("tensor")
    by_rows = lax.all_to_all(tokens, "tensor", 0, 1, tiled=True)
    by_features = lax.all_to_all(by_rows, "dp", 1, 0, tiled=True)
    part = jnp.dot(by_features, width_growth, preferred_element_type=F32).astype(BF16)
    parts = lax.all_to_all(part, "dp", 0, 0, tiled=True)
    own = jnp.sum(parts.reshape(nd, -1, parts.shape[1]).astype(F32), axis=0).astype(BF16)
    copies = jnp.broadcast_to(own[None], (nt,) + own.shape).reshape(-1, own.shape[1])
    return lax.all_to_all(copies, "tensor", 0, 0, tiled=True)


def gathered_form(tokens, small_weights, ffn_growth, width_growth):
    columns = ffn_growth.shape[0]
    small = [lax.all_gather(small_weights[m], "tensor", axis=0, tiled=True) for m in range(2)]
    token_growth = token_rows(tokens, width_growth)
    grown, pre = [], []
    for m in range(2):
        grown_parts, pre_parts = [], []
        for start, width in pieces(columns, WIDTH):
            panel = jnp.einsum(
                "sf,cf->sc", small[m], ffn_growth[start:start + width], preferred_element_type=F32
            ).astype(BF16)
            panels = lax.all_gather(panel, "dp", axis=0, tiled=True)
            grown_parts.append(jnp.dot(width_growth, panels, preferred_element_type=F32).astype(BF16))
            pre_parts.append(jnp.dot(token_growth, panels, preferred_element_type=F32))
        grown.append(jnp.concatenate(grown_parts, axis=1))
        pre.append(jnp.concatenate(pre_parts, axis=1))
    hidden = (jax.nn.silu(pre[0]) * pre[1]).astype(BF16)
    return (jnp.stack(grown), hidden)


SWAP_INNER = [(1, 2), (2, 1)]
TO_INNER = [(0, 1), (3, 2)]
TO_OUTER = [(1, 0), (2, 3)]
SLOTS = [[0, 1, 2, 3], [1, 0, 2, 3], [2, 3, 1, 0], [3, 0, 1, 2]]


def panel_kernel(steps, valid, small_ref, growth_ref, out_ref, acc_ref):
    step = pl.program_id(0)
    wide = out_ref.shape[1]
    part = lax.dot_general(
        small_ref[...], growth_ref[:wide, :], (((1,), (1,)), ((), ())), preferred_element_type=F32
    )

    @pl.when(step == 0)
    def _():
        acc_ref[...] = part

    @pl.when((step > 0) & (step < steps - 1))
    def _():
        acc_ref[...] += part

    @pl.when(step == steps - 1)
    def _():
        total = acc_ref[...] + part
        if valid < wide:
            column = lax.broadcasted_iota(jnp.int32, total.shape, 1)
            total = jnp.where(column < valid, total, 0.0)
        out_ref[...] = total.astype(BF16)


def panel_of(small, growth, start, width):
    rows, depth = small.shape
    wide = -(-width // 128) * 128
    steps = 7
    deep = depth // steps
    return pl.pallas_call(
        functools.partial(panel_kernel, steps, width),
        out_shape=jax.ShapeDtypeStruct((rows, wide), BF16),
        grid=(steps,),
        in_specs=[
            pl.BlockSpec((rows, deep), lambda k: (0, k)),
            pl.BlockSpec((WIDTH, deep), lambda k: (start // WIDTH, k)),
        ],
        out_specs=pl.BlockSpec((rows, wide), lambda k: (0, 0)),
        scratch_shapes=[pltpu.VMEM((rows, wide), F32)],
        compiler_params=pltpu.CompilerParams(vmem_limit_bytes=VMEM_LIMIT),
        cost_estimate=pl.CostEstimate(
            flops=2 * rows * depth * wide, bytes_accessed=2 * depth * (rows + wide), transcendentals=0
        ),
        name="panel",
    )(small, growth)


def gated(gate, up):
    return (gate / (1.0 + jnp.exp(-gate)) * up).astype(BF16)


def products_kernel(m, start, width, slots_ref, *refs):
    refs = list(refs)
    rows_out_ref, tokens_out_ref, rows_ref, tokens_ref = (refs.pop(0) for _ in range(4))
    own_ref, outer_ref, mate_ref, far_ref = (refs.pop(0) for _ in range(4))
    if m:
        gate_ref = refs.pop(0)
    if m or start:
        refs.pop(0)
    if m and start:
        refs.pop(0)
    out_ref, grown_ref, last_ref = (refs.pop(0) for _ in range(3))
    panels_ref, slab_ref, hidden_ref, sems, out_sems = refs
    step = pl.program_id(0)
    block = own_ref.shape[0]
    half = rows_ref.shape[0]

    def placed(s):
        row = pl.multiple_of(slots_ref[s] * block, 16)
        source = (own_ref, outer_ref, mate_ref, far_ref)[s]
        return pltpu.make_async_copy(source, panels_ref.at[pl.ds(row, block), :], sems.at[s])

    outer_row = pl.multiple_of(slots_ref[1] * block, 16)
    inner = slots_ref[4] == 1

    def product(ref):
        return jnp.dot(ref[...], panels_ref[...], preferred_element_type=F32)

    @pl.when(inner & (step == 0))
    def _():
        first = [placed(s) for s in (0, 2, 3)]
        for copy in first:
            copy.start()
        panels_ref[pl.ds(outer_row, block), :] = jnp.zeros((block, panels_ref.shape[1]), BF16)
        for copy in first:
            copy.wait()

    for i in range(2):
        @pl.when(inner & (step == i))
        def _():
            out_ref[i * half:(i + 1) * half, :] = product(rows_out_ref).astype(BF16)

    @pl.when(inner & (step == 2))
    def _():
        out_ref[2 * half:, :] = product(tokens_out_ref).astype(BF16)
        copy = placed(1)
        copy.start()
        copy.wait()
        pre = product(tokens_ref)
        if m:
            hidden_ref[...] = gated(gate_ref[...], pre).T
        else:
            last_ref[...] = pre

    for i in range(2):
        @pl.when(inner & (step == 3 + i))
        def _():
            slab_ref[:, i * half:(i + 1) * half] = product(rows_ref).astype(BF16).T

    @pl.when(inner & (step == 4))
    def _():
        ends = [pltpu.make_async_copy(
            slab_ref.at[:width, :], grown_ref.at[m, pl.ds(start, width), :], out_sems.at[0])]
        if m:
            ends.append(pltpu.make_async_copy(
                hidden_ref.at[:width, :], last_ref.at[pl.ds(start, width), :], out_sems.at[1]))
        for copy in ends:
            copy.start()
        for copy in ends:
            copy.wait()


def products(m, start, width, slots, mine, theirs, panels, gate, grown, hidden, columns):
    (rows, token_growth), (rows_out, token_growth_out) = mine, theirs
    count, depth = rows.shape
    extra = token_growth.shape[0]
    block, wide = panels[0].shape
    half = count // 2
    whole = lambda i, s: (0, 0)
    in_specs = [
        pl.BlockSpec((half, depth), lambda i, s: (jnp.minimum(i, 1), 0)),
        pl.BlockSpec((extra, depth), whole),
        pl.BlockSpec((half, depth), lambda i, s: (jnp.clip(i - 3, 0, 1), 0)),
        pl.BlockSpec((extra, depth), whole),
    ] + [ANY] * 4
    args = [rows_out, token_growth_out, rows, token_growth, *panels]
    aliases = {}
    if m:
        in_specs.append(pl.BlockSpec((extra, wide), whole))
        args.append(gate)
    if grown is not None:
        aliases[len(args) + 1] = 1
        in_specs.append(ANY)
        args.append(grown)
    if m and hidden is not None:
        aliases[len(args) + 1] = 2
        in_specs.append(ANY)
        args.append(hidden)
    return pl.pallas_call(
        functools.partial(products_kernel, m, start, width),
        out_shape=(
            jax.ShapeDtypeStruct((count + extra, wide), BF16),
            jax.ShapeDtypeStruct((2, columns, count), BF16),
            jax.ShapeDtypeStruct((columns, extra), BF16) if m else jax.ShapeDtypeStruct((extra, wide), F32),
        ),
        grid_spec=pltpu.PrefetchScalarGridSpec(
            num_scalar_prefetch=1,
            grid=(5,),
            in_specs=in_specs,
            out_specs=(
                pl.BlockSpec((count + extra, wide), whole),
                ANY,
                ANY if m else pl.BlockSpec((extra, wide), whole),
            ),
            scratch_shapes=[
                pltpu.VMEM((depth, wide), BF16),
                pltpu.VMEM((wide, count), BF16),
                pltpu.VMEM((wide, extra), BF16),
                pltpu.SemaphoreType.DMA((4,)),
                pltpu.SemaphoreType.DMA((2,)),
            ],
        ),
        input_output_aliases=aliases,
        compiler_params=pltpu.CompilerParams(vmem_limit_bytes=VMEM_LIMIT),
        cost_estimate=pl.CostEstimate(
            flops=4 * (count + extra) * depth * wide,
            bytes_accessed=4 * (count + extra) * (depth + wide),
            transcendentals=0,
        ),
        name="products",
    )(slots, *args)


def finish_kernel(m, start, width, slots_ref, rows_ref, tokens_ref, own_ref, got_ref, *refs):
    refs = list(refs)
    gate_ref = refs.pop(0)
    del refs[:2 if m else 1]
    grown_ref, last_ref = refs.pop(0), refs.pop(0)
    panels_ref, slab_ref, hidden_ref, sems, out_sems = refs
    block = own_ref.shape[0]
    count = rows_ref.shape[0]

    @pl.when(slots_ref[4] == 0)
    def _():
        place = pl.multiple_of(slots_ref[5] * block, 16)
        other = pl.multiple_of((1 - slots_ref[5]) * block, 16)
        copy = pltpu.make_async_copy(own_ref, panels_ref.at[pl.ds(place, block), :], sems.at[0])
        copy.start()
        panels_ref[pl.ds(other, block), :] = jnp.zeros((block, panels_ref.shape[1]), BF16)
        copy.wait()
        pre = jnp.dot(tokens_ref[...], panels_ref[...], preferred_element_type=F32)
        pre = pre + got_ref[count:, :].astype(F32)
        if m:
            hidden_ref[...] = gated(gate_ref[...], pre).T
        else:
            last = pltpu.make_async_copy(hidden_ref, last_ref, out_sems.at[1])
            hidden_ref[...] = pre
            last.start()
        half = count // 2
        for i in range(2):
            part = slice(i * half, (i + 1) * half)
            sums = jnp.dot(rows_ref[part, :], panels_ref[...], preferred_element_type=F32)
            slab_ref[:, part] = (sums + got_ref[part, :].astype(F32)).astype(BF16).T
        ends = [pltpu.make_async_copy(
            slab_ref.at[:width, :], grown_ref.at[m, pl.ds(start, width), :], out_sems.at[0])]
        ends[0].start()
        if m:
            ends.append(pltpu.make_async_copy(
                hidden_ref.at[:width, :], last_ref.at[pl.ds(start, width), :], out_sems.at[1]))
            ends[1].start()
        else:
            ends.append(last)
        for copy in ends:
            copy.wait()


def finish(m, start, width, slots, mine, own, got, gate, grown, hidden, columns):
    rows, token_growth = mine
    count, depth = rows.shape
    extra = token_growth.shape[0]
    block, wide = own.shape
    whole = lambda i, s: (0, 0)
    side = lambda i, s: (0, s[5])
    in_specs = [
        pl.BlockSpec((count, depth // 2), side),
        pl.BlockSpec((extra, depth // 2), side),
        ANY,
        pl.BlockSpec((count + extra, wide), whole),
    ]
    args = [rows, token_growth, own, got]
    if m:
        in_specs += [pl.BlockSpec((extra, wide), whole), ANY, ANY]
        args += [gate, grown, hidden]
        aliases = {6: 0, 7: 1}
    else:
        in_specs += [ANY, ANY]
        args += [gate, grown]
        aliases = {6: 0, 5: 1}
    return pl.pallas_call(
        functools.partial(finish_kernel, m, start, width),
        out_shape=(
            jax.ShapeDtypeStruct((2, columns, count), BF16),
            jax.ShapeDtypeStruct((columns, extra), BF16) if m else jax.ShapeDtypeStruct((extra, wide), F32),
        ),
        grid_spec=pltpu.PrefetchScalarGridSpec(
            num_scalar_prefetch=1,
            grid=(1,),
            in_specs=in_specs,
            out_specs=(ANY, ANY),
            scratch_shapes=[
                pltpu.VMEM((2 * block, wide), BF16),
                pltpu.VMEM((wide, count), BF16),
                pltpu.VMEM((wide, extra), BF16) if m else pltpu.VMEM((extra, wide), F32),
                pltpu.SemaphoreType.DMA((1,)),
                pltpu.SemaphoreType.DMA((2,)),
            ],
        ),
        input_output_aliases=aliases,
        compiler_params=pltpu.CompilerParams(vmem_limit_bytes=VMEM_LIMIT),
        cost_estimate=pl.CostEstimate(
            flops=4 * (count + extra) * block * wide,
            bytes_accessed=2 * (count + extra) * (depth + wide),
            transcendentals=0,
        ),
        name="finish",
    )(slots, *args)


def rows_of_outer(rows):
    nt = lax.axis_size("tensor")
    half = rows.shape[0] // 2
    core = lax.rem(lax.axis_index("tensor"), 2)
    mine = lax.dynamic_slice(rows, (core * half, 0), (half, rows.shape[1]))
    got = lax.ppermute(mine, "dp", TO_INNER)
    other = lax.ppermute(got, "tensor", [(j, j ^ 1) for j in range(nt)])
    first = jnp.where(core == 0, got, other)
    second = jnp.where(core == 0, other, got)
    return jnp.concatenate([first, second], axis=0)


def line_form(tokens, small_weights, ffn_growth, width_growth):
    columns = ffn_growth.shape[0]
    index = lax.axis_index("dp")
    is_inner = ((index == 1) | (index == 2)).astype(jnp.int32)
    slots = jnp.concatenate(
        [jnp.array(SLOTS, jnp.int32)[index], jnp.stack([is_inner, (index == 3).astype(jnp.int32)])]
    )
    small = [lax.all_gather(small_weights[m], "tensor", axis=0, tiled=True) for m in range(2)]
    rows_out = rows_of_outer(width_growth)
    token_growth = token_rows(tokens, width_growth)
    token_growth_out = rows_of_outer(token_growth)
    mine, theirs = (width_growth, token_growth), (rows_out, token_growth_out)

    work = [(m, start, width) for m in range(2) for start, width in pieces(columns, WIDTH)]
    count = len(work)
    per = count // 2
    own, outer, mate, far, out, received, gate = ({} for _ in range(7))
    grown = hidden = None

    def send_panel(k):
        m, start, width = work[k]
        made = [own[k - 1]] if k else []
        made += [out[k - 3]] if k >= 3 else []
        own[k] = panel_of(after(small[m], *made), ffn_growth, start, width)
        sent = after(own[k], outer[k - 2]) if k >= 2 else own[k]
        outer[k] = lax.ppermute(sent, "dp", TO_INNER)
        mate[k] = lax.ppermute(sent, "dp", SWAP_INNER)

    def finish_piece(k):
        nonlocal grown, hidden
        m, start, width = work[k]
        got = after(received[k], out[min(k + 1, count - 1)])
        grown, last = finish(m, start, width, slots, mine, own[k], got, gate[k % per], grown, hidden, columns)
        if m:
            hidden = last
        else:
            gate[k] = last

    send_panel(0)
    send_panel(1)
    for k in range(count):
        m, start, width = work[k]
        far[k] = lax.ppermute(outer[k], "dp", SWAP_INNER)
        if k + 2 < count:
            send_panel(k + 2)
        panels = [after(own[k], own[min(k + 2, count - 1)]), outer[k], mate[k], far[k]]
        out[k], grown, last = products(
            m, start, width, slots, mine, theirs, panels, gate.get(k % per), grown, hidden, columns
        )
        if m:
            hidden = last
        else:
            gate[k] = last
        received[k] = lax.ppermute(out[k], "dp", TO_OUTER)
        if k:
            finish_piece(k - 1)
    finish_piece(count - 1)
    return jnp.swapaxes(grown, 1, 2), hidden.T


def solution(mesh):
    placed = (P("dp", "tensor"), P(None, ("dp", "tensor"), None), P("tensor", None), P("dp", None))
    return jax.shard_map(
        line_form if mesh.shape["dp"] == 4 else gathered_form,
        mesh=mesh,
        in_specs=placed,
        out_specs=(P(None, "dp", "tensor"), P("dp", "tensor")),
        check_vma=False,
    )
```

```python
import functools

import jax
import jax.numpy as jnp
from jax import lax
from jax.experimental import pallas as pl
from jax.experimental.pallas import tpu as pltpu
from jax.sharding import PartitionSpec as P

BF16, F32 = jnp.bfloat16, jnp.float32
WIDTH = 512
VMEM_LIMIT = 56 * 1024 * 1024
ANY = pl.BlockSpec(memory_space=pl.ANY)


def pieces(extent, width):
    starts = list(range(0, extent, width))
    return [(start, min(width, extent - start)) for start in starts]


def after(array, *made):
    return lax.optimization_barrier((array,) + made)[0]


def token_rows(tokens, width_growth):
    nd = lax.axis_size("dp")
    by_rows = lax.all_to_all(tokens, "tensor", 0, 1, tiled=True)
    by_features = lax.all_to_all(by_rows, "dp", 1, 0, tiled=True)
    part = jnp.dot(by_features, width_growth, preferred_element_type=F32).astype(BF16)
    parts = lax.all_to_all(part, "dp", 0, 0, tiled=True)
    return jnp.sum(parts.reshape(nd, -1, parts.shape[1]).astype(F32), axis=0).astype(BF16)


def gathered_form(tokens, small_weights, ffn_growth, width_growth):
    columns = ffn_growth.shape[0]
    small = [lax.all_gather(small_weights[m], "tensor", axis=0, tiled=True) for m in range(2)]
    token_growth = lax.all_gather(token_rows(tokens, width_growth), "tensor", axis=0, tiled=True)
    grown, pre = [], []
    for m in range(2):
        grown_parts, pre_parts = [], []
        for start, width in pieces(columns, WIDTH):
            panel = jnp.einsum(
                "sf,cf->sc", small[m], ffn_growth[start:start + width], preferred_element_type=F32
            ).astype(BF16)
            panels = lax.all_gather(panel, "dp", axis=0, tiled=True)
            grown_parts.append(jnp.dot(width_growth, panels, preferred_element_type=F32).astype(BF16))
            pre_parts.append(jnp.dot(token_growth, panels, preferred_element_type=F32))
        grown.append(jnp.concatenate(grown_parts, axis=1))
        pre.append(jnp.concatenate(pre_parts, axis=1))
    hidden = (jax.nn.silu(pre[0]) * pre[1]).astype(BF16)
    return (jnp.stack(grown), hidden)


SWAP_INNER = [(1, 2), (2, 1)]
TO_INNER = [(0, 1), (3, 2)]
TO_OUTER = [(1, 0), (2, 3)]
SLOTS = [[0, 1, 2, 3], [1, 0, 2, 3], [2, 3, 1, 0], [3, 0, 1, 2]]


def panel_kernel(steps, splits, small_ref, growth_ref, *refs):
    out_refs, acc_ref = refs[:-1], refs[-1]
    step = pl.program_id(0)
    part = lax.dot_general(
        small_ref[...], growth_ref[...], (((1,), (1,)), ((), ())), preferred_element_type=F32
    )

    @pl.when(step == 0)
    def _():
        acc_ref[...] = part

    @pl.when((step > 0) & (step < steps - 1))
    def _():
        acc_ref[...] += part

    @pl.when(step == steps - 1)
    def _():
        total = acc_ref[...] + part
        for (start, width), out_ref in zip(splits, out_refs):
            wide = out_ref.shape[1]
            piece = total[:, start:start + wide]
            if width < wide:
                column = lax.broadcasted_iota(jnp.int32, piece.shape, 1)
                piece = jnp.where(column < width, piece, 0.0)
            out_ref[...] = piece.astype(BF16)


def tiled(width):
    return -(-width // 128) * 128


def panel_of(small, growth, splits):
    rows, depth = small.shape
    wide = tiled(growth.shape[0])
    steps = 7
    deep = depth // steps
    return pl.pallas_call(
        functools.partial(panel_kernel, steps, splits),
        out_shape=[jax.ShapeDtypeStruct((rows, tiled(width)), BF16) for _, width in splits],
        grid=(steps,),
        in_specs=[
            pl.BlockSpec((rows, deep), lambda k: (0, k)),
            pl.BlockSpec((wide, deep), lambda k: (0, k)),
        ],
        out_specs=[pl.BlockSpec((rows, tiled(width)), lambda k: (0, 0)) for _, width in splits],
        scratch_shapes=[pltpu.VMEM((rows, wide), F32)],
        compiler_params=pltpu.CompilerParams(vmem_limit_bytes=VMEM_LIMIT),
        cost_estimate=pl.CostEstimate(
            flops=2 * rows * depth * wide, bytes_accessed=2 * depth * (rows + wide), transcendentals=0
        ),
        name="panel",
    )(small, growth)


def gated(gate, up):
    return (gate / (1.0 + jnp.exp(-gate)) * up).astype(BF16)


def products_kernel(m, start, width, slots_ref, *refs):
    refs = list(refs)
    theirs, their_tokens = (refs.pop(0), refs.pop(0)), (refs.pop(0), refs.pop(0))
    rows_ref, tokens_ref = refs.pop(0), refs.pop(0)
    sources = [refs.pop(0) for _ in range(4)]
    if m:
        gate_ref = refs.pop(0)
    if m or start:
        refs.pop(0)
    if m and start:
        refs.pop(0)
    out_ref, grown_ref, last_ref = (refs.pop(0) for _ in range(3))
    panels_ref, factors_ref, stage_ref, slab_ref, extra_ref, gate_buf, sems, factor_sems, end_sems = refs
    block = sources[0].shape[0]
    count = rows_ref.shape[0]
    extra = tokens_ref.shape[0]
    half, few = count // 2, extra // 2

    def placed(s):
        row = pl.multiple_of(slots_ref[s] * block, 16)
        return pltpu.make_async_copy(sources[s], panels_ref.at[pl.ds(row, block), :], sems.at[s])

    def from_either(pair, i, buffer, offset, sem):
        size = pair[0].shape[0]
        copies = [
            pltpu.make_async_copy(ref, factors_ref.at[buffer, pl.ds(offset, size), :], sem) for ref in pair
        ]
        mine = slots_ref[6] == i

        @pl.when(mine)
        def _():
            copies[0].start()

        @pl.when(jnp.logical_not(mine))
        def _():
            copies[1].start()

        return copies[0]

    def plain(ref, first, size, buffer, offset, sem):
        copy = pltpu.make_async_copy(
            ref.at[pl.ds(first, size), :], factors_ref.at[buffer, pl.ds(offset, size), :], sem
        )
        copy.start()
        return copy

    def fetch(i):
        buffer = i % 3
        sem = [factor_sems.at[buffer, j] for j in range(3)]
        if i < 2:
            return [from_either(theirs, i, buffer, 0, sem[0])]
        if i == 2:
            return [
                from_either(their_tokens, 0, buffer, 0, sem[0]),
                from_either(their_tokens, 1, buffer, few, sem[1]),
                plain(tokens_ref, 0, extra, buffer, extra, sem[2]),
            ]
        return [plain(rows_ref, (i - 3) * half, half, buffer, 0, sem[0])]

    def product(buffer, first, size):
        return jnp.dot(factors_ref[buffer, first:first + size, :], panels_ref[...], preferred_element_type=F32)

    @pl.when(slots_ref[4] == 1)
    def _():
        first = [placed(s) for s in (0, 2, 3)]
        for copy in first:
            copy.start()
        coming = [fetch(0), fetch(1)]
        outer_row = pl.multiple_of(slots_ref[1] * block, 16)
        panels_ref[pl.ds(outer_row, block), :] = jnp.zeros((block, panels_ref.shape[1]), BF16)
        if m:
            gate_copy = pltpu.make_async_copy(gate_ref, gate_buf, end_sems.at[4])
            gate_copy.start()
        for copy in first:
            copy.wait()
        coming.append(fetch(2))
        ends = []

        def send(source, target):
            copy = pltpu.make_async_copy(source, target, end_sems.at[len(ends)])
            copy.start()
            ends.append(copy)

        for i in range(5):
            for copy in coming[i]:
                copy.wait()
            if i < 2:
                stage_ref[i * half:(i + 1) * half, :] = product(i, 0, half).astype(BF16)
                coming.append(fetch(i + 3))
            elif i == 2:
                stage_ref[count:, :] = product(2, 0, extra).astype(BF16)
                send(stage_ref, out_ref)
                outer = placed(1)
                outer.start()
                outer.wait()
                pre = product(2, extra, extra)
                if m:
                    gate_copy.wait()
                    extra_ref[...] = gated(gate_buf[...], pre).T
                    send(extra_ref.at[:width, :], last_ref.at[pl.ds(start, width), :])
                else:
                    extra_ref[...] = pre
                    send(extra_ref, last_ref)
            else:
                part = slice((i - 3) * half, (i - 2) * half)
                slab_ref[:, part] = product(i % 3, 0, half).astype(BF16).T
        send(slab_ref.at[:width, :], grown_ref.at[m, pl.ds(start, width), :])
        for copy in ends:
            copy.wait()


def products(m, start, width, slots, mine, theirs, panels, gate, grown, hidden, columns):
    rows, token_growth = mine
    count, depth = rows.shape
    extra = token_growth.shape[0]
    block, wide = panels[0].shape
    args = [*theirs, rows, token_growth, *panels]
    aliases = {}
    if m:
        args.append(gate)
    if grown is not None:
        aliases[len(args) + 1] = 1
        args.append(grown)
    if m and hidden is not None:
        aliases[len(args) + 1] = 2
        args.append(hidden)
    return pl.pallas_call(
        functools.partial(products_kernel, m, start, width),
        out_shape=(
            jax.ShapeDtypeStruct((count + extra, wide), BF16),
            jax.ShapeDtypeStruct((2, columns, count), BF16),
            jax.ShapeDtypeStruct((columns, extra), BF16) if m else jax.ShapeDtypeStruct((extra, wide), F32),
        ),
        grid_spec=pltpu.PrefetchScalarGridSpec(
            num_scalar_prefetch=1,
            grid=(1,),
            in_specs=[ANY] * len(args),
            out_specs=(ANY, ANY, ANY),
            scratch_shapes=[
                pltpu.VMEM((depth, wide), BF16),
                pltpu.VMEM((3, count // 2, depth), BF16),
                pltpu.VMEM((count + extra, wide), BF16),
                pltpu.VMEM((wide, count), BF16),
                pltpu.VMEM((wide, extra), BF16) if m else pltpu.VMEM((extra, wide), F32),
                pltpu.VMEM((extra, wide), F32),
                pltpu.SemaphoreType.DMA((4,)),
                pltpu.SemaphoreType.DMA((3, 3)),
                pltpu.SemaphoreType.DMA((5,)),
            ],
        ),
        input_output_aliases=aliases,
        compiler_params=pltpu.CompilerParams(vmem_limit_bytes=VMEM_LIMIT),
        cost_estimate=pl.CostEstimate(
            flops=4 * (count + extra) * depth * wide,
            bytes_accessed=4 * (count + extra) * (depth + wide),
            transcendentals=0,
        ),
        name="products",
    )(slots, *args)


def finish_kernel(m, start, width, slots_ref, rows_ref, tokens_ref, own_ref, got_ref, gate_ref, *refs):
    grown_ref, last_ref = refs[2 if m else 1:][:2]
    factors_ref, panels_ref, got_buf, gate_buf, slab_ref, extra_ref, sems = refs[2 if m else 1:][2:]
    block = own_ref.shape[0]
    count = rows_ref.shape[0]
    wide = panels_ref.shape[1]
    half = count // 2
    depth = factors_ref.shape[1]

    @pl.when(slots_ref[4] == 0)
    def _():
        side = pl.multiple_of(slots_ref[5] * depth, 128)
        place = pl.multiple_of(slots_ref[5] * block, 16)
        other = pl.multiple_of((1 - slots_ref[5]) * block, 16)
        copies = [
            pltpu.make_async_copy(own_ref, panels_ref.at[pl.ds(place, block), :], sems.at[0]),
            pltpu.make_async_copy(
                tokens_ref.at[:, pl.ds(side, depth)], factors_ref.at[pl.ds(count, tokens_ref.shape[0]), :], sems.at[1]),
            pltpu.make_async_copy(rows_ref.at[:, pl.ds(side, depth)], factors_ref.at[pl.ds(0, count), :], sems.at[2]),
            pltpu.make_async_copy(got_ref, got_buf, sems.at[3]),
        ]
        if m:
            copies.append(pltpu.make_async_copy(gate_ref, gate_buf, sems.at[4]))
        for copy in copies:
            copy.start()
        panels_ref[pl.ds(other, block), :] = jnp.zeros((block, wide), BF16)
        for copy in copies:
            copy.wait()

        def product(first, size):
            sums = jnp.dot(factors_ref[first:first + size, :], panels_ref[...], preferred_element_type=F32)
            return sums + got_buf[first:first + size, :].astype(F32)

        pre = product(count, tokens_ref.shape[0])
        if m:
            extra_ref[...] = gated(gate_buf[...], pre).T
            end = pltpu.make_async_copy(
                extra_ref.at[:width, :], last_ref.at[pl.ds(start, width), :], sems.at[0])
        else:
            extra_ref[...] = pre
            end = pltpu.make_async_copy(extra_ref, last_ref, sems.at[0])
        end.start()
        for i in range(2):
            slab_ref[:, i * half:(i + 1) * half] = product(i * half, half).astype(BF16).T
        slab = pltpu.make_async_copy(
            slab_ref.at[:width, :], grown_ref.at[m, pl.ds(start, width), :], sems.at[1])
        slab.start()
        end.wait()
        slab.wait()


def finish(m, start, width, slots, mine, own, got, gate, grown, hidden, columns):
    rows, token_growth = mine
    count, depth = rows.shape
    extra = token_growth.shape[0]
    block, wide = own.shape
    args = [rows, token_growth, own, got, gate, grown] + ([hidden] if m else [])
    return pl.pallas_call(
        functools.partial(finish_kernel, m, start, width),
        out_shape=(
            jax.ShapeDtypeStruct((2, columns, count), BF16),
            jax.ShapeDtypeStruct((columns, extra), BF16) if m else jax.ShapeDtypeStruct((extra, wide), F32),
        ),
        grid_spec=pltpu.PrefetchScalarGridSpec(
            num_scalar_prefetch=1,
            grid=(1,),
            in_specs=[ANY] * len(args),
            out_specs=(ANY, ANY),
            scratch_shapes=[
                pltpu.VMEM((count + extra, 2 * block), BF16),
                pltpu.VMEM((2 * block, wide), BF16),
                pltpu.VMEM((count + extra, wide), BF16),
                pltpu.VMEM((extra, wide), F32),
                pltpu.VMEM((wide, count), BF16),
                pltpu.VMEM((wide, extra), BF16) if m else pltpu.VMEM((extra, wide), F32),
                pltpu.SemaphoreType.DMA((5,)),
            ],
        ),
        input_output_aliases={6: 0, 7: 1} if m else {6: 0, 5: 1},
        compiler_params=pltpu.CompilerParams(vmem_limit_bytes=VMEM_LIMIT),
        cost_estimate=pl.CostEstimate(
            flops=2 * (count + extra) * block * wide,
            bytes_accessed=2 * (count + extra) * (block + wide),
            transcendentals=0,
        ),
        name="finish",
    )(slots, *args)


def fetch_half(rows):
    half = rows.shape[0] // 2
    core = lax.rem(lax.axis_index("tensor"), 2)
    return lax.ppermute(lax.dynamic_slice(rows, (core * half, 0), (half, rows.shape[1])), "dp", TO_INNER)


def other_half(half):
    return lax.ppermute(half, "tensor", [(j, j ^ 1) for j in range(lax.axis_size("tensor"))])


def line_form(tokens, small_weights, ffn_growth, width_growth):
    columns = ffn_growth.shape[0]
    index = lax.axis_index("dp")
    is_inner = ((index == 1) | (index == 2)).astype(jnp.int32)
    core = lax.rem(lax.axis_index("tensor"), 2)
    slots = jnp.concatenate(
        [jnp.array(SLOTS, jnp.int32)[index], jnp.stack([is_inner, (index == 3).astype(jnp.int32), core])]
    )
    rows_half = fetch_half(width_growth)
    small = [lax.all_gather(small_weights[0], "tensor", axis=0, tiled=True)]
    token_part = token_rows(tokens, width_growth)
    token_growth = lax.all_gather(token_part, "tensor", axis=0, tiled=True)
    small.append(lax.all_gather(after(small_weights[1], token_part), "tensor", axis=0, tiled=True))

    splits = pieces(columns, WIDTH)
    per = len(splits)
    count = 2 * per
    own, outer, mate, far, out, received, gate = ({} for _ in range(7))
    grown = hidden = token = None

    def panel(m):
        nonlocal token
        source = small[m] if token is None else after(small[m], token)
        for k, made in enumerate(panel_of(source, ffn_growth, splits)):
            own[m * per + k] = made
        token = own[m * per]

    def send(k):
        sent = after(own[k], token)
        outer[k] = lax.ppermute(sent, "dp", TO_INNER)
        mate[k] = lax.ppermute(sent, "dp", SWAP_INNER)

    def forward(k):
        nonlocal token
        outer[k] = after(outer[k], token)
        far[k] = lax.ppermute(outer[k], "dp", SWAP_INNER)
        token = outer[k]

    def multiply(k):
        nonlocal token, grown, hidden
        (start, width), m = splits[k % per], k // per
        panels = [after(own[k], token), outer[k], mate[k], far[k]]
        out[k], grown, last = products(
            m, start, width, slots, mine, theirs, panels, gate.get(k % per), grown, hidden, columns
        )
        if m:
            hidden = last
        else:
            gate[k] = last
        received[k] = lax.ppermute(out[k], "dp", TO_OUTER)
        token = out[k]

    def conclude(k):
        nonlocal grown, hidden
        (start, width), m = splits[k % per], k // per
        got = after(received[k], token)
        grown, last = finish(m, start, width, slots, mine, own[k], got, gate[k % per], grown, hidden, columns)
        if m:
            hidden = last
        else:
            gate[k] = last

    panel(0)
    send(0)
    rows_half = after(rows_half, own[0])
    forward(0)
    send(1)
    token_half = fetch_half(after(token_growth, own[0]))
    mine = (width_growth, token_growth)
    theirs = (rows_half, other_half(rows_half), token_half, other_half(token_half))
    for k in range(1, per):
        forward(k)
        if k + 1 < per:
            send(k + 1)
    multiply(0)
    panel(1)
    send(per)
    for k in range(1, per):
        multiply(k)
    for k in range(per, count):
        forward(k)
        if k + 1 < count:
            send(k + 1)
        conclude(k - per)
        if k > per:
            multiply(k - 1)
    multiply(count - 1)
    for k in range(per, count):
        conclude(k)
    return jnp.swapaxes(grown, 1, 2), hidden.T


def solution(mesh):
    placed = (P("dp", "tensor"), P(None, ("dp", "tensor"), None), P("tensor", None), P("dp", None))
    return jax.shard_map(
        line_form if mesh.shape["dp"] == 4 else gathered_form,
        mesh=mesh,
        in_specs=placed,
        out_specs=(P(None, "dp", "tensor"), P("dp", "tensor")),
        check_vma=False,
    )
```

```python
import functools

import jax
import jax.numpy as jnp
from jax import lax
from jax.experimental import pallas as pl
from jax.experimental.pallas import tpu as pltpu
from jax.sharding import PartitionSpec as P

BF16, F32 = jnp.bfloat16, jnp.float32
WIDTH = 512
VMEM_LIMIT = 56 * 1024 * 1024
ANY = pl.BlockSpec(memory_space=pl.ANY)


def pieces(extent, width):
    starts = list(range(0, extent, width))
    return [(start, min(width, extent - start)) for start in starts]


def after(array, *made):
    return lax.optimization_barrier((array,) + made)[0]


def token_rows(tokens, width_growth):
    nd = lax.axis_size("dp")
    by_rows = lax.all_to_all(tokens, "tensor", 0, 1, tiled=True)
    by_features = lax.all_to_all(by_rows, "dp", 1, 0, tiled=True)
    part = jnp.dot(by_features, width_growth, preferred_element_type=F32).astype(BF16)
    parts = lax.all_to_all(part, "dp", 0, 0, tiled=True)
    return jnp.sum(parts.reshape(nd, -1, parts.shape[1]).astype(F32), axis=0).astype(BF16)


def doubled(rows):
    place = lax.axis_index("tensor")
    bit = 1
    while bit < lax.axis_size("tensor"):
        got = lax.ppermute(rows, "tensor", [(j, j ^ bit) for j in range(lax.axis_size("tensor"))])
        low = (place // bit) % 2 == 0
        rows = jnp.concatenate([jnp.where(low, rows, got), jnp.where(low, got, rows)], axis=0)
        bit *= 2
    return rows


def gathered_form(tokens, small_weights, ffn_growth, width_growth):
    columns = ffn_growth.shape[0]
    small = [lax.all_gather(small_weights[m], "tensor", axis=0, tiled=True) for m in range(2)]
    token_growth = lax.all_gather(token_rows(tokens, width_growth), "tensor", axis=0, tiled=True)
    grown, pre = [], []
    for m in range(2):
        grown_parts, pre_parts = [], []
        for start, width in pieces(columns, WIDTH):
            panel = jnp.einsum(
                "sf,cf->sc", small[m], ffn_growth[start:start + width], preferred_element_type=F32
            ).astype(BF16)
            panels = lax.all_gather(panel, "dp", axis=0, tiled=True)
            grown_parts.append(jnp.dot(width_growth, panels, preferred_element_type=F32).astype(BF16))
            pre_parts.append(jnp.dot(token_growth, panels, preferred_element_type=F32))
        grown.append(jnp.concatenate(grown_parts, axis=1))
        pre.append(jnp.concatenate(pre_parts, axis=1))
    hidden = (jax.nn.silu(pre[0]) * pre[1]).astype(BF16)
    return (jnp.stack(grown), hidden)


SWAP_INNER = [(1, 2), (2, 1)]
TO_INNER = [(0, 1), (3, 2)]
TO_OUTER = [(1, 0), (2, 3)]
SLOTS = [[0, 1, 2, 3], [1, 0, 2, 3], [2, 3, 1, 0], [3, 0, 1, 2]]


def panel_kernel(steps, splits, small_ref, growth_ref, *refs):
    out_refs, acc_ref = refs[:-1], refs[-1]
    step = pl.program_id(0)
    part = lax.dot_general(
        small_ref[...], growth_ref[...], (((1,), (1,)), ((), ())), preferred_element_type=F32
    )

    @pl.when(step == 0)
    def _():
        acc_ref[...] = part

    @pl.when((step > 0) & (step < steps - 1))
    def _():
        acc_ref[...] += part

    @pl.when(step == steps - 1)
    def _():
        total = acc_ref[...] + part
        for (start, width), out_ref in zip(splits, out_refs):
            wide = out_ref.shape[1]
            piece = total[:, start - splits[0][0]:start - splits[0][0] + wide]
            if width < wide:
                column = lax.broadcasted_iota(jnp.int32, piece.shape, 1)
                piece = jnp.where(column < width, piece, 0.0)
            out_ref[...] = piece.astype(BF16)


def tiled(width):
    return -(-width // 128) * 128


def panel_of(small, growth, splits):
    rows, depth = small.shape
    first = splits[0][0]
    wide = tiled(splits[-1][0] + splits[-1][1] - first)
    steps = 7
    deep = depth // steps
    return pl.pallas_call(
        functools.partial(panel_kernel, steps, splits),
        out_shape=[jax.ShapeDtypeStruct((rows, tiled(width)), BF16) for _, width in splits],
        grid=(steps,),
        in_specs=[
            pl.BlockSpec((rows, deep), lambda k: (0, k)),
            pl.BlockSpec((pl.Element(wide, (0, max(0, first + wide - growth.shape[0]))), pl.Element(deep)), lambda k: (first, k * deep)),
        ],
        out_specs=[pl.BlockSpec((rows, tiled(width)), lambda k: (0, 0)) for _, width in splits],
        scratch_shapes=[pltpu.VMEM((rows, wide), F32)],
        compiler_params=pltpu.CompilerParams(vmem_limit_bytes=VMEM_LIMIT),
        cost_estimate=pl.CostEstimate(flops=3 * rows * depth * wide, bytes_accessed=0, transcendentals=0),
        name="panel",
    )(small, growth)


def gated(gate, up):
    return (gate / (1.0 + jnp.exp(-gate)) * up).astype(BF16)


def products_kernel(m, start, width, sending, keeping, slots_ref, *refs):
    refs = list(refs)
    theirs, their_tokens = (refs.pop(0), refs.pop(0)), (refs.pop(0), refs.pop(0))
    rows_ref, tokens_ref = refs.pop(0), refs.pop(0)
    sources = [refs.pop(0) for _ in range(4)]
    if keeping:
        if m:
            gate_ref = refs.pop(0)
        if m or start:
            refs.pop(0)
        if m and start:
            refs.pop(0)
    if sending:
        out_ref = refs.pop(0)
    if keeping:
        grown_ref, last_ref = refs.pop(0), refs.pop(0)
    panels_ref, factors_ref, stage_ref, slab_ref, extra_ref, gate_buf, sems, factor_sems, end_sems = refs
    block = sources[0].shape[0]
    count = rows_ref.shape[0]
    extra = tokens_ref.shape[0]
    half, few = count // 2, extra // 2

    def placed(s):
        row = pl.multiple_of(slots_ref[s] * block, 16)
        return pltpu.make_async_copy(sources[s], panels_ref.at[pl.ds(row, block), :], sems.at[s])

    def from_either(pair, i, buffer, offset, sem):
        size = pair[0].shape[0]
        copies = [
            pltpu.make_async_copy(ref, factors_ref.at[buffer, pl.ds(offset, size), :], sem) for ref in pair
        ]
        mine = slots_ref[6] == i

        @pl.when(mine)
        def _():
            copies[0].start()

        @pl.when(jnp.logical_not(mine))
        def _():
            copies[1].start()

        return copies[0]

    def plain(ref, first, size, buffer, offset, sem):
        copy = pltpu.make_async_copy(
            ref.at[pl.ds(first, size), :], factors_ref.at[buffer, pl.ds(offset, size), :], sem
        )
        copy.start()
        return copy

    work = ["sent", "sent", "tokens", "kept", "kept"][0 if sending else 2:5 if keeping else 3]
    place = {"sent": 0, "kept": 0}

    def fetch(i):
        buffer = i % 3
        sem = [factor_sems.at[buffer, j] for j in range(3)]
        if work[i] == "sent":
            place["sent"] += 1
            return [from_either(theirs, place["sent"] - 1, buffer, 0, sem[0])]
        if work[i] == "kept":
            place["kept"] += 1
            return [plain(rows_ref, (place["kept"] - 1) * half, half, buffer, 0, sem[0])]
        copies = []
        if sending:
            copies.append(from_either(their_tokens, 0, buffer, 0, sem[0]))
            copies.append(from_either(their_tokens, 1, buffer, few, sem[1]))
        if keeping:
            copies.append(plain(tokens_ref, 0, extra, buffer, extra, sem[2]))
        return copies

    def product(buffer, first, size):
        return jnp.dot(factors_ref[buffer, first:first + size, :], panels_ref[...], preferred_element_type=F32)

    @pl.when(slots_ref[4] == 1)
    def _():
        first = [placed(s) for s in ((0, 2, 3) if sending else (0, 1, 2, 3))]
        for copy in first:
            copy.start()
        coming = [fetch(0), fetch(1)]
        if sending:
            outer_row = pl.multiple_of(slots_ref[1] * block, 16)
            panels_ref[pl.ds(outer_row, block), :] = jnp.zeros((block, panels_ref.shape[1]), BF16)
        if m and keeping:
            gate_copy = pltpu.make_async_copy(gate_ref, gate_buf, end_sems.at[4])
            gate_copy.start()
        for copy in first:
            copy.wait()
        ends = []

        def finished(source, target):
            copy = pltpu.make_async_copy(source, target, end_sems.at[len(ends)])
            copy.start()
            ends.append(copy)

        done = {"sent": 0, "kept": 0}
        for i, kind in enumerate(work):
            if i + 2 < len(work):
                coming.append(fetch(i + 2))
            for copy in coming[i]:
                copy.wait()
            if kind == "sent":
                stage_ref[done[kind] * half:(done[kind] + 1) * half, :] = product(i % 3, 0, half).astype(BF16)
                done[kind] += 1
            elif kind == "kept":
                part = slice(done[kind] * half, (done[kind] + 1) * half)
                slab_ref[:, part] = product(i % 3, 0, half).astype(BF16).T
                done[kind] += 1
            else:
                if sending:
                    stage_ref[count:, :] = product(i % 3, 0, extra).astype(BF16)
                    finished(stage_ref, out_ref)
                if sending and keeping:
                    outer = placed(1)
                    outer.start()
                    outer.wait()
                if keeping:
                    pre = product(i % 3, extra, extra)
                    if m:
                        gate_copy.wait()
                        extra_ref[...] = gated(gate_buf[...], pre).T
                        finished(extra_ref.at[:width, :], last_ref.at[pl.ds(start, width), :])
                    else:
                        extra_ref[...] = pre
                        finished(extra_ref, last_ref)
        if keeping:
            finished(slab_ref.at[:width, :], grown_ref.at[m, pl.ds(start, width), :])
        for copy in ends:
            copy.wait()


def products(m, start, width, slots, mine, theirs, panels, gate, grown, hidden, columns, sending, keeping):
    rows, token_growth = mine
    count, depth = rows.shape
    extra = token_growth.shape[0]
    block, wide = panels[0].shape
    args = [*theirs, rows, token_growth, *panels]
    aliases = {}
    if keeping and m:
        args.append(gate)
    if keeping and grown is not None:
        aliases[len(args) + 1] = int(sending)
        args.append(grown)
    if keeping and m and hidden is not None:
        aliases[len(args) + 1] = int(sending) + 1
        args.append(hidden)
    out_shape = []
    if sending:
        out_shape.append(jax.ShapeDtypeStruct((count + extra, wide), BF16))
    if keeping:
        out_shape.append(jax.ShapeDtypeStruct((2, columns, count), BF16))
        out_shape.append(
            jax.ShapeDtypeStruct((columns, extra), BF16) if m else jax.ShapeDtypeStruct((extra, wide), F32)
        )
    return pl.pallas_call(
        functools.partial(products_kernel, m, start, width, sending, keeping),
        out_shape=out_shape,
        grid_spec=pltpu.PrefetchScalarGridSpec(
            num_scalar_prefetch=1,
            grid=(1,),
            in_specs=[ANY] * len(args),
            out_specs=[ANY] * len(out_shape),
            scratch_shapes=[
                pltpu.VMEM((depth, wide), BF16),
                pltpu.VMEM((3, count // 2, depth), BF16),
                pltpu.VMEM((count + extra, wide), BF16),
                pltpu.VMEM((wide, count), BF16),
                pltpu.VMEM((wide, extra), BF16) if m else pltpu.VMEM((extra, wide), F32),
                pltpu.VMEM((extra, wide), F32),
                pltpu.SemaphoreType.DMA((4,)),
                pltpu.SemaphoreType.DMA((3, 3)),
                pltpu.SemaphoreType.DMA((5,)),
            ],
        ),
        input_output_aliases=aliases,
        compiler_params=pltpu.CompilerParams(vmem_limit_bytes=VMEM_LIMIT),
        cost_estimate=pl.CostEstimate(flops=3 * (sending + keeping) * (count + extra) * depth * wide, bytes_accessed=0, transcendentals=0),
        name="products",
    )(slots, *args)


def finish_kernel(m, start, width, slots_ref, rows_ref, tokens_ref, own_ref, got_ref, gate_ref, *refs):
    grown_ref, last_ref = refs[2 if m else 1:][:2]
    factors_ref, panels_ref, got_buf, gate_buf, slab_ref, extra_ref, sems = refs[2 if m else 1:][2:]
    block = own_ref.shape[0]
    count = rows_ref.shape[0]
    wide = panels_ref.shape[1]
    half = count // 2
    depth = factors_ref.shape[1]

    @pl.when(slots_ref[4] == 0)
    def _():
        side = pl.multiple_of(slots_ref[5] * depth, 128)
        place = pl.multiple_of(slots_ref[5] * block, 16)
        other = pl.multiple_of((1 - slots_ref[5]) * block, 16)
        copies = [
            pltpu.make_async_copy(own_ref, panels_ref.at[pl.ds(place, block), :], sems.at[0]),
            pltpu.make_async_copy(
                tokens_ref.at[:, pl.ds(side, depth)], factors_ref.at[pl.ds(count, tokens_ref.shape[0]), :], sems.at[1]),
            pltpu.make_async_copy(rows_ref.at[:, pl.ds(side, depth)], factors_ref.at[pl.ds(0, count), :], sems.at[2]),
            pltpu.make_async_copy(got_ref, got_buf, sems.at[3]),
        ]
        if m:
            copies.append(pltpu.make_async_copy(gate_ref, gate_buf, sems.at[4]))
        for copy in copies:
            copy.start()
        panels_ref[pl.ds(other, block), :] = jnp.zeros((block, wide), BF16)
        for copy in copies:
            copy.wait()

        def product(first, size):
            sums = jnp.dot(factors_ref[first:first + size, :], panels_ref[...], preferred_element_type=F32)
            return sums + got_buf[first:first + size, :].astype(F32)

        pre = product(count, tokens_ref.shape[0])
        if m:
            extra_ref[...] = gated(gate_buf[...], pre).T
            end = pltpu.make_async_copy(
                extra_ref.at[:width, :], last_ref.at[pl.ds(start, width), :], sems.at[0])
        else:
            extra_ref[...] = pre
            end = pltpu.make_async_copy(extra_ref, last_ref, sems.at[0])
        end.start()
        for i in range(2):
            slab_ref[:, i * half:(i + 1) * half] = product(i * half, half).astype(BF16).T
        slab = pltpu.make_async_copy(
            slab_ref.at[:width, :], grown_ref.at[m, pl.ds(start, width), :], sems.at[1])
        slab.start()
        end.wait()
        slab.wait()


def finish(m, start, width, slots, mine, own, got, gate, grown, hidden, columns):
    rows, token_growth = mine
    count, depth = rows.shape
    extra = token_growth.shape[0]
    block, wide = own.shape
    args = [rows, token_growth, own, got, gate, grown] + ([hidden] if m else [])
    return pl.pallas_call(
        functools.partial(finish_kernel, m, start, width),
        out_shape=(
            jax.ShapeDtypeStruct((2, columns, count), BF16),
            jax.ShapeDtypeStruct((columns, extra), BF16) if m else jax.ShapeDtypeStruct((extra, wide), F32),
        ),
        grid_spec=pltpu.PrefetchScalarGridSpec(
            num_scalar_prefetch=1,
            grid=(1,),
            in_specs=[ANY] * len(args),
            out_specs=(ANY, ANY),
            scratch_shapes=[
                pltpu.VMEM((count + extra, 2 * block), BF16),
                pltpu.VMEM((2 * block, wide), BF16),
                pltpu.VMEM((count + extra, wide), BF16),
                pltpu.VMEM((extra, wide), F32),
                pltpu.VMEM((wide, count), BF16),
                pltpu.VMEM((wide, extra), BF16) if m else pltpu.VMEM((extra, wide), F32),
                pltpu.SemaphoreType.DMA((5,)),
            ],
        ),
        input_output_aliases={6: 0, 7: 1} if m else {6: 0, 5: 1},
        compiler_params=pltpu.CompilerParams(vmem_limit_bytes=VMEM_LIMIT),
        cost_estimate=pl.CostEstimate(flops=0, bytes_accessed=0, transcendentals=0),
        name="finish",
    )(slots, *args)


def fetch_half(rows):
    half = rows.shape[0] // 2
    core = lax.rem(lax.axis_index("tensor"), 2)
    return lax.ppermute(lax.dynamic_slice(rows, (core * half, 0), (half, rows.shape[1])), "dp", TO_INNER)


def other_half(half):
    return lax.ppermute(half, "tensor", [(j, j ^ 1) for j in range(lax.axis_size("tensor"))])


def line_form(tokens, small_weights, ffn_growth, width_growth):
    columns = ffn_growth.shape[0]
    index = lax.axis_index("dp")
    is_inner = ((index == 1) | (index == 2)).astype(jnp.int32)
    core = lax.rem(lax.axis_index("tensor"), 2)
    slots = jnp.concatenate(
        [jnp.array(SLOTS, jnp.int32)[index], jnp.stack([is_inner, (index == 3).astype(jnp.int32), core])]
    )
    small = [lax.all_gather(small_weights[m], "tensor", axis=0, tiled=True) for m in range(2)]
    rows_half = fetch_half(width_growth)
    token_growth = doubled(token_rows(tokens, width_growth))
    token_half = fetch_half(token_growth)
    mine = (width_growth, token_growth)

    splits = pieces(columns, WIDTH)
    per = len(splits)
    count = 2 * per
    own, outer, mate, far, out, received, gate = ({} for _ in range(7))
    grown = hidden = theirs = None

    def panel(m, chosen, *made):
        source = after(small[m], *made) if made else small[m]
        for k, part in zip(chosen, panel_of(source, ffn_growth, [splits[k] for k in chosen])):
            own[m * per + k] = part

    def send(k, *made):
        sent = after(own[k], *made) if made else own[k]
        with jax.named_scope(f"outer{k}"):
            outer[k] = lax.ppermute(sent, "dp", TO_INNER)
        with jax.named_scope(f"mate{k}"):
            mate[k] = lax.ppermute(sent, "dp", SWAP_INNER)

    def forward(k, *made):
        outer[k] = after(outer[k], *made)
        with jax.named_scope(f"far{k}"):
            far[k] = lax.ppermute(outer[k], "dp", SWAP_INNER)

    def multiply(k, *made, sending=True, keeping=True):
        nonlocal grown, hidden
        (start, width), m = splits[k % per], k // per
        panels = [after(own[k], *made), outer[k], mate[k], far[k]]
        made = products(
            m, start, width, slots, mine, theirs, panels, gate.get(k % per), grown, hidden, columns, sending, keeping
        )
        if sending:
            out[k] = made[0]
            with jax.named_scope(f"sums{k}"):
                received[k] = lax.ppermute(out[k], "dp", TO_OUTER)
        if keeping:
            grown = made[-2]
            if m:
                hidden = made[-1]
            else:
                gate[k] = made[-1]

    def conclude(k, *made):
        nonlocal grown, hidden
        (start, width), m = splits[k % per], k // per
        got = after(received[k], *made) if made else received[k]
        grown, last = finish(m, start, width, slots, mine, own[k], got, gate[k % per], grown, hidden, columns)
        if m:
            hidden = last
        else:
            gate[k] = last

    panel(0, [0])
    send(0)
    panel(0, [1, 2], own[0])
    forward(0, mate[0], own[1])
    rows_half, token_half = after(rows_half, outer[0]), after(token_half, outer[0])
    theirs = (rows_half, other_half(rows_half), token_half, other_half(token_half))
    send(1, outer[0])
    forward(1, far[0])
    send(2, outer[1])
    multiply(0, outer[1])
    forward(2, out[0])
    panel(1, [0, 1, 2], outer[2], mate[1])
    send(3)
    multiply(1, own[3], received[0], far[2])
    forward(3, out[1], mate[3])
    send(4, outer[3])
    multiply(2, outer[3])
    conclude(0)
    forward(4, out[2], far[3])
    send(5, outer[4])
    conclude(1)
    multiply(3, outer[4])
    forward(5, out[3], far[4])
    conclude(2)
    multiply(4, outer[5])
    conclude(3)
    multiply(5, out[4], keeping=False)
    multiply(5, out[5], sending=False)
    conclude(4, out[5])
    conclude(5)
    return jnp.swapaxes(grown, 1, 2), hidden.T


def solution(mesh):
    placed = (P("dp", "tensor"), P(None, ("dp", "tensor"), None), P("tensor", None), P("dp", None))
    return jax.shard_map(
        line_form if mesh.shape["dp"] == 4 else gathered_form,
        mesh=mesh,
        in_specs=placed,
        out_specs=(P(None, "dp", "tensor"), P("dp", "tensor")),
        check_vma=False,
    )
```

```python
import functools

import jax
import jax.numpy as jnp
from jax import lax
from jax.experimental import pallas as pl
from jax.experimental.pallas import tpu as pltpu
from jax.sharding import PartitionSpec as P

BF16, F32 = jnp.bfloat16, jnp.float32
WIDTH = 512
VMEM_LIMIT = 56 * 1024 * 1024
ANY = pl.BlockSpec(memory_space=pl.ANY)


def pieces(extent, width):
    starts = list(range(0, extent, width))
    return [(start, min(width, extent - start)) for start in starts]


def after(array, *made):
    return lax.optimization_barrier((array,) + made)[0]


def token_rows(tokens, width_growth, *fetched):
    nd = lax.axis_size("dp")
    by_rows = lax.all_to_all(tokens, "tensor", 0, 1, tiled=True)
    by_features = lax.all_to_all(by_rows, "dp", 1, 0, tiled=True)
    by_features = after(by_features, *fetched[:1])
    part = jnp.dot(by_features, width_growth, preferred_element_type=F32).astype(BF16)
    parts = after(lax.all_to_all(part, "dp", 0, 0, tiled=True), *fetched[1:2])
    return jnp.sum(parts.reshape(nd, -1, parts.shape[1]).astype(F32), axis=0).astype(BF16)


def doubled(rows, *fetched):
    place = lax.axis_index("tensor")
    bit = 1
    while bit < lax.axis_size("tensor"):
        got = lax.ppermute(rows, "tensor", [(j, j ^ bit) for j in range(lax.axis_size("tensor"))])
        low = (place // bit) % 2 == 0
        rows = jnp.concatenate([jnp.where(low, rows, got), jnp.where(low, got, rows)], axis=0)
        rows, fetched = after(rows, *fetched), ()
        bit *= 2
    return rows


def gathered_form(tokens, small_weights, ffn_growth, width_growth):
    columns = ffn_growth.shape[0]
    small = [lax.all_gather(small_weights[m], "tensor", axis=0, tiled=True) for m in range(2)]
    token_growth = lax.all_gather(token_rows(tokens, width_growth), "tensor", axis=0, tiled=True)
    grown, pre = [], []
    for m in range(2):
        grown_parts, pre_parts = [], []
        for start, width in pieces(columns, WIDTH):
            panel = jnp.einsum(
                "sf,cf->sc", small[m], ffn_growth[start:start + width], preferred_element_type=F32
            ).astype(BF16)
            panels = lax.all_gather(panel, "dp", axis=0, tiled=True)
            grown_parts.append(jnp.dot(width_growth, panels, preferred_element_type=F32).astype(BF16))
            pre_parts.append(jnp.dot(token_growth, panels, preferred_element_type=F32))
        grown.append(jnp.concatenate(grown_parts, axis=1))
        pre.append(jnp.concatenate(pre_parts, axis=1))
    hidden = (jax.nn.silu(pre[0]) * pre[1]).astype(BF16)
    return (jnp.stack(grown), hidden)


SWAP_INNER = [(1, 2), (2, 1)]
TO_INNER = [(0, 1), (3, 2)]
TO_OUTER = [(1, 0), (2, 3)]
SLOTS = [[0, 1, 2, 3], [1, 0, 2, 3], [2, 3, 1, 0], [3, 0, 1, 2]]


def panel_kernel(steps, splits, small_ref, growth_ref, *refs):
    out_refs, acc_ref = refs[:-1], refs[-1]
    step = pl.program_id(0)
    part = lax.dot_general(
        small_ref[...], growth_ref[...], (((1,), (1,)), ((), ())), preferred_element_type=F32
    )

    @pl.when(step == 0)
    def _():
        acc_ref[...] = part

    @pl.when((step > 0) & (step < steps - 1))
    def _():
        acc_ref[...] += part

    @pl.when(step == steps - 1)
    def _():
        total = acc_ref[...] + part
        for (start, width), out_ref in zip(splits, out_refs):
            wide = out_ref.shape[1]
            piece = total[:, start - splits[0][0]:start - splits[0][0] + wide]
            if width < wide:
                column = lax.broadcasted_iota(jnp.int32, piece.shape, 1)
                piece = jnp.where(column < width, piece, 0.0)
            out_ref[...] = piece.astype(BF16)


def tiled(width):
    return -(-width // 128) * 128


def panel_of(small, growth, splits):
    rows, depth = small.shape
    first = splits[0][0]
    wide = tiled(splits[-1][0] + splits[-1][1] - first)
    steps = 7
    deep = depth // steps
    return pl.pallas_call(
        functools.partial(panel_kernel, steps, splits),
        out_shape=[jax.ShapeDtypeStruct((rows, tiled(width)), BF16) for _, width in splits],
        grid=(steps,),
        in_specs=[
            pl.BlockSpec((rows, deep), lambda k: (0, k)),
            pl.BlockSpec((pl.Element(wide, (0, max(0, first + wide - growth.shape[0]))), pl.Element(deep)), lambda k: (first, k * deep)),
        ],
        out_specs=[pl.BlockSpec((rows, tiled(width)), lambda k: (0, 0)) for _, width in splits],
        scratch_shapes=[pltpu.VMEM((rows, wide), F32)],
        compiler_params=pltpu.CompilerParams(vmem_limit_bytes=VMEM_LIMIT),
        cost_estimate=pl.CostEstimate(flops=3 * rows * depth * wide, bytes_accessed=0, transcendentals=0),
        name="panel",
    )(small, growth)


def gated(gate, up):
    return (gate / (1.0 + jnp.exp(-gate)) * up).astype(BF16)


def products_kernel(m, start, width, sending, keeping, slots_ref, *refs):
    refs = list(refs)
    theirs, their_tokens = (refs.pop(0), refs.pop(0)), (refs.pop(0), refs.pop(0))
    rows_ref, tokens_ref = refs.pop(0), refs.pop(0)
    sources = [refs.pop(0) for _ in range(4)]
    if keeping:
        if m:
            gate_ref = refs.pop(0)
        if m or start:
            refs.pop(0)
        if start:
            refs.pop(0)
    if sending:
        out_ref = refs.pop(0)
    if keeping:
        grown_ref, last_ref = refs.pop(0), refs.pop(0)
    panels_ref, factors_ref, stage_ref, slab_ref, extra_ref, gate_buf, sems, factor_sems, end_sems = refs
    block = sources[0].shape[0]
    count = rows_ref.shape[0]
    extra = tokens_ref.shape[0]
    half, few = count // 2, extra // 2
    depth, used = panels_ref.shape[0], their_tokens[0].shape[1]

    def placed(s):
        row = pl.multiple_of(slots_ref[s] * block, 16)
        return pltpu.make_async_copy(sources[s], panels_ref.at[pl.ds(row, block), :], sems.at[s])

    def from_either(pair, i, buffer, offset, sem):
        size = pair[0].shape[0]
        copies = [
            pltpu.make_async_copy(ref, factors_ref.at[buffer, pl.ds(offset, size), pl.ds(0, used)], sem) for ref in pair
        ]
        mine = slots_ref[6] == i

        @pl.when(mine)
        def _():
            copies[0].start()

        @pl.when(jnp.logical_not(mine))
        def _():
            copies[1].start()

        return copies[0]

    def plain(ref, first, size, buffer, offset, sem):
        copy = pltpu.make_async_copy(
            ref.at[pl.ds(first, size), :], factors_ref.at[buffer, pl.ds(offset, size), :], sem
        )
        copy.start()
        return copy

    work = ["sent", "sent", "tokens", "kept", "kept"][0 if sending else 2:5 if keeping else 3]
    place = {"sent": 0, "kept": 0}

    def fetch(i):
        buffer = i % 3
        sem = [factor_sems.at[buffer, j] for j in range(3)]
        if work[i] == "sent":
            place["sent"] += 1
            return [from_either(theirs, place["sent"] - 1, buffer, 0, sem[0])]
        if work[i] == "kept":
            place["kept"] += 1
            return [plain(rows_ref, (place["kept"] - 1) * half, half, buffer, 0, sem[0])]
        copies = []
        if sending:
            copies.append(from_either(their_tokens, 0, buffer, 0, sem[0]))
            copies.append(from_either(their_tokens, 1, buffer, few, sem[1]))
        if keeping:
            copies.append(plain(tokens_ref, 0, extra, buffer, extra, sem[2]))
        return copies

    def product(buffer, first, size):
        return jnp.dot(factors_ref[buffer, first:first + size, :], panels_ref[...], preferred_element_type=F32)

    def product_out(buffer, size):
        row = pl.multiple_of(jnp.where(slots_ref[0] == 1, depth - used, 0), 128)
        return jnp.dot(
            factors_ref[buffer, :size, :used], panels_ref[pl.ds(row, used), :], preferred_element_type=F32
        )

    @pl.when(slots_ref[4] == 1)
    def _():
        first = [placed(s) for s in ((0, 2, 3) if sending else (0, 1, 2, 3))]
        for copy in first:
            copy.start()
        coming = [fetch(0), fetch(1)]
        if sending:
            outer_row = pl.multiple_of(slots_ref[1] * block, 16)
            panels_ref[pl.ds(outer_row, block), :] = jnp.zeros((block, panels_ref.shape[1]), BF16)
        if m and keeping:
            gate_copy = pltpu.make_async_copy(
                gate_ref.at[:, pl.ds(start, tiled(width))], gate_buf, end_sems.at[4])
            gate_copy.start()
        for copy in first:
            copy.wait()
        ends = []

        def finished(source, target):
            copy = pltpu.make_async_copy(source, target, end_sems.at[len(ends)])
            copy.start()
            ends.append(copy)

        done = {"sent": 0, "kept": 0}
        for i, kind in enumerate(work):
            if i + 2 < len(work):
                coming.append(fetch(i + 2))
            for copy in coming[i]:
                copy.wait()
            if kind == "sent":
                stage_ref[done[kind] * half:(done[kind] + 1) * half, :] = product_out(i % 3, half).astype(BF16)
                done[kind] += 1
            elif kind == "kept":
                part = slice(done[kind] * half, (done[kind] + 1) * half)
                slab_ref[:, part] = product(i % 3, 0, half).astype(BF16).T
                done[kind] += 1
            else:
                if sending:
                    stage_ref[count:, :] = product_out(i % 3, extra).astype(BF16)
                    finished(stage_ref, out_ref)
                if sending and keeping:
                    outer = placed(1)
                    outer.start()
                    outer.wait()
                if keeping:
                    pre = product(i % 3, extra, extra)
                    if m:
                        gate_copy.wait()
                        extra_ref[...] = gated(gate_buf[...], pre).T
                        finished(extra_ref.at[:width, :], last_ref.at[pl.ds(start, width), :])
                    else:
                        extra_ref[...] = pre
                        finished(extra_ref, last_ref.at[:, pl.ds(start, tiled(width))])
        if keeping:
            finished(slab_ref.at[:width, :], grown_ref.at[m, pl.ds(start, width), :])
        for copy in ends:
            copy.wait()


def products(m, start, width, slots, mine, theirs, panels, gate, grown, last, columns, sending, keeping):
    rows, token_growth = mine
    count, depth = rows.shape
    extra = token_growth.shape[0]
    block, wide = panels[0].shape
    args = [*theirs, rows, token_growth, *panels]
    aliases = {}
    if keeping and m:
        args.append(gate)
    if keeping and grown is not None:
        aliases[len(args) + 1] = int(sending)
        args.append(grown)
    if keeping and last is not None:
        aliases[len(args) + 1] = int(sending) + 1
        args.append(last)
    out_shape = []
    if sending:
        out_shape.append(jax.ShapeDtypeStruct((count + extra, wide), BF16))
    if keeping:
        out_shape.append(jax.ShapeDtypeStruct((2, columns, count), BF16))
        out_shape.append(
            jax.ShapeDtypeStruct((columns, extra), BF16) if m else jax.ShapeDtypeStruct((extra, tiled(columns)), F32)
        )
    return pl.pallas_call(
        functools.partial(products_kernel, m, start, width, sending, keeping),
        out_shape=out_shape,
        grid_spec=pltpu.PrefetchScalarGridSpec(
            num_scalar_prefetch=1,
            grid=(1,),
            in_specs=[ANY] * len(args),
            out_specs=[ANY] * len(out_shape),
            scratch_shapes=[
                pltpu.VMEM((depth, wide), BF16),
                pltpu.VMEM((3, count // 2, depth), BF16),
                pltpu.VMEM((count + extra, wide), BF16),
                pltpu.VMEM((wide, count), BF16),
                pltpu.VMEM((wide, extra), BF16) if m else pltpu.VMEM((extra, wide), F32),
                pltpu.VMEM((extra, wide), F32),
                pltpu.SemaphoreType.DMA((4,)),
                pltpu.SemaphoreType.DMA((3, 3)),
                pltpu.SemaphoreType.DMA((5,)),
            ],
        ),
        input_output_aliases=aliases,
        compiler_params=pltpu.CompilerParams(vmem_limit_bytes=VMEM_LIMIT),
        cost_estimate=pl.CostEstimate(flops=3 * (sending + keeping) * (count + extra) * depth * wide, bytes_accessed=0, transcendentals=0),
        name="products",
    )(slots, *args)


def finish_kernel(m, start, width, slots_ref, rows_ref, tokens_ref, own_ref, got_ref, gate_ref, *refs):
    grown_ref, last_ref = refs[2 if m else 1:][:2]
    factors_ref, panels_ref, got_buf, gate_buf, slab_ref, extra_ref, sems = refs[2 if m else 1:][2:]
    block = own_ref.shape[0]
    count = rows_ref.shape[0]
    wide = panels_ref.shape[1]
    half = count // 2
    depth = factors_ref.shape[1]

    @pl.when(slots_ref[4] == 0)
    def _():
        side = pl.multiple_of(slots_ref[5] * depth, 128)
        place = pl.multiple_of(slots_ref[5] * block, 16)
        other = pl.multiple_of((1 - slots_ref[5]) * block, 16)
        copies = [
            pltpu.make_async_copy(own_ref, panels_ref.at[pl.ds(place, block), :], sems.at[0]),
            pltpu.make_async_copy(
                tokens_ref.at[:, pl.ds(side, depth)], factors_ref.at[pl.ds(count, tokens_ref.shape[0]), :], sems.at[1]),
            pltpu.make_async_copy(rows_ref.at[:, pl.ds(side, depth)], factors_ref.at[pl.ds(0, count), :], sems.at[2]),
            pltpu.make_async_copy(got_ref, got_buf, sems.at[3]),
        ]
        if m:
            copies.append(pltpu.make_async_copy(gate_ref.at[:, pl.ds(start, tiled(width))], gate_buf, sems.at[4]))
        for copy in copies:
            copy.start()
        panels_ref[pl.ds(other, block), :] = jnp.zeros((block, wide), BF16)
        for copy in copies:
            copy.wait()

        def product(first, size):
            sums = jnp.dot(factors_ref[first:first + size, :], panels_ref[...], preferred_element_type=F32)
            return sums + got_buf[first:first + size, :].astype(F32)

        pre = product(count, tokens_ref.shape[0])
        if m:
            extra_ref[...] = gated(gate_buf[...], pre).T
            end = pltpu.make_async_copy(
                extra_ref.at[:width, :], last_ref.at[pl.ds(start, width), :], sems.at[0])
        else:
            extra_ref[...] = pre
            end = pltpu.make_async_copy(extra_ref, last_ref.at[:, pl.ds(start, tiled(width))], sems.at[0])
        end.start()
        for i in range(2):
            slab_ref[:, i * half:(i + 1) * half] = product(i * half, half).astype(BF16).T
        slab = pltpu.make_async_copy(
            slab_ref.at[:width, :], grown_ref.at[m, pl.ds(start, width), :], sems.at[1])
        slab.start()
        end.wait()
        slab.wait()


def finish(m, start, width, slots, mine, own, got, gate, grown, hidden, columns):
    rows, token_growth = mine
    count, depth = rows.shape
    extra = token_growth.shape[0]
    block, wide = own.shape
    args = [rows, token_growth, own, got, gate, grown] + ([hidden] if m else [])
    return pl.pallas_call(
        functools.partial(finish_kernel, m, start, width),
        out_shape=(
            jax.ShapeDtypeStruct((2, columns, count), BF16),
            jax.ShapeDtypeStruct((columns, extra), BF16) if m else jax.ShapeDtypeStruct((extra, tiled(columns)), F32),
        ),
        grid_spec=pltpu.PrefetchScalarGridSpec(
            num_scalar_prefetch=1,
            grid=(1,),
            in_specs=[ANY] * len(args),
            out_specs=(ANY, ANY),
            scratch_shapes=[
                pltpu.VMEM((count + extra, 2 * block), BF16),
                pltpu.VMEM((2 * block, wide), BF16),
                pltpu.VMEM((count + extra, wide), BF16),
                pltpu.VMEM((extra, wide), F32),
                pltpu.VMEM((wide, count), BF16),
                pltpu.VMEM((wide, extra), BF16) if m else pltpu.VMEM((extra, wide), F32),
                pltpu.SemaphoreType.DMA((5,)),
            ],
        ),
        input_output_aliases={6: 0, 7: 1} if m else {6: 0, 5: 1},
        compiler_params=pltpu.CompilerParams(vmem_limit_bytes=VMEM_LIMIT),
        cost_estimate=pl.CostEstimate(flops=0, bytes_accessed=0, transcendentals=0),
        name="finish",
    )(slots, *args)


def used_depth(depth):
    return tiled(3 * depth // 4)


def fetch_half(rows, parts):
    half, depth = rows.shape[0] // 2, rows.shape[1]
    core = lax.rem(lax.axis_index("tensor"), 2)
    first = jnp.where(lax.axis_index("dp") == 0, depth - used_depth(depth), 0)
    size = -(-half // parts // 16) * 16
    fetched = []
    for start in range(0, half, size):
        part = lax.dynamic_slice(rows, (core * half + start, first), (min(size, half - start), used_depth(depth)))
        fetched.append(lax.ppermute(after(part, *fetched[-1:]), "dp", TO_INNER))
    return fetched


def other_half(half):
    return lax.ppermute(half, "tensor", [(j, j ^ 1) for j in range(lax.axis_size("tensor"))])


def line_form(tokens, small_weights, ffn_growth, width_growth):
    columns = ffn_growth.shape[0]
    index = lax.axis_index("dp")
    is_inner = ((index == 1) | (index == 2)).astype(jnp.int32)
    core = lax.rem(lax.axis_index("tensor"), 2)
    slots = jnp.concatenate(
        [jnp.array(SLOTS, jnp.int32)[index], jnp.stack([is_inner, (index == 3).astype(jnp.int32), core])]
    )
    small = [lax.all_gather(small_weights[m], "tensor", axis=0, tiled=True) for m in range(2)]
    fetched = fetch_half(width_growth, 3)
    rows_half = jnp.concatenate(fetched, axis=0)
    token_growth = doubled(token_rows(tokens, width_growth, *fetched[:2]), *fetched[2:])
    token_half, = fetch_half(token_growth, 1)
    mine = (width_growth, token_growth)

    work = [(0, 0, WIDTH), (0, WIDTH, columns - WIDTH)]
    work += [(1, start, width) for start, width in pieces(columns, WIDTH)]
    own, outer, mate, far, out, received = ({} for _ in range(6))
    grown = gate = hidden = theirs = None

    def panel(chosen, *made):
        m = work[chosen[0]][0]
        source = after(small[m], *made) if made else small[m]
        for k, part in zip(chosen, panel_of(source, ffn_growth, [work[k][1:] for k in chosen])):
            own[k] = part

    def send(k, *made):
        sent = after(own[k], *made) if made else own[k]
        with jax.named_scope(f"outer{k}"):
            outer[k] = lax.ppermute(sent, "dp", TO_INNER)
        with jax.named_scope(f"mate{k}"):
            mate[k] = lax.ppermute(sent, "dp", SWAP_INNER)

    def forward(k, *made):
        outer[k] = after(outer[k], *made)
        with jax.named_scope(f"far{k}"):
            far[k] = lax.ppermute(outer[k], "dp", SWAP_INNER)

    def multiply(k, *made, sending=True, keeping=True):
        nonlocal grown, gate, hidden
        m, start, width = work[k]
        panels = [after(own[k], *made), outer[k], mate[k], far[k]]
        last = hidden if m else gate
        made = products(
            m, start, width, slots, mine, theirs, panels, gate, grown, last, columns, sending, keeping
        )
        if sending:
            out[k] = made[0]
            with jax.named_scope(f"sums{k}"):
                received[k] = lax.ppermute(out[k], "dp", TO_OUTER)
        if keeping:
            grown = made[-2]
            if m:
                hidden = made[-1]
            else:
                gate = made[-1]

    def conclude(k, *made):
        nonlocal grown, gate, hidden
        m, start, width = work[k]
        got = after(received[k], *made) if made else received[k]
        grown, last = finish(m, start, width, slots, mine, own[k], got, gate, grown, hidden, columns)
        if m:
            hidden = last
        else:
            gate = last

    panel([0])
    send(0)
    panel([1], own[0], token_growth)
    forward(0, mate[0], own[1])
    token_half = after(token_half, outer[0])
    theirs = (rows_half, other_half(rows_half), token_half, other_half(token_half))
    send(1, outer[0])
    multiply(0, far[0])
    forward(1, out[0])
    panel([2], outer[1], out[0], mate[1])
    send(2)
    panel([3, 4], own[2], received[0])
    forward(2, own[3], mate[1])
    send(3, outer[2])
    conclude(0)
    multiply(1, outer[2])
    multiply(2, out[1], mate[3])
    forward(3, out[2])
    send(4, outer[3])
    conclude(1)
    multiply(3, outer[3])
    forward(4, out[3])
    conclude(2)
    multiply(4, out[3], received[2], keeping=False)
    multiply(4, out[4], sending=False)
    conclude(3)
    conclude(4)
    return jnp.swapaxes(grown, 1, 2), hidden.T


def solution(mesh):
    placed = (P("dp", "tensor"), P(None, ("dp", "tensor"), None), P("tensor", None), P("dp", None))
    return jax.shard_map(
        line_form if mesh.shape["dp"] == 4 else gathered_form,
        mesh=mesh,
        in_specs=placed,
        out_specs=(P(None, "dp", "tensor"), P("dp", "tensor")),
        check_vma=False,
    )
```

```python
import functools

import jax
import jax.numpy as jnp
from jax import lax
from jax.experimental import pallas as pl
from jax.experimental.pallas import tpu as pltpu
from jax.sharding import PartitionSpec as P

BF16, F32 = jnp.bfloat16, jnp.float32
WIDTH = 512
VMEM_LIMIT = 56 * 1024 * 1024
ANY = pl.BlockSpec(memory_space=pl.ANY)


def pieces(extent, width):
    starts = list(range(0, extent, width))
    return [(start, min(width, extent - start)) for start in starts]


def after(array, *made):
    return lax.optimization_barrier((array,) + made)[0]


def token_rows(tokens, width_growth, *fetched):
    nd = lax.axis_size("dp")
    by_rows = lax.all_to_all(tokens, "tensor", 0, 1, tiled=True)
    by_features = lax.all_to_all(by_rows, "dp", 1, 0, tiled=True)
    by_features = after(by_features, *fetched[:1])
    part = jnp.dot(by_features, width_growth, preferred_element_type=F32).astype(BF16)
    parts = lax.all_to_all(part, "dp", 0, 0, tiled=True)
    return jnp.sum(parts.reshape(nd, -1, parts.shape[1]).astype(F32), axis=0).astype(BF16)


def swap(rows, bit):
    return lax.ppermute(rows, "tensor", [(j, j ^ bit) for j in range(lax.axis_size("tensor"))])


def joined(rows, got, bit):
    low = (lax.axis_index("tensor") // bit) % 2 == 0
    return jnp.concatenate([jnp.where(low, rows, got), jnp.where(low, got, rows)], axis=0)


def gathered_form(tokens, small_weights, ffn_growth, width_growth):
    columns = ffn_growth.shape[0]
    small = [lax.all_gather(small_weights[m], "tensor", axis=0, tiled=True) for m in range(2)]
    token_growth = lax.all_gather(token_rows(tokens, width_growth), "tensor", axis=0, tiled=True)
    grown, pre = [], []
    for m in range(2):
        grown_parts, pre_parts = [], []
        for start, width in pieces(columns, WIDTH):
            panel = jnp.einsum(
                "sf,cf->sc", small[m], ffn_growth[start:start + width], preferred_element_type=F32
            ).astype(BF16)
            panels = lax.all_gather(panel, "dp", axis=0, tiled=True)
            grown_parts.append(jnp.dot(width_growth, panels, preferred_element_type=F32).astype(BF16))
            pre_parts.append(jnp.dot(token_growth, panels, preferred_element_type=F32))
        grown.append(jnp.concatenate(grown_parts, axis=1))
        pre.append(jnp.concatenate(pre_parts, axis=1))
    hidden = (jax.nn.silu(pre[0]) * pre[1]).astype(BF16)
    return (jnp.stack(grown), hidden)


SWAP_INNER = [(1, 2), (2, 1)]
TO_INNER = [(0, 1), (3, 2)]
TO_OUTER = [(1, 0), (2, 3)]
SLOTS = [[0, 1, 2, 3], [1, 0, 2, 3], [2, 3, 1, 0], [3, 0, 1, 2]]


def panel_kernel(steps, splits, small_ref, growth_ref, *refs):
    out_refs, acc_ref = refs[:-1], refs[-1]
    step = pl.program_id(0)
    part = lax.dot_general(
        small_ref[...], growth_ref[...], (((1,), (1,)), ((), ())), preferred_element_type=F32
    )

    @pl.when(step == 0)
    def _():
        acc_ref[...] = part

    @pl.when((step > 0) & (step < steps - 1))
    def _():
        acc_ref[...] += part

    @pl.when(step == steps - 1)
    def _():
        total = acc_ref[...] + part
        for (start, width), out_ref in zip(splits, out_refs):
            wide = out_ref.shape[1]
            piece = total[:, start - splits[0][0]:start - splits[0][0] + wide]
            if width < wide:
                column = lax.broadcasted_iota(jnp.int32, piece.shape, 1)
                piece = jnp.where(column < width, piece, 0.0)
            out_ref[...] = piece.astype(BF16)


def tiled(width):
    return -(-width // 128) * 128


def panel_of(small, growth, splits):
    rows, depth = small.shape
    first = splits[0][0]
    wide = tiled(splits[-1][0] + splits[-1][1] - first)
    steps = 7
    deep = depth // steps
    return pl.pallas_call(
        functools.partial(panel_kernel, steps, splits),
        out_shape=[jax.ShapeDtypeStruct((rows, tiled(width)), BF16) for _, width in splits],
        grid=(steps,),
        in_specs=[
            pl.BlockSpec((rows, deep), lambda k: (0, k)),
            pl.BlockSpec((pl.Element(wide, (0, max(0, first + wide - growth.shape[0]))), pl.Element(deep)), lambda k: (first, k * deep)),
        ],
        out_specs=[pl.BlockSpec((rows, tiled(width)), lambda k: (0, 0)) for _, width in splits],
        scratch_shapes=[pltpu.VMEM((rows, wide), F32)],
        compiler_params=pltpu.CompilerParams(vmem_limit_bytes=VMEM_LIMIT),
        cost_estimate=pl.CostEstimate(flops=3 * rows * depth * wide, bytes_accessed=0, transcendentals=0),
        name="panel",
    )(small, growth)


def gated(gate, up):
    return (gate / (1.0 + jnp.exp(-gate)) * up).astype(BF16)


def products_kernel(m, start, width, sending, keeping, slots_ref, *refs):
    refs = list(refs)
    theirs, their_tokens = (refs.pop(0), refs.pop(0)), (refs.pop(0), refs.pop(0))
    rows_ref, tokens_ref = refs.pop(0), refs.pop(0)
    sources = [refs.pop(0) for _ in range(4)]
    if keeping:
        if m:
            gate_ref = refs.pop(0)
        if m or start:
            refs.pop(0)
        if start:
            refs.pop(0)
    if sending:
        out_ref = refs.pop(0)
    if keeping:
        grown_ref, last_ref = refs.pop(0), refs.pop(0)
    panels_ref, factors_ref, stage_ref, slab_ref, extra_ref, gate_buf, sems, factor_sems, end_sems = refs
    block = sources[0].shape[0]
    count = rows_ref.shape[0]
    extra = tokens_ref.shape[0]
    half, few = count // 2, extra // 2
    depth, used = panels_ref.shape[0], their_tokens[0].shape[1]

    def placed(s):
        row = pl.multiple_of(slots_ref[s] * block, 16)
        return pltpu.make_async_copy(sources[s], panels_ref.at[pl.ds(row, block), :], sems.at[s])

    def from_either(pair, i, buffer, offset, sem):
        size = pair[0].shape[0]
        copies = [
            pltpu.make_async_copy(ref, factors_ref.at[buffer, pl.ds(offset, size), pl.ds(0, used)], sem) for ref in pair
        ]
        mine = slots_ref[6] == i

        @pl.when(mine)
        def _():
            copies[0].start()

        @pl.when(jnp.logical_not(mine))
        def _():
            copies[1].start()

        return copies[0]

    def plain(ref, first, size, buffer, offset, sem):
        copy = pltpu.make_async_copy(
            ref.at[pl.ds(first, size), :], factors_ref.at[buffer, pl.ds(offset, size), :], sem
        )
        copy.start()
        return copy

    work = ["sent", "sent", "tokens", "kept", "kept"][0 if sending else 2:5 if keeping else 3]
    place = {"sent": 0, "kept": 0}

    def fetch(i):
        buffer = i % 3
        sem = [factor_sems.at[buffer, j] for j in range(3)]
        if work[i] == "sent":
            place["sent"] += 1
            return [from_either(theirs, place["sent"] - 1, buffer, 0, sem[0])]
        if work[i] == "kept":
            place["kept"] += 1
            return [plain(rows_ref, (place["kept"] - 1) * half, half, buffer, 0, sem[0])]
        copies = []
        if sending:
            copies.append(from_either(their_tokens, 0, buffer, 0, sem[0]))
            copies.append(from_either(their_tokens, 1, buffer, few, sem[1]))
        if keeping:
            copies.append(plain(tokens_ref, 0, extra, buffer, extra, sem[2]))
        return copies

    def product(buffer, first, size):
        return jnp.dot(factors_ref[buffer, first:first + size, :], panels_ref[...], preferred_element_type=F32)

    def product_out(buffer, size):
        row = pl.multiple_of(jnp.where(slots_ref[0] == 1, depth - used, 0), 128)
        return jnp.dot(
            factors_ref[buffer, :size, :used], panels_ref[pl.ds(row, used), :], preferred_element_type=F32
        )

    @pl.when(slots_ref[4] == 1)
    def _():
        first = [placed(s) for s in ((0, 2, 3) if sending else (0, 1, 2, 3))]
        for copy in first:
            copy.start()
        coming = [fetch(0), fetch(1)]
        if sending:
            outer_row = pl.multiple_of(slots_ref[1] * block, 16)
            panels_ref[pl.ds(outer_row, block), :] = jnp.zeros((block, panels_ref.shape[1]), BF16)
        if m and keeping:
            gate_copy = pltpu.make_async_copy(
                gate_ref.at[:, pl.ds(start, tiled(width))], gate_buf, end_sems.at[4])
            gate_copy.start()
        for copy in first:
            copy.wait()
        ends = []

        def finished(source, target):
            copy = pltpu.make_async_copy(source, target, end_sems.at[len(ends)])
            copy.start()
            ends.append(copy)

        done = {"sent": 0, "kept": 0}
        for i, kind in enumerate(work):
            if i + 2 < len(work):
                coming.append(fetch(i + 2))
            for copy in coming[i]:
                copy.wait()
            if kind == "sent":
                stage_ref[done[kind] * half:(done[kind] + 1) * half, :] = product_out(i % 3, half).astype(BF16)
                done[kind] += 1
            elif kind == "kept":
                part = slice(done[kind] * half, (done[kind] + 1) * half)
                slab_ref[:, part] = product(i % 3, 0, half).astype(BF16).T
                done[kind] += 1
            else:
                if sending:
                    stage_ref[count:, :] = product_out(i % 3, extra).astype(BF16)
                    finished(stage_ref, out_ref)
                if sending and keeping:
                    outer = placed(1)
                    outer.start()
                    outer.wait()
                if keeping:
                    pre = product(i % 3, extra, extra)
                    if m:
                        gate_copy.wait()
                        extra_ref[...] = gated(gate_buf[...], pre).T
                        finished(extra_ref.at[:width, :], last_ref.at[pl.ds(start, width), :])
                    else:
                        extra_ref[...] = pre
                        finished(extra_ref, last_ref.at[:, pl.ds(start, tiled(width))])
        if keeping:
            finished(slab_ref.at[:width, :], grown_ref.at[m, pl.ds(start, width), :])
        for copy in ends:
            copy.wait()


def products(m, start, width, slots, mine, theirs, panels, gate, grown, last, columns, sending, keeping):
    rows, token_growth = mine
    count, depth = rows.shape
    extra = token_growth.shape[0]
    block, wide = panels[0].shape
    args = [*theirs, rows, token_growth, *panels]
    aliases = {}
    if keeping and m:
        args.append(gate)
    if keeping and grown is not None:
        aliases[len(args) + 1] = int(sending)
        args.append(grown)
    if keeping and last is not None:
        aliases[len(args) + 1] = int(sending) + 1
        args.append(last)
    out_shape = []
    if sending:
        out_shape.append(jax.ShapeDtypeStruct((count + extra, wide), BF16))
    if keeping:
        out_shape.append(jax.ShapeDtypeStruct((2, columns, count), BF16))
        out_shape.append(
            jax.ShapeDtypeStruct((columns, extra), BF16) if m else jax.ShapeDtypeStruct((extra, tiled(columns)), F32)
        )
    return pl.pallas_call(
        functools.partial(products_kernel, m, start, width, sending, keeping),
        out_shape=out_shape,
        grid_spec=pltpu.PrefetchScalarGridSpec(
            num_scalar_prefetch=1,
            grid=(1,),
            in_specs=[ANY] * len(args),
            out_specs=[ANY] * len(out_shape),
            scratch_shapes=[
                pltpu.VMEM((depth, wide), BF16),
                pltpu.VMEM((3, count // 2, depth), BF16),
                pltpu.VMEM((count + extra, wide), BF16),
                pltpu.VMEM((wide, count), BF16),
                pltpu.VMEM((wide, extra), BF16) if m else pltpu.VMEM((extra, wide), F32),
                pltpu.VMEM((extra, wide), F32),
                pltpu.SemaphoreType.DMA((4,)),
                pltpu.SemaphoreType.DMA((3, 3)),
                pltpu.SemaphoreType.DMA((5,)),
            ],
        ),
        input_output_aliases=aliases,
        compiler_params=pltpu.CompilerParams(vmem_limit_bytes=VMEM_LIMIT),
        cost_estimate=pl.CostEstimate(flops=3 * (sending + keeping) * (count + extra) * depth * wide, bytes_accessed=0, transcendentals=0),
        name="products",
    )(slots, *args)


def finish_kernel(m, start, width, slots_ref, rows_ref, tokens_ref, own_ref, got_ref, gate_ref, *refs):
    grown_ref, last_ref = refs[2 if m else 1:][:2]
    factors_ref, panels_ref, got_buf, gate_buf, slab_ref, extra_ref, sems = refs[2 if m else 1:][2:]
    block = own_ref.shape[0]
    count = rows_ref.shape[0]
    wide = panels_ref.shape[1]
    half = count // 2
    depth = factors_ref.shape[1]

    @pl.when(slots_ref[4] == 0)
    def _():
        side = pl.multiple_of(slots_ref[5] * depth, 128)
        place = pl.multiple_of(slots_ref[5] * block, 16)
        other = pl.multiple_of((1 - slots_ref[5]) * block, 16)
        copies = [
            pltpu.make_async_copy(own_ref, panels_ref.at[pl.ds(place, block), :], sems.at[0]),
            pltpu.make_async_copy(
                tokens_ref.at[:, pl.ds(side, depth)], factors_ref.at[pl.ds(count, tokens_ref.shape[0]), :], sems.at[1]),
            pltpu.make_async_copy(rows_ref.at[:, pl.ds(side, depth)], factors_ref.at[pl.ds(0, count), :], sems.at[2]),
            pltpu.make_async_copy(got_ref, got_buf, sems.at[3]),
        ]
        if m:
            copies.append(pltpu.make_async_copy(gate_ref.at[:, pl.ds(start, tiled(width))], gate_buf, sems.at[4]))
        for copy in copies:
            copy.start()
        panels_ref[pl.ds(other, block), :] = jnp.zeros((block, wide), BF16)
        for copy in copies:
            copy.wait()

        def product(first, size):
            sums = jnp.dot(factors_ref[first:first + size, :], panels_ref[...], preferred_element_type=F32)
            return sums + got_buf[first:first + size, :].astype(F32)

        pre = product(count, tokens_ref.shape[0])
        if m:
            extra_ref[...] = gated(gate_buf[...], pre).T
            end = pltpu.make_async_copy(
                extra_ref.at[:width, :], last_ref.at[pl.ds(start, width), :], sems.at[0])
        else:
            extra_ref[...] = pre
            end = pltpu.make_async_copy(extra_ref, last_ref.at[:, pl.ds(start, tiled(width))], sems.at[0])
        end.start()
        for i in range(2):
            slab_ref[:, i * half:(i + 1) * half] = product(i * half, half).astype(BF16).T
        slab = pltpu.make_async_copy(
            slab_ref.at[:width, :], grown_ref.at[m, pl.ds(start, width), :], sems.at[1])
        slab.start()
        end.wait()
        slab.wait()


def finish(m, start, width, slots, mine, own, got, gate, grown, hidden, columns):
    rows, token_growth = mine
    count, depth = rows.shape
    extra = token_growth.shape[0]
    block, wide = own.shape
    args = [rows, token_growth, own, got, gate, grown] + ([hidden] if m else [])
    return pl.pallas_call(
        functools.partial(finish_kernel, m, start, width),
        out_shape=(
            jax.ShapeDtypeStruct((2, columns, count), BF16),
            jax.ShapeDtypeStruct((columns, extra), BF16) if m else jax.ShapeDtypeStruct((extra, tiled(columns)), F32),
        ),
        grid_spec=pltpu.PrefetchScalarGridSpec(
            num_scalar_prefetch=1,
            grid=(1,),
            in_specs=[ANY] * len(args),
            out_specs=(ANY, ANY),
            scratch_shapes=[
                pltpu.VMEM((count + extra, 2 * block), BF16),
                pltpu.VMEM((2 * block, wide), BF16),
                pltpu.VMEM((count + extra, wide), BF16),
                pltpu.VMEM((extra, wide), F32),
                pltpu.VMEM((wide, count), BF16),
                pltpu.VMEM((wide, extra), BF16) if m else pltpu.VMEM((extra, wide), F32),
                pltpu.SemaphoreType.DMA((5,)),
            ],
        ),
        input_output_aliases={6: 0, 7: 1} if m else {6: 0, 5: 1},
        compiler_params=pltpu.CompilerParams(vmem_limit_bytes=VMEM_LIMIT),
        cost_estimate=pl.CostEstimate(flops=0, bytes_accessed=0, transcendentals=0),
        name="finish",
    )(slots, *args)


def used_depth(depth):
    return tiled(3 * depth // 4)


def fetch_half(rows, parts):
    half, depth = rows.shape[0] // 2, rows.shape[1]
    core = lax.rem(lax.axis_index("tensor"), 2)
    first = jnp.where(lax.axis_index("dp") == 0, depth - used_depth(depth), 0)
    size = -(-half // parts // 16) * 16
    fetched = []
    for start in range(0, half, size):
        part = lax.dynamic_slice(rows, (core * half + start, first), (min(size, half - start), used_depth(depth)))
        fetched.append(lax.ppermute(after(part, *fetched[-1:]), "dp", TO_INNER))
    return fetched


def line_form(tokens, small_weights, ffn_growth, width_growth):
    columns = ffn_growth.shape[0]
    index = lax.axis_index("dp")
    is_inner = ((index == 1) | (index == 2)).astype(jnp.int32)
    core = lax.rem(lax.axis_index("tensor"), 2)
    slots = jnp.concatenate(
        [jnp.array(SLOTS, jnp.int32)[index], jnp.stack([is_inner, (index == 3).astype(jnp.int32), core])]
    )
    small = [lax.all_gather(small_weights[m], "tensor", axis=0, tiled=True) for m in range(2)]
    fetched = fetch_half(width_growth, 3)
    token_share = token_rows(tokens, width_growth, fetched[0])
    token_share = joined(token_share, swap(token_share, 1), 1)
    token_share = joined(token_share, swap(token_share, 2), 2)
    token_rest = swap(token_share, 4)

    work = [(0, start, width) for start, width in pieces(columns, 768)]
    work += [(1, start, width) for start, width in pieces(columns, WIDTH)]
    own, outer, mate, far, out, received = ({} for _ in range(6))
    grown = gate = hidden = theirs = None

    def panel(chosen, *made):
        m = work[chosen[0]][0]
        source = after(small[m], *made) if made else small[m]
        for k, part in zip(chosen, panel_of(source, ffn_growth, [work[k][1:] for k in chosen])):
            own[k] = part

    def send(k, *made):
        sent = after(own[k], *made) if made else own[k]
        with jax.named_scope(f"outer{k}"):
            outer[k] = lax.ppermute(sent, "dp", TO_INNER)
        with jax.named_scope(f"mate{k}"):
            mate[k] = lax.ppermute(sent, "dp", SWAP_INNER)

    def forward(k, *made):
        outer[k] = after(outer[k], *made)
        with jax.named_scope(f"far{k}"):
            far[k] = lax.ppermute(outer[k], "dp", SWAP_INNER)

    def multiply(k, *made, sending=True, keeping=True):
        nonlocal grown, gate, hidden
        m, start, width = work[k]
        panels = [after(own[k], *made), outer[k], mate[k], far[k]]
        last = hidden if m else gate
        made = products(
            m, start, width, slots, mine, theirs, panels, gate, grown, last, columns, sending, keeping
        )
        if sending:
            out[k] = made[0]
            with jax.named_scope(f"sums{k}"):
                received[k] = lax.ppermute(out[k], "dp", TO_OUTER)
        if keeping:
            grown = made[-2]
            if m:
                hidden = made[-1]
            else:
                gate = made[-1]

    def conclude(k, *made):
        nonlocal grown, gate, hidden
        m, start, width = work[k]
        got = after(received[k], *made) if made else received[k]
        grown, last = finish(m, start, width, slots, mine, own[k], got, gate, grown, hidden, columns)
        if m:
            hidden = last
        else:
            gate = last

    panel([0], fetched[1], token_share)
    token_growth = joined(token_share, after(token_rest, own[0]), 4)
    token_half, = fetch_half(token_growth, 1)
    mine = (width_growth, token_growth)
    rows_half = jnp.concatenate(fetched[:2] + [after(fetched[2], own[0])], axis=0)
    send(0)
    panel([1], own[0], token_growth, rows_half)
    forward(0, mate[0], own[1])
    token_half = after(token_half, own[1])
    theirs = (rows_half, swap(rows_half, 1), token_half, swap(token_half, 1))
    send(1, outer[0])
    multiply(0, far[0])
    forward(1, out[0])
    panel([2], outer[1], out[0], mate[1])
    send(2)
    panel([3, 4], own[2], received[0])
    forward(2, own[3], mate[1])
    send(3, outer[2])
    conclude(0)
    multiply(1, outer[2])
    multiply(2, out[1], mate[3])
    forward(3, out[2])
    send(4, outer[3])
    conclude(1)
    multiply(3, outer[3])
    forward(4, out[3])
    conclude(2)
    multiply(4, out[3], received[2], keeping=False)
    multiply(4, out[4], sending=False)
    conclude(3)
    conclude(4)
    return jnp.swapaxes(grown, 1, 2), hidden.T


def solution(mesh):
    placed = (P("dp", "tensor"), P(None, ("dp", "tensor"), None), P("tensor", None), P("dp", None))
    return jax.shard_map(
        line_form if mesh.shape["dp"] == 4 else gathered_form,
        mesh=mesh,
        in_specs=placed,
        out_specs=(P(None, "dp", "tensor"), P("dp", "tensor")),
        check_vma=False,
    )
```

```python
import functools

import jax
import jax.numpy as jnp
from jax import lax
from jax.experimental import pallas as pl
from jax.experimental.pallas import tpu as pltpu
from jax.sharding import PartitionSpec as P

BF16, F32 = jnp.bfloat16, jnp.float32
WIDTH = 512
DEEP = 1280
VMEM_LIMIT = 56 * 1024 * 1024
ANY = pl.BlockSpec(memory_space=pl.ANY)


def pieces(extent, width):
    starts = list(range(0, extent, width))
    return [(start, min(width, extent - start)) for start in starts]


def after(array, *made):
    return lax.optimization_barrier((array,) + made)[0]


def token_rows(tokens, width_growth, *fetched):
    nd = lax.axis_size("dp")
    by_rows = lax.all_to_all(tokens, "tensor", 0, 1, tiled=True)
    by_features = lax.all_to_all(by_rows, "dp", 1, 0, tiled=True)
    by_features = after(by_features, *fetched[:1])
    part = jnp.dot(by_features, width_growth, preferred_element_type=F32).astype(BF16)
    parts = lax.all_to_all(part, "dp", 0, 0, tiled=True)
    return jnp.sum(parts.reshape(nd, -1, parts.shape[1]).astype(F32), axis=0).astype(BF16)


def swap(rows, bit):
    return lax.ppermute(rows, "tensor", [(j, j ^ bit) for j in range(lax.axis_size("tensor"))])


def joined(rows, got, bit):
    low = (lax.axis_index("tensor") // bit) % 2 == 0
    return jnp.concatenate([jnp.where(low, rows, got), jnp.where(low, got, rows)], axis=0)


def gathered_form(tokens, small_weights, ffn_growth, width_growth):
    columns = ffn_growth.shape[0]
    small = [lax.all_gather(small_weights[m], "tensor", axis=0, tiled=True) for m in range(2)]
    token_growth = lax.all_gather(token_rows(tokens, width_growth), "tensor", axis=0, tiled=True)
    grown, pre = [], []
    for m in range(2):
        grown_parts, pre_parts = [], []
        for start, width in pieces(columns, WIDTH):
            panel = jnp.einsum(
                "sf,cf->sc", small[m], ffn_growth[start:start + width], preferred_element_type=F32
            ).astype(BF16)
            panels = lax.all_gather(panel, "dp", axis=0, tiled=True)
            grown_parts.append(jnp.dot(width_growth, panels, preferred_element_type=F32).astype(BF16))
            pre_parts.append(jnp.dot(token_growth, panels, preferred_element_type=F32))
        grown.append(jnp.concatenate(grown_parts, axis=1))
        pre.append(jnp.concatenate(pre_parts, axis=1))
    hidden = (jax.nn.silu(pre[0]) * pre[1]).astype(BF16)
    return (jnp.stack(grown), hidden)


SWAP_INNER = [(1, 2), (2, 1)]
TO_INNER = [(0, 1), (3, 2)]
TO_OUTER = [(1, 0), (2, 3)]
SLOTS = [[0, 1, 2, 3], [1, 0, 2, 3], [2, 3, 1, 0], [3, 0, 1, 2]]


def panel_kernel(steps, splits, so_far, small_ref, growth_ref, *refs):
    start_ref = refs[0] if so_far else None
    out_refs, acc_ref = refs[so_far:-1], refs[-1]
    step = pl.program_id(0)
    part = lax.dot_general(
        small_ref[...], growth_ref[...], (((1,), (1,)), ((), ())), preferred_element_type=F32
    )

    @pl.when(step == 0)
    def _():
        acc_ref[...] = part + start_ref[...] if so_far else part

    @pl.when((step > 0) & (step < steps - 1))
    def _():
        acc_ref[...] += part

    @pl.when(step == steps - 1)
    def _():
        total = acc_ref[...] + part
        for (start, width), out_ref in zip(splits, out_refs):
            wide = out_ref.shape[1]
            piece = total[:, start - splits[0][0]:start - splits[0][0] + wide]
            if width < wide and out_ref.dtype == BF16:
                column = lax.broadcasted_iota(jnp.int32, piece.shape, 1)
                piece = jnp.where(column < width, piece, 0.0)
            out_ref[...] = piece.astype(out_ref.dtype)


def tiled(width):
    return -(-width // 128) * 128


def panel_of(small, growth, splits, depth_start=0, so_far=None, dtype=BF16):
    rows, depth = small.shape
    first = splits[0][0]
    wide = tiled(splits[-1][0] + splits[-1][1] - first)
    steps = depth // DEEP
    in_specs = [
        pl.BlockSpec((rows, DEEP), lambda k: (0, k)),
        pl.BlockSpec(
            (pl.Element(wide, (0, max(0, first + wide - growth.shape[0]))), pl.Element(DEEP)),
            lambda k: (first, (k + depth_start // DEEP) * DEEP),
        ),
    ]
    args = [small, growth]
    if so_far is not None:
        in_specs.append(pl.BlockSpec((rows, wide), lambda k: (0, 0)))
        args.append(so_far)
    return pl.pallas_call(
        functools.partial(panel_kernel, steps, splits, int(so_far is not None)),
        out_shape=[jax.ShapeDtypeStruct((rows, tiled(width)), dtype) for _, width in splits],
        grid=(steps,),
        in_specs=in_specs,
        out_specs=[pl.BlockSpec((rows, tiled(width)), lambda k: (0, 0)) for _, width in splits],
        scratch_shapes=[pltpu.VMEM((rows, wide), F32)],
        compiler_params=pltpu.CompilerParams(vmem_limit_bytes=VMEM_LIMIT),
        cost_estimate=pl.CostEstimate(flops=3 * rows * depth * wide, bytes_accessed=0, transcendentals=0),
        name="panel",
    )(*args)


def gated(gate, up):
    return (gate / (1.0 + jnp.exp(-gate)) * up).astype(BF16)


def products_kernel(m, start, width, sending, keeping, slots_ref, *refs):
    refs = list(refs)
    theirs, their_tokens = (refs.pop(0), refs.pop(0)), (refs.pop(0), refs.pop(0))
    rows_ref, tokens_ref = refs.pop(0), refs.pop(0)
    sources = [refs.pop(0) for _ in range(4)]
    if keeping:
        if m:
            gate_ref = refs.pop(0)
        if m or start:
            refs.pop(0)
        if start:
            refs.pop(0)
    if sending:
        out_ref = refs.pop(0)
    if keeping:
        grown_ref, last_ref = refs.pop(0), refs.pop(0)
    panels_ref, factors_ref, stage_ref, slab_ref, extra_ref, gate_buf, sems, factor_sems, end_sems = refs
    block = sources[0].shape[0]
    count = rows_ref.shape[0]
    extra = tokens_ref.shape[0]
    half, few = count // 2, extra // 2
    depth, used = panels_ref.shape[0], their_tokens[0].shape[1]

    def placed(s):
        row = pl.multiple_of(slots_ref[s] * block, 16)
        return pltpu.make_async_copy(sources[s], panels_ref.at[pl.ds(row, block), :], sems.at[s])

    def from_either(pair, i, buffer, offset, sem):
        size = pair[0].shape[0]
        copies = [
            pltpu.make_async_copy(ref, factors_ref.at[buffer, pl.ds(offset, size), pl.ds(0, used)], sem) for ref in pair
        ]
        mine = slots_ref[6] == i

        @pl.when(mine)
        def _():
            copies[0].start()

        @pl.when(jnp.logical_not(mine))
        def _():
            copies[1].start()

        return copies[0]

    def plain(ref, first, size, buffer, offset, sem):
        copy = pltpu.make_async_copy(
            ref.at[pl.ds(first, size), :], factors_ref.at[buffer, pl.ds(offset, size), :], sem
        )
        copy.start()
        return copy

    work = ["sent", "sent", "tokens", "kept", "kept"][0 if sending else 2:5 if keeping else 3]
    place = {"sent": 0, "kept": 0}

    def fetch(i):
        buffer = i % 3
        sem = [factor_sems.at[buffer, j] for j in range(3)]
        if work[i] == "sent":
            place["sent"] += 1
            return [from_either(theirs, place["sent"] - 1, buffer, 0, sem[0])]
        if work[i] == "kept":
            place["kept"] += 1
            return [plain(rows_ref, (place["kept"] - 1) * half, half, buffer, 0, sem[0])]
        copies = []
        if sending:
            copies.append(from_either(their_tokens, 0, buffer, 0, sem[0]))
            copies.append(from_either(their_tokens, 1, buffer, few, sem[1]))
        if keeping:
            copies.append(plain(tokens_ref, 0, extra, buffer, extra, sem[2]))
        return copies

    def product(buffer, first, size):
        return jnp.dot(factors_ref[buffer, first:first + size, :], panels_ref[...], preferred_element_type=F32)

    def product_out(buffer, size):
        row = pl.multiple_of(jnp.where(slots_ref[0] == 1, depth - used, 0), 128)
        return jnp.dot(
            factors_ref[buffer, :size, :used], panels_ref[pl.ds(row, used), :], preferred_element_type=F32
        )

    @pl.when(slots_ref[4] == 1)
    def _():
        first = [placed(s) for s in ((0, 2, 3) if sending else (0, 1, 2, 3))]
        for copy in first:
            copy.start()
        coming = [fetch(0), fetch(1)]
        if sending:
            outer_row = pl.multiple_of(slots_ref[1] * block, 16)
            panels_ref[pl.ds(outer_row, block), :] = jnp.zeros((block, panels_ref.shape[1]), BF16)
        if m and keeping:
            gate_copy = pltpu.make_async_copy(
                gate_ref.at[:, pl.ds(start, tiled(width))], gate_buf, end_sems.at[4])
            gate_copy.start()
        for copy in first:
            copy.wait()
        ends = []

        def finished(source, target):
            copy = pltpu.make_async_copy(source, target, end_sems.at[len(ends)])
            copy.start()
            ends.append(copy)

        done = {"sent": 0, "kept": 0}
        for i, kind in enumerate(work):
            if i + 2 < len(work):
                coming.append(fetch(i + 2))
            for copy in coming[i]:
                copy.wait()
            if kind == "sent":
                stage_ref[done[kind] * half:(done[kind] + 1) * half, :] = product_out(i % 3, half).astype(BF16)
                done[kind] += 1
            elif kind == "kept":
                part = slice(done[kind] * half, (done[kind] + 1) * half)
                slab_ref[:, part] = product(i % 3, 0, half).astype(BF16).T
                done[kind] += 1
            else:
                if sending:
                    stage_ref[count:, :] = product_out(i % 3, extra).astype(BF16)
                    finished(stage_ref, out_ref)
                if sending and keeping:
                    outer = placed(1)
                    outer.start()
                    outer.wait()
                if keeping:
                    pre = product(i % 3, extra, extra)
                    if m:
                        gate_copy.wait()
                        extra_ref[...] = gated(gate_buf[...], pre).T
                        finished(extra_ref.at[:width, :], last_ref.at[pl.ds(start, width), :])
                    else:
                        extra_ref[...] = pre
                        finished(extra_ref, last_ref.at[:, pl.ds(start, tiled(width))])
        if keeping:
            finished(slab_ref.at[:width, :], grown_ref.at[m, pl.ds(start, width), :])
        for copy in ends:
            copy.wait()


def products(m, start, width, slots, mine, theirs, panels, gate, grown, last, columns, sending, keeping):
    rows, token_growth = mine
    count, depth = rows.shape
    extra = token_growth.shape[0]
    block, wide = panels[0].shape
    args = [*theirs, rows, token_growth, *panels]
    aliases = {}
    if keeping and m:
        args.append(gate)
    if keeping and grown is not None:
        aliases[len(args) + 1] = int(sending)
        args.append(grown)
    if keeping and last is not None:
        aliases[len(args) + 1] = int(sending) + 1
        args.append(last)
    out_shape = []
    if sending:
        out_shape.append(jax.ShapeDtypeStruct((count + extra, wide), BF16))
    if keeping:
        out_shape.append(jax.ShapeDtypeStruct((2, columns, count), BF16))
        out_shape.append(
            jax.ShapeDtypeStruct((columns, extra), BF16) if m else jax.ShapeDtypeStruct((extra, tiled(columns)), F32)
        )
    return pl.pallas_call(
        functools.partial(products_kernel, m, start, width, sending, keeping),
        out_shape=out_shape,
        grid_spec=pltpu.PrefetchScalarGridSpec(
            num_scalar_prefetch=1,
            grid=(1,),
            in_specs=[ANY] * len(args),
            out_specs=[ANY] * len(out_shape),
            scratch_shapes=[
                pltpu.VMEM((depth, wide), BF16),
                pltpu.VMEM((3, count // 2, depth), BF16),
                pltpu.VMEM((count + extra, wide), BF16),
                pltpu.VMEM((wide, count), BF16),
                pltpu.VMEM((wide, extra), BF16) if m else pltpu.VMEM((extra, wide), F32),
                pltpu.VMEM((extra, wide), F32),
                pltpu.SemaphoreType.DMA((4,)),
                pltpu.SemaphoreType.DMA((3, 3)),
                pltpu.SemaphoreType.DMA((5,)),
            ],
        ),
        input_output_aliases=aliases,
        compiler_params=pltpu.CompilerParams(vmem_limit_bytes=VMEM_LIMIT),
        cost_estimate=pl.CostEstimate(flops=3 * (sending + keeping) * (count + extra) * depth * wide, bytes_accessed=0, transcendentals=0),
        name="products",
    )(slots, *args)


def finish_kernel(m, start, width, slots_ref, rows_ref, tokens_ref, own_ref, got_ref, gate_ref, *refs):
    grown_ref, last_ref = refs[2 if m else 1:][:2]
    factors_ref, panels_ref, got_buf, gate_buf, slab_ref, extra_ref, sems = refs[2 if m else 1:][2:]
    block = own_ref.shape[0]
    count = rows_ref.shape[0]
    wide = panels_ref.shape[1]
    half = count // 2
    depth = factors_ref.shape[1]

    @pl.when(slots_ref[4] == 0)
    def _():
        side = pl.multiple_of(slots_ref[5] * depth, 128)
        place = pl.multiple_of(slots_ref[5] * block, 16)
        other = pl.multiple_of((1 - slots_ref[5]) * block, 16)
        copies = [
            pltpu.make_async_copy(own_ref, panels_ref.at[pl.ds(place, block), :], sems.at[0]),
            pltpu.make_async_copy(
                tokens_ref.at[:, pl.ds(side, depth)], factors_ref.at[pl.ds(count, tokens_ref.shape[0]), :], sems.at[1]),
            pltpu.make_async_copy(rows_ref.at[:, pl.ds(side, depth)], factors_ref.at[pl.ds(0, count), :], sems.at[2]),
            pltpu.make_async_copy(got_ref, got_buf, sems.at[3]),
        ]
        if m:
            copies.append(pltpu.make_async_copy(gate_ref.at[:, pl.ds(start, tiled(width))], gate_buf, sems.at[4]))
        for copy in copies:
            copy.start()
        panels_ref[pl.ds(other, block), :] = jnp.zeros((block, wide), BF16)
        for copy in copies:
            copy.wait()

        def product(first, size):
            sums = jnp.dot(factors_ref[first:first + size, :], panels_ref[...], preferred_element_type=F32)
            return sums + got_buf[first:first + size, :].astype(F32)

        pre = product(count, tokens_ref.shape[0])
        if m:
            extra_ref[...] = gated(gate_buf[...], pre).T
            end = pltpu.make_async_copy(
                extra_ref.at[:width, :], last_ref.at[pl.ds(start, width), :], sems.at[0])
        else:
            extra_ref[...] = pre
            end = pltpu.make_async_copy(extra_ref, last_ref.at[:, pl.ds(start, tiled(width))], sems.at[0])
        end.start()
        for i in range(2):
            slab_ref[:, i * half:(i + 1) * half] = product(i * half, half).astype(BF16).T
        slab = pltpu.make_async_copy(
            slab_ref.at[:width, :], grown_ref.at[m, pl.ds(start, width), :], sems.at[1])
        slab.start()
        end.wait()
        slab.wait()


def finish(m, start, width, slots, mine, own, got, gate, grown, hidden, columns):
    rows, token_growth = mine
    count, depth = rows.shape
    extra = token_growth.shape[0]
    block, wide = own.shape
    args = [rows, token_growth, own, got, gate, grown] + ([hidden] if m else [])
    return pl.pallas_call(
        functools.partial(finish_kernel, m, start, width),
        out_shape=(
            jax.ShapeDtypeStruct((2, columns, count), BF16),
            jax.ShapeDtypeStruct((columns, extra), BF16) if m else jax.ShapeDtypeStruct((extra, tiled(columns)), F32),
        ),
        grid_spec=pltpu.PrefetchScalarGridSpec(
            num_scalar_prefetch=1,
            grid=(1,),
            in_specs=[ANY] * len(args),
            out_specs=(ANY, ANY),
            scratch_shapes=[
                pltpu.VMEM((count + extra, 2 * block), BF16),
                pltpu.VMEM((2 * block, wide), BF16),
                pltpu.VMEM((count + extra, wide), BF16),
                pltpu.VMEM((extra, wide), F32),
                pltpu.VMEM((wide, count), BF16),
                pltpu.VMEM((wide, extra), BF16) if m else pltpu.VMEM((extra, wide), F32),
                pltpu.SemaphoreType.DMA((5,)),
            ],
        ),
        input_output_aliases={6: 0, 7: 1} if m else {6: 0, 5: 1},
        compiler_params=pltpu.CompilerParams(vmem_limit_bytes=VMEM_LIMIT),
        cost_estimate=pl.CostEstimate(flops=0, bytes_accessed=0, transcendentals=0),
        name="finish",
    )(slots, *args)


def used_depth(depth):
    return tiled(3 * depth // 4)


def fetch_half(rows, parts):
    half, depth = rows.shape[0] // 2, rows.shape[1]
    core = lax.rem(lax.axis_index("tensor"), 2)
    first = jnp.where(lax.axis_index("dp") == 0, depth - used_depth(depth), 0)
    size = -(-half // parts // 16) * 16
    fetched = []
    for start in range(0, half, size):
        part = lax.dynamic_slice(rows, (core * half + start, first), (min(size, half - start), used_depth(depth)))
        fetched.append(lax.ppermute(after(part, *fetched[-1:]), "dp", TO_INNER))
    return fetched


def line_form(tokens, small_weights, ffn_growth, width_growth):
    columns = ffn_growth.shape[0]
    index = lax.axis_index("dp")
    is_inner = ((index == 1) | (index == 2)).astype(jnp.int32)
    core = lax.rem(lax.axis_index("tensor"), 2)
    slots = jnp.concatenate(
        [jnp.array(SLOTS, jnp.int32)[index], jnp.stack([is_inner, (index == 3).astype(jnp.int32), core])]
    )
    early = 5 * DEEP
    ranges = [small_weights[0, :, :early], small_weights[0, :, early:], small_weights[1]]
    small = [lax.all_gather(part, "tensor", axis=0, tiled=True) for part in ranges]
    fetched = fetch_half(width_growth, 1)
    token_share = token_rows(tokens, width_growth)
    token_share = joined(after(token_share, *fetched), swap(token_share, 1), 1)
    token_rest = swap(token_share, 2)

    work = [(m, start, width) for m in range(2) for start, width in pieces(columns, WIDTH)]
    own, outer, mate, far, out, received = ({} for _ in range(6))
    grown = gate = hidden = theirs = None

    def panel(chosen, *made):
        m = work[chosen[0]][0]
        splits = [work[k][1:] for k in chosen]
        source = after(small[m + 1], *made) if made else small[m + 1]
        if m:
            parts = panel_of(source, ffn_growth, splits)
        else:
            parts = panel_of(source, ffn_growth, splits, early, sums[chosen[0]])
        for k, part in zip(chosen, parts):
            own[k] = part

    def send(k, *made):
        sent = after(own[k], *made) if made else own[k]
        with jax.named_scope(f"outer{k}"):
            outer[k] = lax.ppermute(sent, "dp", TO_INNER)
        with jax.named_scope(f"mate{k}"):
            mate[k] = lax.ppermute(sent, "dp", SWAP_INNER)

    def forward(k, *made):
        outer[k] = after(outer[k], *made)
        with jax.named_scope(f"far{k}"):
            far[k] = lax.ppermute(outer[k], "dp", SWAP_INNER)

    def multiply(k, *made, sending=True, keeping=True):
        nonlocal grown, gate, hidden
        m, start, width = work[k]
        panels = [after(own[k], *made), outer[k], mate[k], far[k]]
        last = hidden if m else gate
        made = products(
            m, start, width, slots, mine, theirs, panels, gate, grown, last, columns, sending, keeping
        )
        if sending:
            out[k] = made[0]
            with jax.named_scope(f"sums{k}"):
                received[k] = lax.ppermute(out[k], "dp", TO_OUTER)
        if keeping:
            grown = made[-2]
            if m:
                hidden = made[-1]
            else:
                gate = made[-1]

    def conclude(k, *made):
        nonlocal grown, gate, hidden
        m, start, width = work[k]
        got = after(received[k], *made) if made else received[k]
        grown, last = finish(m, start, width, slots, mine, own[k], got, gate, grown, hidden, columns)
        if m:
            hidden = last
        else:
            gate = last

    sums = {}
    halves = [(0, WIDTH), (WIDTH, columns - WIDTH)]
    sums[0], sums[1] = panel_of(after(small[0], token_share), ffn_growth, halves, dtype=F32)
    token_share = joined(token_share, after(token_rest, sums[0]), 2)
    token_rest = swap(token_share, 4)
    panel([0], token_share, *fetched)
    token_growth = joined(token_share, after(token_rest, own[0]), 4)
    token_half, = fetch_half(token_growth, 1)
    mine = (width_growth, token_growth)
    rows_half = jnp.concatenate(fetched, axis=0)
    send(0)
    panel([1, 2], own[0], token_growth)
    forward(0, mate[0], own[1])
    token_half = after(token_half, own[1])
    theirs = (rows_half, swap(rows_half, 1), token_half, swap(token_half, 1))
    send(1, outer[0])
    multiply(0, far[0])
    forward(1, out[0])
    send(2, outer[1])
    multiply(1, outer[1])
    forward(2, out[1])
    panel([3], outer[2], out[1])
    send(3)
    panel([4, 5], own[3])
    conclude(0)
    multiply(2, own[4], received[1])
    forward(3, out[2], mate[3])
    send(4, outer[3])
    conclude(1)
    multiply(3, outer[3], far[3])
    forward(4, out[3])
    send(5, outer[4])
    conclude(2)
    multiply(4, outer[4])
    forward(5, out[4])
    conclude(3)
    multiply(5, out[4], received[3], keeping=False)
    multiply(5, out[5], sending=False)
    conclude(4)
    conclude(5)
    return jnp.swapaxes(grown, 1, 2), hidden.T


def solution(mesh):
    placed = (P("dp", "tensor"), P(None, ("dp", "tensor"), None), P("tensor", None), P("dp", None))
    return jax.shard_map(
        line_form if mesh.shape["dp"] == 4 else gathered_form,
        mesh=mesh,
        in_specs=placed,
        out_specs=(P(None, "dp", "tensor"), P("dp", "tensor")),
        check_vma=False,
    )
```

```python
import functools

import jax
import jax.numpy as jnp
from jax import lax
from jax.experimental import pallas as pl
from jax.experimental.pallas import tpu as pltpu
from jax.sharding import PartitionSpec as P

BF16, F32 = jnp.bfloat16, jnp.float32
WIDTH = 512
VMEM_LIMIT = 56 * 1024 * 1024
ANY = pl.BlockSpec(memory_space=pl.ANY)


def pieces(extent, width):
    starts = list(range(0, extent, width))
    return [(start, min(width, extent - start)) for start in starts]


def after(array, *made):
    return lax.optimization_barrier((array,) + made)[0]


def token_rows(tokens, width_growth, *fetched):
    nd = lax.axis_size("dp")
    by_rows = lax.all_to_all(tokens, "tensor", 0, 1, tiled=True)
    by_features = lax.all_to_all(by_rows, "dp", 1, 0, tiled=True)
    by_features = after(by_features, *fetched[:1])
    part = jnp.dot(by_features, width_growth, preferred_element_type=F32).astype(BF16)
    parts = lax.all_to_all(part, "dp", 0, 0, tiled=True)
    return jnp.sum(parts.reshape(nd, -1, parts.shape[1]).astype(F32), axis=0).astype(BF16)


def swap(rows, bit):
    return lax.ppermute(rows, "tensor", [(j, j ^ bit) for j in range(lax.axis_size("tensor"))])


def joined(rows, got, bit):
    low = (lax.axis_index("tensor") // bit) % 2 == 0
    return jnp.concatenate([jnp.where(low, rows, got), jnp.where(low, got, rows)], axis=0)


def gathered_form(tokens, small_weights, ffn_growth, width_growth):
    columns = ffn_growth.shape[0]
    small = [lax.all_gather(small_weights[m], "tensor", axis=0, tiled=True) for m in range(2)]
    token_growth = lax.all_gather(token_rows(tokens, width_growth), "tensor", axis=0, tiled=True)
    grown, pre = [], []
    for m in range(2):
        grown_parts, pre_parts = [], []
        for start, width in pieces(columns, WIDTH):
            panel = jnp.einsum(
                "sf,cf->sc", small[m], ffn_growth[start:start + width], preferred_element_type=F32
            ).astype(BF16)
            panels = lax.all_gather(panel, "dp", axis=0, tiled=True)
            grown_parts.append(jnp.dot(width_growth, panels, preferred_element_type=F32).astype(BF16))
            pre_parts.append(jnp.dot(token_growth, panels, preferred_element_type=F32))
        grown.append(jnp.concatenate(grown_parts, axis=1))
        pre.append(jnp.concatenate(pre_parts, axis=1))
    hidden = (jax.nn.silu(pre[0]) * pre[1]).astype(BF16)
    return (jnp.stack(grown), hidden)


SWAP_INNER = [(1, 2), (2, 1)]
TO_INNER = [(0, 1), (3, 2)]
TO_OUTER = [(1, 0), (2, 3)]
SLOTS = [[0, 1, 2, 3], [1, 0, 2, 3], [2, 3, 1, 0], [3, 0, 1, 2]]


def panel_kernel(steps, splits, small_ref, growth_ref, *refs):
    out_refs, acc_ref = refs[:-1], refs[-1]
    step = pl.program_id(0)
    part = lax.dot_general(
        small_ref[...], growth_ref[...], (((1,), (1,)), ((), ())), preferred_element_type=F32
    )

    @pl.when(step == 0)
    def _():
        acc_ref[...] = part

    @pl.when((step > 0) & (step < steps - 1))
    def _():
        acc_ref[...] += part

    @pl.when(step == steps - 1)
    def _():
        total = acc_ref[...] + part
        for (start, width), out_ref in zip(splits, out_refs):
            wide = out_ref.shape[1]
            piece = total[:, start - splits[0][0]:start - splits[0][0] + wide]
            if width < wide:
                column = lax.broadcasted_iota(jnp.int32, piece.shape, 1)
                piece = jnp.where(column < width, piece, 0.0)
            out_ref[...] = piece.astype(BF16)


def tiled(width):
    return -(-width // 128) * 128


def panel_of(small, growth, splits):
    rows, depth = small.shape
    first = splits[0][0]
    wide = tiled(splits[-1][0] + splits[-1][1] - first)
    steps = 7
    deep = depth // steps
    return pl.pallas_call(
        functools.partial(panel_kernel, steps, splits),
        out_shape=[jax.ShapeDtypeStruct((rows, tiled(width)), BF16) for _, width in splits],
        grid=(steps,),
        in_specs=[
            pl.BlockSpec((rows, deep), lambda k: (0, k)),
            pl.BlockSpec((pl.Element(wide, (0, max(0, first + wide - growth.shape[0]))), pl.Element(deep)), lambda k: (first, k * deep)),
        ],
        out_specs=[pl.BlockSpec((rows, tiled(width)), lambda k: (0, 0)) for _, width in splits],
        scratch_shapes=[pltpu.VMEM((rows, wide), F32)],
        compiler_params=pltpu.CompilerParams(vmem_limit_bytes=VMEM_LIMIT),
        cost_estimate=pl.CostEstimate(flops=3 * rows * depth * wide, bytes_accessed=0, transcendentals=0),
        name="panel",
    )(small, growth)


def gated(gate, up):
    return (gate / (1.0 + jnp.exp(-gate)) * up).astype(BF16)


def products_kernel(m, start, width, sending, keeping, slots_ref, *refs):
    refs = list(refs)
    theirs, their_tokens = (refs.pop(0), refs.pop(0)), (refs.pop(0), refs.pop(0))
    rows_ref, tokens_ref = refs.pop(0), refs.pop(0)
    sources = [refs.pop(0) for _ in range(4)]
    if keeping:
        if m:
            gate_ref = refs.pop(0)
        if m or start:
            refs.pop(0)
        if start:
            refs.pop(0)
    if sending:
        out_ref = refs.pop(0)
    if keeping:
        grown_ref, last_ref = refs.pop(0), refs.pop(0)
    panels_ref, factors_ref, stage_ref, slab_ref, extra_ref, gate_buf, sems, factor_sems, end_sems = refs
    block = sources[0].shape[0]
    count = rows_ref.shape[0]
    extra = tokens_ref.shape[0]
    half, few = count // 2, extra // 2
    depth, used = panels_ref.shape[0], their_tokens[0].shape[1]

    def placed(s):
        row = pl.multiple_of(slots_ref[s] * block, 16)
        return pltpu.make_async_copy(sources[s], panels_ref.at[pl.ds(row, block), :], sems.at[s])

    def from_either(pair, i, buffer, offset, sem):
        size = pair[0].shape[0]
        copies = [
            pltpu.make_async_copy(ref, factors_ref.at[buffer, pl.ds(offset, size), pl.ds(0, used)], sem) for ref in pair
        ]
        mine = slots_ref[6] == i

        @pl.when(mine)
        def _():
            copies[0].start()

        @pl.when(jnp.logical_not(mine))
        def _():
            copies[1].start()

        return copies[0]

    def plain(ref, first, size, buffer, offset, sem):
        copy = pltpu.make_async_copy(
            ref.at[pl.ds(first, size), :], factors_ref.at[buffer, pl.ds(offset, size), :], sem
        )
        copy.start()
        return copy

    work = ["sent", "sent", "tokens", "kept", "kept"][0 if sending else 2:5 if keeping else 3]
    place = {"sent": 0, "kept": 0}

    def fetch(i):
        buffer = i % 3
        sem = [factor_sems.at[buffer, j] for j in range(3)]
        if work[i] == "sent":
            place["sent"] += 1
            return [from_either(theirs, place["sent"] - 1, buffer, 0, sem[0])]
        if work[i] == "kept":
            place["kept"] += 1
            return [plain(rows_ref, (place["kept"] - 1) * half, half, buffer, 0, sem[0])]
        copies = []
        if sending:
            copies.append(from_either(their_tokens, 0, buffer, 0, sem[0]))
            copies.append(from_either(their_tokens, 1, buffer, few, sem[1]))
        if keeping:
            copies.append(plain(tokens_ref, 0, extra, buffer, extra, sem[2]))
        return copies

    def product(buffer, first, size):
        return jnp.dot(factors_ref[buffer, first:first + size, :], panels_ref[...], preferred_element_type=F32)

    def product_out(buffer, size):
        row = pl.multiple_of(jnp.where(slots_ref[0] == 1, depth - used, 0), 128)
        return jnp.dot(
            factors_ref[buffer, :size, :used], panels_ref[pl.ds(row, used), :], preferred_element_type=F32
        )

    @pl.when(slots_ref[4] == 1)
    def _():
        first = [placed(s) for s in ((0, 2, 3) if sending else (0, 1, 2, 3))]
        for copy in first:
            copy.start()
        coming = [fetch(0), fetch(1)]
        if sending:
            outer_row = pl.multiple_of(slots_ref[1] * block, 16)
            panels_ref[pl.ds(outer_row, block), :] = jnp.zeros((block, panels_ref.shape[1]), BF16)
        if m and keeping:
            gate_copy = pltpu.make_async_copy(
                gate_ref.at[:, pl.ds(start, tiled(width))], gate_buf, end_sems.at[4])
            gate_copy.start()
        for copy in first:
            copy.wait()
        ends = []

        def finished(source, target):
            copy = pltpu.make_async_copy(source, target, end_sems.at[len(ends)])
            copy.start()
            ends.append(copy)

        done = {"sent": 0, "kept": 0}
        for i, kind in enumerate(work):
            if i + 2 < len(work):
                coming.append(fetch(i + 2))
            for copy in coming[i]:
                copy.wait()
            if kind == "sent":
                stage_ref[done[kind] * half:(done[kind] + 1) * half, :] = product_out(i % 3, half).astype(BF16)
                done[kind] += 1
            elif kind == "kept":
                part = slice(done[kind] * half, (done[kind] + 1) * half)
                slab_ref[:, part] = product(i % 3, 0, half).astype(BF16).T
                done[kind] += 1
            else:
                if sending:
                    stage_ref[count:, :] = product_out(i % 3, extra).astype(BF16)
                    finished(stage_ref, out_ref)
                if sending and keeping:
                    outer = placed(1)
                    outer.start()
                    outer.wait()
                if keeping:
                    pre = product(i % 3, extra, extra)
                    if m:
                        gate_copy.wait()
                        extra_ref[...] = gated(gate_buf[...], pre).T
                        finished(extra_ref.at[:width, :], last_ref.at[pl.ds(start, width), :])
                    else:
                        extra_ref[...] = pre
                        finished(extra_ref, last_ref.at[:, pl.ds(start, tiled(width))])
        if keeping:
            finished(slab_ref.at[:width, :], grown_ref.at[m, pl.ds(start, width), :])
        for copy in ends:
            copy.wait()


def products(m, start, width, slots, mine, theirs, panels, gate, grown, last, columns, sending, keeping):
    rows, token_growth = mine
    count, depth = rows.shape
    extra = token_growth.shape[0]
    block, wide = panels[0].shape
    args = [*theirs, rows, token_growth, *panels]
    aliases = {}
    if keeping and m:
        args.append(gate)
    if keeping and grown is not None:
        aliases[len(args) + 1] = int(sending)
        args.append(grown)
    if keeping and last is not None:
        aliases[len(args) + 1] = int(sending) + 1
        args.append(last)
    out_shape = []
    if sending:
        out_shape.append(jax.ShapeDtypeStruct((count + extra, wide), BF16))
    if keeping:
        out_shape.append(jax.ShapeDtypeStruct((2, columns, count), BF16))
        out_shape.append(
            jax.ShapeDtypeStruct((columns, extra), BF16) if m else jax.ShapeDtypeStruct((extra, tiled(columns)), F32)
        )
    return pl.pallas_call(
        functools.partial(products_kernel, m, start, width, sending, keeping),
        out_shape=out_shape,
        grid_spec=pltpu.PrefetchScalarGridSpec(
            num_scalar_prefetch=1,
            grid=(1,),
            in_specs=[ANY] * len(args),
            out_specs=[ANY] * len(out_shape),
            scratch_shapes=[
                pltpu.VMEM((depth, wide), BF16),
                pltpu.VMEM((3, count // 2, depth), BF16),
                pltpu.VMEM((count + extra, wide), BF16),
                pltpu.VMEM((wide, count), BF16),
                pltpu.VMEM((wide, extra), BF16) if m else pltpu.VMEM((extra, wide), F32),
                pltpu.VMEM((extra, wide), F32),
                pltpu.SemaphoreType.DMA((4,)),
                pltpu.SemaphoreType.DMA((3, 3)),
                pltpu.SemaphoreType.DMA((5,)),
            ],
        ),
        input_output_aliases=aliases,
        compiler_params=pltpu.CompilerParams(vmem_limit_bytes=VMEM_LIMIT),
        cost_estimate=pl.CostEstimate(flops=3 * (sending + keeping) * (count + extra) * depth * wide, bytes_accessed=0, transcendentals=0),
        name="products",
    )(slots, *args)


def finish_kernel(m, start, width, slots_ref, rows_ref, tokens_ref, own_ref, got_ref, gate_ref, *refs):
    grown_ref, last_ref = refs[2 if m else 1:][:2]
    factors_ref, panels_ref, got_buf, gate_buf, slab_ref, extra_ref, sems = refs[2 if m else 1:][2:]
    block = own_ref.shape[0]
    count = rows_ref.shape[0]
    wide = panels_ref.shape[1]
    half = count // 2
    depth = factors_ref.shape[1]

    @pl.when(slots_ref[4] == 0)
    def _():
        side = pl.multiple_of(slots_ref[5] * depth, 128)
        place = pl.multiple_of(slots_ref[5] * block, 16)
        other = pl.multiple_of((1 - slots_ref[5]) * block, 16)
        copies = [
            pltpu.make_async_copy(own_ref, panels_ref.at[pl.ds(place, block), :], sems.at[0]),
            pltpu.make_async_copy(
                tokens_ref.at[:, pl.ds(side, depth)], factors_ref.at[pl.ds(count, tokens_ref.shape[0]), :], sems.at[1]),
            pltpu.make_async_copy(rows_ref.at[:, pl.ds(side, depth)], factors_ref.at[pl.ds(0, count), :], sems.at[2]),
            pltpu.make_async_copy(got_ref, got_buf, sems.at[3]),
        ]
        if m:
            copies.append(pltpu.make_async_copy(gate_ref.at[:, pl.ds(start, tiled(width))], gate_buf, sems.at[4]))
        for copy in copies:
            copy.start()
        panels_ref[pl.ds(other, block), :] = jnp.zeros((block, wide), BF16)
        for copy in copies:
            copy.wait()

        def product(first, size):
            sums = jnp.dot(factors_ref[first:first + size, :], panels_ref[...], preferred_element_type=F32)
            return sums + got_buf[first:first + size, :].astype(F32)

        pre = product(count, tokens_ref.shape[0])
        if m:
            extra_ref[...] = gated(gate_buf[...], pre).T
            end = pltpu.make_async_copy(
                extra_ref.at[:width, :], last_ref.at[pl.ds(start, width), :], sems.at[0])
        else:
            extra_ref[...] = pre
            end = pltpu.make_async_copy(extra_ref, last_ref.at[:, pl.ds(start, tiled(width))], sems.at[0])
        end.start()
        for i in range(2):
            slab_ref[:, i * half:(i + 1) * half] = product(i * half, half).astype(BF16).T
        slab = pltpu.make_async_copy(
            slab_ref.at[:width, :], grown_ref.at[m, pl.ds(start, width), :], sems.at[1])
        slab.start()
        end.wait()
        slab.wait()


def finish(m, start, width, slots, mine, own, got, gate, grown, hidden, columns):
    rows, token_growth = mine
    count, depth = rows.shape
    extra = token_growth.shape[0]
    block, wide = own.shape
    args = [rows, token_growth, own, got, gate, grown] + ([hidden] if m else [])
    return pl.pallas_call(
        functools.partial(finish_kernel, m, start, width),
        out_shape=(
            jax.ShapeDtypeStruct((2, columns, count), BF16),
            jax.ShapeDtypeStruct((columns, extra), BF16) if m else jax.ShapeDtypeStruct((extra, tiled(columns)), F32),
        ),
        grid_spec=pltpu.PrefetchScalarGridSpec(
            num_scalar_prefetch=1,
            grid=(1,),
            in_specs=[ANY] * len(args),
            out_specs=(ANY, ANY),
            scratch_shapes=[
                pltpu.VMEM((count + extra, 2 * block), BF16),
                pltpu.VMEM((2 * block, wide), BF16),
                pltpu.VMEM((count + extra, wide), BF16),
                pltpu.VMEM((extra, wide), F32),
                pltpu.VMEM((wide, count), BF16),
                pltpu.VMEM((wide, extra), BF16) if m else pltpu.VMEM((extra, wide), F32),
                pltpu.SemaphoreType.DMA((5,)),
            ],
        ),
        input_output_aliases={6: 0, 7: 1} if m else {6: 0, 5: 1},
        compiler_params=pltpu.CompilerParams(vmem_limit_bytes=VMEM_LIMIT),
        cost_estimate=pl.CostEstimate(flops=0, bytes_accessed=0, transcendentals=0),
        name="finish",
    )(slots, *args)


def used_depth(depth):
    return tiled(3 * depth // 4)


def fetch_half(rows, parts):
    half, depth = rows.shape[0] // 2, rows.shape[1]
    core = lax.rem(lax.axis_index("tensor"), 2)
    first = jnp.where(lax.axis_index("dp") == 0, depth - used_depth(depth), 0)
    size = -(-half // parts // 16) * 16
    fetched = []
    for start in range(0, half, size):
        part = lax.dynamic_slice(rows, (core * half + start, first), (min(size, half - start), used_depth(depth)))
        fetched.append(lax.ppermute(after(part, *fetched[-1:]), "dp", TO_INNER))
    return fetched


def line_form(tokens, small_weights, ffn_growth, width_growth):
    columns = ffn_growth.shape[0]
    index = lax.axis_index("dp")
    is_inner = ((index == 1) | (index == 2)).astype(jnp.int32)
    core = lax.rem(lax.axis_index("tensor"), 2)
    slots = jnp.concatenate(
        [jnp.array(SLOTS, jnp.int32)[index], jnp.stack([is_inner, (index == 3).astype(jnp.int32), core])]
    )
    small = [lax.all_gather(small_weights[m], "tensor", axis=0, tiled=True) for m in range(2)]
    fetched = fetch_half(width_growth, 3)
    token_share = token_rows(tokens, width_growth, fetched[0])
    token_share = joined(token_share, swap(token_share, 1), 1)
    token_share = joined(token_share, swap(token_share, 2), 2)
    token_rest = swap(token_share, 4)

    work = [(m, start, width) for m in range(2) for start, width in pieces(columns, WIDTH)]
    own, outer, mate, far, out, received = ({} for _ in range(6))
    grown = gate = hidden = theirs = None

    def panel(chosen, *made):
        m = work[chosen[0]][0]
        source = after(small[m], *made) if made else small[m]
        for k, part in zip(chosen, panel_of(source, ffn_growth, [work[k][1:] for k in chosen])):
            own[k] = part

    def send(k, *made):
        sent = after(own[k], *made) if made else own[k]
        with jax.named_scope(f"outer{k}"):
            outer[k] = lax.ppermute(sent, "dp", TO_INNER)
        with jax.named_scope(f"mate{k}"):
            mate[k] = lax.ppermute(sent, "dp", SWAP_INNER)

    def forward(k, *made):
        outer[k] = after(outer[k], *made)
        with jax.named_scope(f"far{k}"):
            far[k] = lax.ppermute(outer[k], "dp", SWAP_INNER)

    def multiply(k, *made, sending=True, keeping=True):
        nonlocal grown, gate, hidden
        m, start, width = work[k]
        panels = [after(own[k], *made), outer[k], mate[k], far[k]]
        last = hidden if m else gate
        made = products(
            m, start, width, slots, mine, theirs, panels, gate, grown, last, columns, sending, keeping
        )
        if sending:
            out[k] = made[0]
            with jax.named_scope(f"sums{k}"):
                received[k] = lax.ppermute(out[k], "dp", TO_OUTER)
        if keeping:
            grown = made[-2]
            if m:
                hidden = made[-1]
            else:
                gate = made[-1]

    def conclude(k, *made):
        nonlocal grown, gate, hidden
        m, start, width = work[k]
        got = after(received[k], *made) if made else received[k]
        grown, last = finish(m, start, width, slots, mine, own[k], got, gate, grown, hidden, columns)
        if m:
            hidden = last
        else:
            gate = last

    panel([0], fetched[1], token_share)
    token_growth = joined(token_share, after(token_rest, own[0]), 4)
    token_half, = fetch_half(token_growth, 1)
    mine = (width_growth, token_growth)
    rows_half = jnp.concatenate(fetched[:2] + [after(fetched[2], own[0])], axis=0)
    send(0)
    panel([1, 2], own[0], token_growth, rows_half)
    forward(0, mate[0], own[1])
    token_half = after(token_half, own[1])
    theirs = (rows_half, swap(rows_half, 1), token_half, swap(token_half, 1))
    send(1, outer[0])
    forward(1, far[0])
    send(2, outer[1])
    multiply(0, outer[1])
    forward(2, out[0])
    panel([3, 4, 5], outer[2], mate[1])
    send(3)
    multiply(1, own[3], received[0], far[2])
    forward(3, out[1], mate[3])
    send(4, outer[3])
    multiply(2, outer[3])
    conclude(0)
    forward(4, out[2], far[3])
    send(5, outer[4])
    conclude(1)
    multiply(3, outer[4])
    forward(5, out[3], far[4])
    conclude(2)
    multiply(4, outer[5])
    conclude(3)
    multiply(5, out[4], keeping=False)
    multiply(5, out[5], sending=False)
    conclude(4)
    conclude(5)
    return jnp.swapaxes(grown, 1, 2), hidden.T


def solution(mesh):
    placed = (P("dp", "tensor"), P(None, ("dp", "tensor"), None), P("tensor", None), P("dp", None))
    return jax.shard_map(
        line_form if mesh.shape["dp"] == 4 else gathered_form,
        mesh=mesh,
        in_specs=placed,
        out_specs=(P(None, "dp", "tensor"), P("dp", "tensor")),
        check_vma=False,
    )
```

```python
import functools

import jax
import jax.numpy as jnp
from jax import lax
from jax.experimental import pallas as pl
from jax.experimental.pallas import tpu as pltpu
from jax.sharding import PartitionSpec as P

BF16, F32 = jnp.bfloat16, jnp.float32
WIDTH = 512
VMEM_LIMIT = 56 * 1024 * 1024
ANY = pl.BlockSpec(memory_space=pl.ANY)


def pieces(extent, width):
    starts = list(range(0, extent, width))
    return [(start, min(width, extent - start)) for start in starts]


def after(array, *made):
    return lax.optimization_barrier((array,) + made)[0]


def token_rows(tokens, width_growth, *fetched):
    nd = lax.axis_size("dp")
    by_rows = lax.all_to_all(tokens, "tensor", 0, 1, tiled=True)
    by_features = lax.all_to_all(by_rows, "dp", 1, 0, tiled=True)
    by_features = after(by_features, *fetched[:1])
    part = jnp.dot(by_features, width_growth, preferred_element_type=F32).astype(BF16)
    parts = lax.all_to_all(part, "dp", 0, 0, tiled=True)
    return jnp.sum(parts.reshape(nd, -1, parts.shape[1]).astype(F32), axis=0).astype(BF16)


def swap(rows, bit):
    return lax.ppermute(rows, "tensor", [(j, j ^ bit) for j in range(lax.axis_size("tensor"))])


def joined(rows, got, bit):
    low = (lax.axis_index("tensor") // bit) % 2 == 0
    return jnp.concatenate([jnp.where(low, rows, got), jnp.where(low, got, rows)], axis=0)


def gathered_form(tokens, small_weights, ffn_growth, width_growth):
    columns = ffn_growth.shape[0]
    small = [lax.all_gather(small_weights[m], "tensor", axis=0, tiled=True) for m in range(2)]
    token_growth = lax.all_gather(token_rows(tokens, width_growth), "tensor", axis=0, tiled=True)
    grown, pre = [], []
    for m in range(2):
        grown_parts, pre_parts = [], []
        for start, width in pieces(columns, WIDTH):
            panel = jnp.einsum(
                "sf,cf->sc", small[m], ffn_growth[start:start + width], preferred_element_type=F32
            ).astype(BF16)
            panels = lax.all_gather(panel, "dp", axis=0, tiled=True)
            grown_parts.append(jnp.dot(width_growth, panels, preferred_element_type=F32).astype(BF16))
            pre_parts.append(jnp.dot(token_growth, panels, preferred_element_type=F32))
        grown.append(jnp.concatenate(grown_parts, axis=1))
        pre.append(jnp.concatenate(pre_parts, axis=1))
    hidden = (jax.nn.silu(pre[0]) * pre[1]).astype(BF16)
    return (jnp.stack(grown), hidden)


SWAP_INNER = [(1, 2), (2, 1)]
TO_INNER = [(0, 1), (3, 2)]
TO_OUTER = [(1, 0), (2, 3)]
SLOTS = [[0, 1, 2, 3], [1, 0, 2, 3], [2, 3, 1, 0], [3, 0, 1, 2]]


def panel_kernel(steps, splits, small_ref, growth_ref, *refs):
    out_refs, acc_ref = refs[:-1], refs[-1]
    step = pl.program_id(0)
    part = lax.dot_general(
        small_ref[...], growth_ref[...], (((1,), (1,)), ((), ())), preferred_element_type=F32
    )

    @pl.when(step == 0)
    def _():
        acc_ref[...] = part

    @pl.when((step > 0) & (step < steps - 1))
    def _():
        acc_ref[...] += part

    @pl.when(step == steps - 1)
    def _():
        total = acc_ref[...] + part
        for (start, width), out_ref in zip(splits, out_refs):
            wide = out_ref.shape[1]
            piece = total[:, start - splits[0][0]:start - splits[0][0] + wide]
            if width < wide:
                column = lax.broadcasted_iota(jnp.int32, piece.shape, 1)
                piece = jnp.where(column < width, piece, 0.0)
            out_ref[...] = piece.astype(BF16)


def tiled(width):
    return -(-width // 128) * 128


def panel_of(small, growth, splits):
    rows, depth = small.shape
    first = splits[0][0]
    wide = tiled(splits[-1][0] + splits[-1][1] - first)
    steps = 7
    deep = depth // steps
    return pl.pallas_call(
        functools.partial(panel_kernel, steps, splits),
        out_shape=[jax.ShapeDtypeStruct((rows, tiled(width)), BF16) for _, width in splits],
        grid=(steps,),
        in_specs=[
            pl.BlockSpec((rows, deep), lambda k: (0, k)),
            pl.BlockSpec((pl.Element(wide, (0, max(0, first + wide - growth.shape[0]))), pl.Element(deep)), lambda k: (first, k * deep)),
        ],
        out_specs=[pl.BlockSpec((rows, tiled(width)), lambda k: (0, 0)) for _, width in splits],
        scratch_shapes=[pltpu.VMEM((rows, wide), F32)],
        compiler_params=pltpu.CompilerParams(vmem_limit_bytes=VMEM_LIMIT),
        cost_estimate=pl.CostEstimate(flops=3 * rows * depth * wide, bytes_accessed=0, transcendentals=0),
        name="panel",
    )(small, growth)


def gated(gate, up):
    return (gate / (1.0 + jnp.exp(-gate)) * up).astype(BF16)


def products_kernel(m, start, width, sending, keeping, slots_ref, *refs):
    refs = list(refs)
    theirs, their_tokens = (refs.pop(0), refs.pop(0)), (refs.pop(0), refs.pop(0))
    rows_ref, tokens_ref = refs.pop(0), refs.pop(0)
    sources = [refs.pop(0) for _ in range(4)]
    if keeping:
        if m:
            gate_ref = refs.pop(0)
        if m or start:
            refs.pop(0)
        if start:
            refs.pop(0)
    if sending:
        out_ref = refs.pop(0)
    if keeping:
        grown_ref, last_ref = refs.pop(0), refs.pop(0)
    panels_ref, factors_ref, stage_ref, slab_ref, extra_ref, gate_buf, sems, factor_sems, end_sems = refs
    block = sources[0].shape[0]
    count = rows_ref.shape[0]
    extra = tokens_ref.shape[0]
    half, few = count // 2, extra // 2
    depth, used = panels_ref.shape[0], their_tokens[0].shape[1]

    def placed(s):
        row = pl.multiple_of(slots_ref[s] * block, 16)
        return pltpu.make_async_copy(sources[s], panels_ref.at[pl.ds(row, block), :], sems.at[s])

    def from_either(pair, i, buffer, offset, sem):
        size = pair[0].shape[0]
        copies = [
            pltpu.make_async_copy(ref, factors_ref.at[buffer, pl.ds(offset, size), pl.ds(0, used)], sem) for ref in pair
        ]
        mine = slots_ref[6] == i

        @pl.when(mine)
        def _():
            copies[0].start()

        @pl.when(jnp.logical_not(mine))
        def _():
            copies[1].start()

        return copies[0]

    def plain(ref, first, size, buffer, offset, sem):
        copy = pltpu.make_async_copy(
            ref.at[pl.ds(first, size), :], factors_ref.at[buffer, pl.ds(offset, size), :], sem
        )
        copy.start()
        return copy

    work = ["sent", "sent", "tokens", "kept", "kept"][0 if sending else 2:5 if keeping else 3]
    place = {"sent": 0, "kept": 0}

    def fetch(i):
        buffer = i % 3
        sem = [factor_sems.at[buffer, j] for j in range(3)]
        if work[i] == "sent":
            place["sent"] += 1
            return [from_either(theirs, place["sent"] - 1, buffer, 0, sem[0])]
        if work[i] == "kept":
            place["kept"] += 1
            return [plain(rows_ref, (place["kept"] - 1) * half, half, buffer, 0, sem[0])]
        copies = []
        if sending:
            copies.append(from_either(their_tokens, 0, buffer, 0, sem[0]))
            copies.append(from_either(their_tokens, 1, buffer, few, sem[1]))
        if keeping:
            copies.append(plain(tokens_ref, 0, extra, buffer, extra, sem[2]))
        return copies

    def product(buffer, first, size):
        return jnp.dot(factors_ref[buffer, first:first + size, :], panels_ref[...], preferred_element_type=F32)

    def product_out(buffer, size):
        row = pl.multiple_of(jnp.where(slots_ref[0] == 1, depth - used, 0), 128)
        return jnp.dot(
            factors_ref[buffer, :size, :used], panels_ref[pl.ds(row, used), :], preferred_element_type=F32
        )

    @pl.when(slots_ref[4] == 1)
    def _():
        first = [placed(s) for s in range(4)]
        for copy in first:
            copy.start()
        coming = [fetch(0), fetch(1)]
        if m and keeping:
            gate_copy = pltpu.make_async_copy(
                gate_ref.at[:, pl.ds(start, tiled(width))], gate_buf, end_sems.at[4])
            gate_copy.start()
        for copy in first:
            copy.wait()
        ends = []

        def finished(source, target):
            copy = pltpu.make_async_copy(source, target, end_sems.at[len(ends)])
            copy.start()
            ends.append(copy)

        done = {"sent": 0, "kept": 0}
        for i, kind in enumerate(work):
            if i + 2 < len(work):
                coming.append(fetch(i + 2))
            for copy in coming[i]:
                copy.wait()
            if kind == "sent":
                stage_ref[done[kind] * half:(done[kind] + 1) * half, :] = product_out(i % 3, half).astype(BF16)
                done[kind] += 1
            elif kind == "kept":
                part = slice(done[kind] * half, (done[kind] + 1) * half)
                slab_ref[:, part] = product(i % 3, 0, half).astype(BF16).T
                done[kind] += 1
            else:
                if sending:
                    stage_ref[count:, :] = product_out(i % 3, extra).astype(BF16)
                    finished(stage_ref, out_ref)
                if keeping:
                    pre = product(i % 3, extra, extra)
                    if m:
                        gate_copy.wait()
                        extra_ref[...] = gated(gate_buf[...], pre).T
                        finished(extra_ref.at[:width, :], last_ref.at[pl.ds(start, width), :])
                    else:
                        extra_ref[...] = pre
                        finished(extra_ref, last_ref.at[:, pl.ds(start, tiled(width))])
        if keeping:
            finished(slab_ref.at[:width, :], grown_ref.at[m, pl.ds(start, width), :])
        for copy in ends:
            copy.wait()


def products(m, start, width, slots, mine, theirs, panels, gate, grown, last, columns, sending, keeping):
    rows, token_growth = mine
    count, depth = rows.shape
    extra = token_growth.shape[0]
    block, wide = panels[0].shape
    args = [*theirs, rows, token_growth, *panels]
    aliases = {}
    if keeping and m:
        args.append(gate)
    if keeping and grown is not None:
        aliases[len(args) + 1] = int(sending)
        args.append(grown)
    if keeping and last is not None:
        aliases[len(args) + 1] = int(sending) + 1
        args.append(last)
    out_shape = []
    if sending:
        out_shape.append(jax.ShapeDtypeStruct((count + extra, wide), BF16))
    if keeping:
        out_shape.append(jax.ShapeDtypeStruct((2, columns, count), BF16))
        out_shape.append(
            jax.ShapeDtypeStruct((columns, extra), BF16) if m else jax.ShapeDtypeStruct((extra, tiled(columns)), F32)
        )
    return pl.pallas_call(
        functools.partial(products_kernel, m, start, width, sending, keeping),
        out_shape=out_shape,
        grid_spec=pltpu.PrefetchScalarGridSpec(
            num_scalar_prefetch=1,
            grid=(1,),
            in_specs=[ANY] * len(args),
            out_specs=[ANY] * len(out_shape),
            scratch_shapes=[
                pltpu.VMEM((depth, wide), BF16),
                pltpu.VMEM((3, count // 2, depth), BF16),
                pltpu.VMEM((count + extra, wide), BF16),
                pltpu.VMEM((wide, count), BF16),
                pltpu.VMEM((wide, extra), BF16) if m else pltpu.VMEM((extra, wide), F32),
                pltpu.VMEM((extra, wide), F32),
                pltpu.SemaphoreType.DMA((4,)),
                pltpu.SemaphoreType.DMA((3, 3)),
                pltpu.SemaphoreType.DMA((5,)),
            ],
        ),
        input_output_aliases=aliases,
        compiler_params=pltpu.CompilerParams(vmem_limit_bytes=VMEM_LIMIT),
        cost_estimate=pl.CostEstimate(flops=3 * (sending + keeping) * (count + extra) * depth * wide, bytes_accessed=0, transcendentals=0),
        name="products",
    )(slots, *args)


def finish_kernel(m, start, width, slots_ref, rows_ref, tokens_ref, own_ref, got_ref, gate_ref, *refs):
    grown_ref, last_ref = refs[2 if m else 1:][:2]
    factors_ref, panels_ref, got_buf, gate_buf, slab_ref, extra_ref, sems = refs[2 if m else 1:][2:]
    block = own_ref.shape[0]
    count = rows_ref.shape[0]
    wide = panels_ref.shape[1]
    half = count // 2
    depth = factors_ref.shape[1]

    @pl.when(slots_ref[4] == 0)
    def _():
        side = pl.multiple_of(slots_ref[5] * depth, 128)
        place = pl.multiple_of(slots_ref[5] * block, 16)
        other = pl.multiple_of((1 - slots_ref[5]) * block, 16)
        copies = [
            pltpu.make_async_copy(own_ref, panels_ref.at[pl.ds(place, block), :], sems.at[0]),
            pltpu.make_async_copy(
                tokens_ref.at[:, pl.ds(side, depth)], factors_ref.at[pl.ds(count, tokens_ref.shape[0]), :], sems.at[1]),
            pltpu.make_async_copy(rows_ref.at[:, pl.ds(side, depth)], factors_ref.at[pl.ds(0, count), :], sems.at[2]),
            pltpu.make_async_copy(got_ref, got_buf, sems.at[3]),
        ]
        if m:
            copies.append(pltpu.make_async_copy(gate_ref.at[:, pl.ds(start, tiled(width))], gate_buf, sems.at[4]))
        for copy in copies:
            copy.start()
        panels_ref[pl.ds(other, block), :] = jnp.zeros((block, wide), BF16)
        for copy in copies:
            copy.wait()

        def product(first, size):
            sums = jnp.dot(factors_ref[first:first + size, :], panels_ref[...], preferred_element_type=F32)
            return sums + got_buf[first:first + size, :].astype(F32)

        pre = product(count, tokens_ref.shape[0])
        if m:
            extra_ref[...] = gated(gate_buf[...], pre).T
            end = pltpu.make_async_copy(
                extra_ref.at[:width, :], last_ref.at[pl.ds(start, width), :], sems.at[0])
        else:
            extra_ref[...] = pre
            end = pltpu.make_async_copy(extra_ref, last_ref.at[:, pl.ds(start, tiled(width))], sems.at[0])
        end.start()
        for i in range(2):
            slab_ref[:, i * half:(i + 1) * half] = product(i * half, half).astype(BF16).T
        slab = pltpu.make_async_copy(
            slab_ref.at[:width, :], grown_ref.at[m, pl.ds(start, width), :], sems.at[1])
        slab.start()
        end.wait()
        slab.wait()


def finish(m, start, width, slots, mine, own, got, gate, grown, hidden, columns):
    rows, token_growth = mine
    count, depth = rows.shape
    extra = token_growth.shape[0]
    block, wide = own.shape
    args = [rows, token_growth, own, got, gate, grown] + ([hidden] if m else [])
    return pl.pallas_call(
        functools.partial(finish_kernel, m, start, width),
        out_shape=(
            jax.ShapeDtypeStruct((2, columns, count), BF16),
            jax.ShapeDtypeStruct((columns, extra), BF16) if m else jax.ShapeDtypeStruct((extra, tiled(columns)), F32),
        ),
        grid_spec=pltpu.PrefetchScalarGridSpec(
            num_scalar_prefetch=1,
            grid=(1,),
            in_specs=[ANY] * len(args),
            out_specs=(ANY, ANY),
            scratch_shapes=[
                pltpu.VMEM((count + extra, 2 * block), BF16),
                pltpu.VMEM((2 * block, wide), BF16),
                pltpu.VMEM((count + extra, wide), BF16),
                pltpu.VMEM((extra, wide), F32),
                pltpu.VMEM((wide, count), BF16),
                pltpu.VMEM((wide, extra), BF16) if m else pltpu.VMEM((extra, wide), F32),
                pltpu.SemaphoreType.DMA((5,)),
            ],
        ),
        input_output_aliases={6: 0, 7: 1} if m else {6: 0, 5: 1},
        compiler_params=pltpu.CompilerParams(vmem_limit_bytes=VMEM_LIMIT),
        cost_estimate=pl.CostEstimate(flops=0, bytes_accessed=0, transcendentals=0),
        name="finish",
    )(slots, *args)


def used_depth(depth):
    return tiled(3 * depth // 4)


def fetch_half(rows, parts):
    half, depth = rows.shape[0] // 2, rows.shape[1]
    core = lax.rem(lax.axis_index("tensor"), 2)
    first = jnp.where(lax.axis_index("dp") == 0, depth - used_depth(depth), 0)
    size = -(-half // parts // 16) * 16
    fetched = []
    for start in range(0, half, size):
        part = lax.dynamic_slice(rows, (core * half + start, first), (min(size, half - start), used_depth(depth)))
        column = first + lax.broadcasted_iota(jnp.int32, part.shape, 1)
        part = jnp.where(column // (depth // 4) == lax.axis_index("dp"), jnp.zeros_like(part), part)
        fetched.append(lax.ppermute(after(part, *fetched[-1:]), "dp", TO_INNER))
    return fetched


def line_form(tokens, small_weights, ffn_growth, width_growth):
    columns = ffn_growth.shape[0]
    index = lax.axis_index("dp")
    is_inner = ((index == 1) | (index == 2)).astype(jnp.int32)
    core = lax.rem(lax.axis_index("tensor"), 2)
    slots = jnp.concatenate(
        [jnp.array(SLOTS, jnp.int32)[index], jnp.stack([is_inner, (index == 3).astype(jnp.int32), core])]
    )
    small = [lax.all_gather(small_weights[m], "tensor", axis=0, tiled=True) for m in range(2)]
    fetched = fetch_half(width_growth, 3)
    token_share = token_rows(tokens, width_growth, fetched[0])
    token_share = joined(token_share, swap(token_share, 1), 1)
    token_share = joined(token_share, swap(token_share, 2), 2)
    token_rest = swap(token_share, 4)

    work = [(m, start, width) for m in range(2) for start, width in pieces(columns, WIDTH)]
    own, outer, mate, far, out, received = ({} for _ in range(6))
    grown = gate = hidden = theirs = None

    def panel(chosen, *made):
        m = work[chosen[0]][0]
        source = after(small[m], *made) if made else small[m]
        for k, part in zip(chosen, panel_of(source, ffn_growth, [work[k][1:] for k in chosen])):
            own[k] = part

    def send(k, *made):
        sent = after(own[k], *made) if made else own[k]
        with jax.named_scope(f"outer{k}"):
            outer[k] = lax.ppermute(sent, "dp", TO_INNER)
        with jax.named_scope(f"mate{k}"):
            mate[k] = lax.ppermute(sent, "dp", SWAP_INNER)

    def forward(k, *made):
        outer[k] = after(outer[k], *made)
        with jax.named_scope(f"far{k}"):
            far[k] = lax.ppermute(outer[k], "dp", SWAP_INNER)

    def multiply(k, *made, sending=True, keeping=True):
        nonlocal grown, gate, hidden
        m, start, width = work[k]
        panels = [after(own[k], *made), outer[k], mate[k], far[k]]
        last = hidden if m else gate
        made = products(
            m, start, width, slots, mine, theirs, panels, gate, grown, last, columns, sending, keeping
        )
        if sending:
            out[k] = made[0]
            with jax.named_scope(f"sums{k}"):
                received[k] = lax.ppermute(out[k], "dp", TO_OUTER)
        if keeping:
            grown = made[-2]
            if m:
                hidden = made[-1]
            else:
                gate = made[-1]

    def conclude(k, *made):
        nonlocal grown, gate, hidden
        m, start, width = work[k]
        got = after(received[k], *made) if made else received[k]
        grown, last = finish(m, start, width, slots, mine, own[k], got, gate, grown, hidden, columns)
        if m:
            hidden = last
        else:
            gate = last

    panel([0], fetched[1], token_share)
    token_growth = joined(token_share, after(token_rest, own[0]), 4)
    token_half, = fetch_half(token_growth, 1)
    mine = (width_growth, token_growth)
    rows_half = jnp.concatenate(fetched[:2] + [after(fetched[2], own[0])], axis=0)
    send(0)
    panel([1, 2], own[0], token_growth, rows_half)
    forward(0, mate[0], own[1])
    token_half = after(token_half, own[1])
    theirs = (rows_half, swap(rows_half, 1), token_half, swap(token_half, 1))
    send(1, outer[0])
    multiply(0, far[0])
    forward(1, out[0])
    send(2, outer[1])
    panel([3], outer[1], out[0], mate[1])
    send(3)
    forward(2, own[3])
    multiply(1, outer[2])
    forward(3, out[1], mate[2])
    panel([4, 5], outer[3], received[0])
    send(4)
    conclude(0)
    multiply(2, own[4], mate[3])
    forward(4, out[2], far[3])
    send(5, outer[4])
    conclude(1)
    multiply(3, outer[4])
    forward(5, out[3], mate[4])
    conclude(2)
    multiply(4, outer[5])
    conclude(3)
    multiply(5, out[4], keeping=False)
    multiply(5, out[5], sending=False)
    conclude(4)
    conclude(5)
    return jnp.swapaxes(grown, 1, 2), hidden.T


def solution(mesh):
    placed = (P("dp", "tensor"), P(None, ("dp", "tensor"), None), P("tensor", None), P("dp", None))
    return jax.shard_map(
        line_form if mesh.shape["dp"] == 4 else gathered_form,
        mesh=mesh,
        in_specs=placed,
        out_specs=(P(None, "dp", "tensor"), P("dp", "tensor")),
        check_vma=False,
    )
```

```python
import functools

import jax
import jax.numpy as jnp
from jax import lax
from jax.experimental import pallas as pl
from jax.experimental.pallas import tpu as pltpu
from jax.sharding import PartitionSpec as P

BF16, F32 = jnp.bfloat16, jnp.float32
WIDTH = 512
VMEM_LIMIT = 56 * 1024 * 1024
ANY = pl.BlockSpec(memory_space=pl.ANY)


def pieces(extent, width):
    starts = list(range(0, extent, width))
    return [(start, min(width, extent - start)) for start in starts]


def after(array, *made):
    return lax.optimization_barrier((array,) + made)[0]


def token_rows(tokens, width_growth, *fetched):
    nd = lax.axis_size("dp")
    by_rows = lax.all_to_all(tokens, "tensor", 0, 1, tiled=True)
    by_features = lax.all_to_all(by_rows, "dp", 1, 0, tiled=True)
    by_features = after(by_features, *fetched[:1])
    part = jnp.dot(by_features, width_growth, preferred_element_type=F32).astype(BF16)
    parts = lax.all_to_all(part, "dp", 0, 0, tiled=True)
    return jnp.sum(parts.reshape(nd, -1, parts.shape[1]).astype(F32), axis=0).astype(BF16)


def swap(rows, bit):
    return lax.ppermute(rows, "tensor", [(j, j ^ bit) for j in range(lax.axis_size("tensor"))])


def joined(rows, got, bit):
    low = (lax.axis_index("tensor") // bit) % 2 == 0
    return jnp.concatenate([jnp.where(low, rows, got), jnp.where(low, got, rows)], axis=0)


def gathered_form(tokens, small_weights, ffn_growth, width_growth):
    columns = ffn_growth.shape[0]
    small = [lax.all_gather(small_weights[m], "tensor", axis=0, tiled=True) for m in range(2)]
    token_growth = lax.all_gather(token_rows(tokens, width_growth), "tensor", axis=0, tiled=True)
    grown, pre = [], []
    for m in range(2):
        grown_parts, pre_parts = [], []
        for start, width in pieces(columns, WIDTH):
            panel = jnp.einsum(
                "sf,cf->sc", small[m], ffn_growth[start:start + width], preferred_element_type=F32
            ).astype(BF16)
            panels = lax.all_gather(panel, "dp", axis=0, tiled=True)
            grown_parts.append(jnp.dot(width_growth, panels, preferred_element_type=F32).astype(BF16))
            pre_parts.append(jnp.dot(token_growth, panels, preferred_element_type=F32))
        grown.append(jnp.concatenate(grown_parts, axis=1))
        pre.append(jnp.concatenate(pre_parts, axis=1))
    hidden = (jax.nn.silu(pre[0]) * pre[1]).astype(BF16)
    return (jnp.stack(grown), hidden)


SWAP_INNER = [(1, 2), (2, 1)]
TO_INNER = [(0, 1), (3, 2)]
TO_OUTER = [(1, 0), (2, 3)]
SLOTS = [[0, 1, 2, 3], [1, 0, 2, 3], [2, 3, 1, 0], [3, 0, 1, 2]]


def panel_kernel(steps, splits, small_ref, growth_ref, *refs):
    out_refs, acc_ref = refs[:-1], refs[-1]
    step = pl.program_id(0)
    part = lax.dot_general(
        small_ref[...], growth_ref[...], (((1,), (1,)), ((), ())), preferred_element_type=F32
    )

    @pl.when(step == 0)
    def _():
        acc_ref[...] = part

    @pl.when((step > 0) & (step < steps - 1))
    def _():
        acc_ref[...] += part

    @pl.when(step == steps - 1)
    def _():
        total = acc_ref[...] + part
        for (start, width), out_ref in zip(splits, out_refs):
            wide = out_ref.shape[1]
            piece = total[:, start - splits[0][0]:start - splits[0][0] + wide]
            if width < wide:
                column = lax.broadcasted_iota(jnp.int32, piece.shape, 1)
                piece = jnp.where(column < width, piece, 0.0)
            out_ref[...] = piece.astype(BF16)


def tiled(width):
    return -(-width // 128) * 128


def panel_of(small, growth, splits):
    rows, depth = small.shape
    first = splits[0][0]
    wide = tiled(splits[-1][0] + splits[-1][1] - first)
    steps = 7
    deep = depth // steps
    return pl.pallas_call(
        functools.partial(panel_kernel, steps, splits),
        out_shape=[jax.ShapeDtypeStruct((rows, tiled(width)), BF16) for _, width in splits],
        grid=(steps,),
        in_specs=[
            pl.BlockSpec((rows, deep), lambda k: (0, k)),
            pl.BlockSpec((pl.Element(wide, (0, max(0, first + wide - growth.shape[0]))), pl.Element(deep)), lambda k: (first, k * deep)),
        ],
        out_specs=[pl.BlockSpec((rows, tiled(width)), lambda k: (0, 0)) for _, width in splits],
        scratch_shapes=[pltpu.VMEM((rows, wide), F32)],
        compiler_params=pltpu.CompilerParams(vmem_limit_bytes=VMEM_LIMIT),
        cost_estimate=pl.CostEstimate(flops=3 * rows * depth * wide, bytes_accessed=0, transcendentals=0),
        name="panel",
    )(small, growth)


def gated(gate, up):
    return (gate / (1.0 + jnp.exp(-gate)) * up).astype(BF16)


def products_kernel(m, start, width, sending, keeping, slots_ref, *refs):
    refs = list(refs)
    theirs, their_tokens = (refs.pop(0), refs.pop(0)), (refs.pop(0), refs.pop(0))
    rows_ref, tokens_ref = refs.pop(0), refs.pop(0)
    sources = [refs.pop(0) for _ in range(4)]
    if keeping:
        if m:
            gate_ref = refs.pop(0)
        if m or start:
            refs.pop(0)
        if start:
            refs.pop(0)
    if sending:
        out_ref = refs.pop(0)
    if keeping:
        grown_ref, last_ref = refs.pop(0), refs.pop(0)
    panels_ref, factors_ref, stage_ref, slab_ref, extra_ref, gate_buf, sems, factor_sems, end_sems = refs
    block = sources[0].shape[0]
    count = rows_ref.shape[0]
    extra = tokens_ref.shape[0]
    half, few = count // 2, extra // 2
    depth, used = panels_ref.shape[0], their_tokens[0].shape[1]

    def placed(s):
        row = pl.multiple_of(slots_ref[s] * block, 16)
        return pltpu.make_async_copy(sources[s], panels_ref.at[pl.ds(row, block), :], sems.at[s])

    def from_either(pair, i, buffer, offset, sem):
        size = pair[0].shape[0]
        copies = [
            pltpu.make_async_copy(ref, factors_ref.at[buffer, pl.ds(offset, size), pl.ds(0, used)], sem) for ref in pair
        ]
        mine = slots_ref[6] == i

        @pl.when(mine)
        def _():
            copies[0].start()

        @pl.when(jnp.logical_not(mine))
        def _():
            copies[1].start()

        return copies[0]

    def plain(ref, first, size, buffer, offset, sem):
        copy = pltpu.make_async_copy(
            ref.at[pl.ds(first, size), :], factors_ref.at[buffer, pl.ds(offset, size), :], sem
        )
        copy.start()
        return copy

    work = ["sent", "sent", "tokens", "kept", "kept"][0 if sending else 2:5 if keeping else 3]
    place = {"sent": 0, "kept": 0}

    def fetch(i):
        buffer = i % 3
        sem = [factor_sems.at[buffer, j] for j in range(3)]
        if work[i] == "sent":
            place["sent"] += 1
            return [from_either(theirs, place["sent"] - 1, buffer, 0, sem[0])]
        if work[i] == "kept":
            place["kept"] += 1
            return [plain(rows_ref, (place["kept"] - 1) * half, half, buffer, 0, sem[0])]
        copies = []
        if sending:
            copies.append(from_either(their_tokens, 0, buffer, 0, sem[0]))
            copies.append(from_either(their_tokens, 1, buffer, few, sem[1]))
        if keeping:
            copies.append(plain(tokens_ref, 0, extra, buffer, extra, sem[2]))
        return copies

    def product(buffer, first, size):
        return jnp.dot(factors_ref[buffer, first:first + size, :], panels_ref[...], preferred_element_type=F32)

    def product_out(buffer, size):
        row = pl.multiple_of(jnp.where(slots_ref[0] == 1, depth - used, 0), 128)
        return jnp.dot(
            factors_ref[buffer, :size, :used], panels_ref[pl.ds(row, used), :], preferred_element_type=F32
        )

    @pl.when(slots_ref[4] == 1)
    def _():
        first = [placed(s) for s in range(4)]
        for copy in first:
            copy.start()
        coming = [fetch(0), fetch(1)]
        if m and keeping:
            gate_copy = pltpu.make_async_copy(
                gate_ref.at[:, pl.ds(start, tiled(width))], gate_buf, end_sems.at[4])
            gate_copy.start()
        for copy in first:
            copy.wait()
        ends = []

        def finished(source, target):
            copy = pltpu.make_async_copy(source, target, end_sems.at[len(ends)])
            copy.start()
            ends.append(copy)

        done = {"sent": 0, "kept": 0}
        for i, kind in enumerate(work):
            if i + 2 < len(work):
                coming.append(fetch(i + 2))
            for copy in coming[i]:
                copy.wait()
            if kind == "sent":
                stage_ref[done[kind] * half:(done[kind] + 1) * half, :] = product_out(i % 3, half).astype(BF16)
                done[kind] += 1
            elif kind == "kept":
                part = slice(done[kind] * half, (done[kind] + 1) * half)
                slab_ref[:, part] = product(i % 3, 0, half).astype(BF16).T
                done[kind] += 1
            else:
                if sending:
                    stage_ref[count:, :] = product_out(i % 3, extra).astype(BF16)
                    finished(stage_ref, out_ref)
                if keeping:
                    pre = product(i % 3, extra, extra)
                    if m:
                        gate_copy.wait()
                        extra_ref[...] = gated(gate_buf[...], pre).T
                        finished(extra_ref.at[:width, :], last_ref.at[pl.ds(start, width), :])
                    else:
                        extra_ref[...] = pre
                        finished(extra_ref, last_ref.at[:, pl.ds(start, tiled(width))])
        if keeping:
            finished(slab_ref.at[:width, :], grown_ref.at[m, pl.ds(start, width), :])
        for copy in ends:
            copy.wait()


def products(m, start, width, slots, mine, theirs, panels, gate, grown, last, columns, sending, keeping):
    rows, token_growth = mine
    count, depth = rows.shape
    extra = token_growth.shape[0]
    block, wide = panels[0].shape
    args = [*theirs, rows, token_growth, *panels]
    aliases = {}
    if keeping and m:
        args.append(gate)
    if keeping and grown is not None:
        aliases[len(args) + 1] = int(sending)
        args.append(grown)
    if keeping and last is not None:
        aliases[len(args) + 1] = int(sending) + 1
        args.append(last)
    out_shape = []
    if sending:
        out_shape.append(jax.ShapeDtypeStruct((count + extra, wide), BF16))
    if keeping:
        out_shape.append(jax.ShapeDtypeStruct((2, columns, count), BF16))
        out_shape.append(
            jax.ShapeDtypeStruct((columns, extra), BF16) if m else jax.ShapeDtypeStruct((extra, tiled(columns)), F32)
        )
    return pl.pallas_call(
        functools.partial(products_kernel, m, start, width, sending, keeping),
        out_shape=out_shape,
        grid_spec=pltpu.PrefetchScalarGridSpec(
            num_scalar_prefetch=1,
            grid=(1,),
            in_specs=[ANY] * len(args),
            out_specs=[ANY] * len(out_shape),
            scratch_shapes=[
                pltpu.VMEM((depth, wide), BF16),
                pltpu.VMEM((3, count // 2, depth), BF16),
                pltpu.VMEM((count + extra, wide), BF16),
                pltpu.VMEM((wide, count), BF16),
                pltpu.VMEM((wide, extra), BF16) if m else pltpu.VMEM((extra, wide), F32),
                pltpu.VMEM((extra, wide), F32),
                pltpu.SemaphoreType.DMA((4,)),
                pltpu.SemaphoreType.DMA((3, 3)),
                pltpu.SemaphoreType.DMA((5,)),
            ],
        ),
        input_output_aliases=aliases,
        compiler_params=pltpu.CompilerParams(vmem_limit_bytes=VMEM_LIMIT),
        cost_estimate=pl.CostEstimate(flops=3 * (sending + keeping) * (count + extra) * depth * wide, bytes_accessed=0, transcendentals=0),
        name="products",
    )(slots, *args)


def own_kernel(slots_ref, rows_ref, tokens_ref, own_ref, sums_ref, factors_ref, panels_ref, sums_buf, sems):
    block = own_ref.shape[0]

    @pl.when(slots_ref[4] == 0)
    def _():
        copies = own_copies(slots_ref, rows_ref, tokens_ref, own_ref, factors_ref, panels_ref, sems)
        for copy in copies:
            copy.start()
        other = pl.multiple_of((1 - slots_ref[5]) * block, 16)
        panels_ref[pl.ds(other, block), :] = jnp.zeros((block, panels_ref.shape[1]), BF16)
        for copy in copies:
            copy.wait()
        sums_buf[...] = jnp.dot(factors_ref[...], panels_ref[...], preferred_element_type=F32)
        end = pltpu.make_async_copy(sums_buf, sums_ref, sems.at[0])
        end.start()
        end.wait()


def own_copies(slots_ref, rows_ref, tokens_ref, own_ref, factors_ref, panels_ref, sems):
    block, count, depth = own_ref.shape[0], rows_ref.shape[0], factors_ref.shape[1]
    side = pl.multiple_of(slots_ref[5] * depth, 128)
    place = pl.multiple_of(slots_ref[5] * block, 16)
    return [
        pltpu.make_async_copy(own_ref, panels_ref.at[pl.ds(place, block), :], sems.at[0]),
        pltpu.make_async_copy(
            tokens_ref.at[:, pl.ds(side, depth)], factors_ref.at[pl.ds(count, tokens_ref.shape[0]), :], sems.at[1]),
        pltpu.make_async_copy(rows_ref.at[:, pl.ds(side, depth)], factors_ref.at[pl.ds(0, count), :], sems.at[2]),
    ]


def own_product(slots, mine, own):
    rows, token_growth = mine
    total, (block, wide) = rows.shape[0] + token_growth.shape[0], own.shape
    return pl.pallas_call(
        own_kernel,
        out_shape=jax.ShapeDtypeStruct((total, wide), F32),
        grid_spec=pltpu.PrefetchScalarGridSpec(
            num_scalar_prefetch=1,
            grid=(1,),
            in_specs=[ANY] * 3,
            out_specs=ANY,
            scratch_shapes=[
                pltpu.VMEM((total, 2 * block), BF16),
                pltpu.VMEM((2 * block, wide), BF16),
                pltpu.VMEM((total, wide), F32),
                pltpu.SemaphoreType.DMA((3,)),
            ],
        ),
        compiler_params=pltpu.CompilerParams(vmem_limit_bytes=VMEM_LIMIT),
        cost_estimate=pl.CostEstimate(flops=0, bytes_accessed=0, transcendentals=0),
        name="own_product",
    )(slots, rows, token_growth, own)


def finish_kernel(m, start, width, made, slots_ref, *refs):
    refs = list(refs)
    sources = [refs.pop(0) for _ in range(1 if made else 3)]
    got_ref, gate_ref = refs.pop(0), refs.pop(0)
    del refs[:2 if m else 1]
    grown_ref, last_ref = refs.pop(0), refs.pop(0)
    bufs = [refs.pop(0) for _ in range(1 if made else 2)]
    got_buf, gate_buf, slab_ref, extra_ref, sems = refs
    wide = got_ref.shape[1]
    count, extra = slab_ref.shape[1], gate_buf.shape[0]
    half = count // 2

    @pl.when(slots_ref[4] == 0)
    def _():
        if made:
            copies = [pltpu.make_async_copy(sources[0], bufs[0], sems.at[0])]
        else:
            copies = own_copies(slots_ref, *sources, *bufs, sems)
        copies.append(pltpu.make_async_copy(got_ref, got_buf, sems.at[3]))
        if m:
            copies.append(pltpu.make_async_copy(gate_ref.at[:, pl.ds(start, tiled(width))], gate_buf, sems.at[4]))
        for copy in copies:
            copy.start()
        if not made:
            block = sources[2].shape[0]
            other = pl.multiple_of((1 - slots_ref[5]) * block, 16)
            bufs[1][pl.ds(other, block), :] = jnp.zeros((block, wide), BF16)
        for copy in copies:
            copy.wait()

        def product(first, size):
            if made:
                sums = bufs[0][first:first + size, :]
            else:
                sums = jnp.dot(bufs[0][first:first + size, :], bufs[1][...], preferred_element_type=F32)
            return sums + got_buf[first:first + size, :].astype(F32)

        pre = product(count, extra)
        if m:
            extra_ref[...] = gated(gate_buf[...], pre).T
            end = pltpu.make_async_copy(
                extra_ref.at[:width, :], last_ref.at[pl.ds(start, width), :], sems.at[0])
        else:
            extra_ref[...] = pre
            end = pltpu.make_async_copy(extra_ref, last_ref.at[:, pl.ds(start, tiled(width))], sems.at[0])
        end.start()
        for i in range(2):
            slab_ref[:, i * half:(i + 1) * half] = product(i * half, half).astype(BF16).T
        slab = pltpu.make_async_copy(
            slab_ref.at[:width, :], grown_ref.at[m, pl.ds(start, width), :], sems.at[1])
        slab.start()
        end.wait()
        slab.wait()


def finish(m, start, width, slots, mine, own, got, gate, grown, hidden, columns, made=None):
    rows, token_growth = mine
    count, depth = rows.shape
    extra = token_growth.shape[0]
    block, wide = own.shape
    args = [rows, token_growth, own] if made is None else [made]
    args += [got, gate, grown] + ([hidden] if m else [])
    last = len(args)
    if made is None:
        scratch = [pltpu.VMEM((count + extra, 2 * block), BF16), pltpu.VMEM((2 * block, wide), BF16)]
    else:
        scratch = [pltpu.VMEM((count + extra, wide), F32)]
    return pl.pallas_call(
        functools.partial(finish_kernel, m, start, width, made is not None),
        out_shape=(
            jax.ShapeDtypeStruct((2, columns, count), BF16),
            jax.ShapeDtypeStruct((columns, extra), BF16) if m else jax.ShapeDtypeStruct((extra, tiled(columns)), F32),
        ),
        grid_spec=pltpu.PrefetchScalarGridSpec(
            num_scalar_prefetch=1,
            grid=(1,),
            in_specs=[ANY] * len(args),
            out_specs=(ANY, ANY),
            scratch_shapes=scratch + [
                pltpu.VMEM((count + extra, wide), BF16),
                pltpu.VMEM((extra, wide), F32),
                pltpu.VMEM((wide, count), BF16),
                pltpu.VMEM((wide, extra), BF16) if m else pltpu.VMEM((extra, wide), F32),
                pltpu.SemaphoreType.DMA((5,)),
            ],
        ),
        input_output_aliases={last - 1: 0, last: 1} if m else {last: 0, last - 1: 1},
        compiler_params=pltpu.CompilerParams(vmem_limit_bytes=VMEM_LIMIT),
        cost_estimate=pl.CostEstimate(flops=0, bytes_accessed=0, transcendentals=0),
        name="finish",
    )(slots, *args)


def used_depth(depth):
    return tiled(3 * depth // 4)


def fetch_half(rows, parts):
    half, depth = rows.shape[0] // 2, rows.shape[1]
    core = lax.rem(lax.axis_index("tensor"), 2)
    first = jnp.where(lax.axis_index("dp") == 0, depth - used_depth(depth), 0)
    size = -(-half // parts // 16) * 16
    fetched = []
    for start in range(0, half, size):
        part = lax.dynamic_slice(rows, (core * half + start, first), (min(size, half - start), used_depth(depth)))
        column = first + lax.broadcasted_iota(jnp.int32, part.shape, 1)
        part = jnp.where(column // (depth // 4) == lax.axis_index("dp"), jnp.zeros_like(part), part)
        fetched.append(lax.ppermute(after(part, *fetched[-1:]), "dp", TO_INNER))
    return fetched


def line_form(tokens, small_weights, ffn_growth, width_growth):
    columns = ffn_growth.shape[0]
    index = lax.axis_index("dp")
    is_inner = ((index == 1) | (index == 2)).astype(jnp.int32)
    core = lax.rem(lax.axis_index("tensor"), 2)
    slots = jnp.concatenate(
        [jnp.array(SLOTS, jnp.int32)[index], jnp.stack([is_inner, (index == 3).astype(jnp.int32), core])]
    )
    small = [lax.all_gather(small_weights[m], "tensor", axis=0, tiled=True) for m in range(2)]
    fetched = fetch_half(width_growth, 3)
    token_share = token_rows(tokens, width_growth, fetched[0])
    token_share = joined(token_share, swap(token_share, 1), 1)
    token_share = joined(token_share, swap(token_share, 2), 2)
    token_rest = swap(token_share, 4)

    work = [(m, start, width) for m in range(2) for start, width in pieces(columns, WIDTH)]
    own, outer, mate, far, out, received = ({} for _ in range(6))
    grown = gate = hidden = theirs = None

    def panel(chosen, *made):
        m = work[chosen[0]][0]
        source = after(small[m], *made) if made else small[m]
        for k, part in zip(chosen, panel_of(source, ffn_growth, [work[k][1:] for k in chosen])):
            own[k] = part

    def send(k, *made):
        sent = after(own[k], *made) if made else own[k]
        with jax.named_scope(f"outer{k}"):
            outer[k] = lax.ppermute(sent, "dp", TO_INNER)
        with jax.named_scope(f"mate{k}"):
            mate[k] = lax.ppermute(sent, "dp", SWAP_INNER)

    def forward(k, *made):
        outer[k] = after(outer[k], *made)
        with jax.named_scope(f"far{k}"):
            far[k] = lax.ppermute(outer[k], "dp", SWAP_INNER)

    def multiply(k, *made, sending=True, keeping=True):
        nonlocal grown, gate, hidden
        m, start, width = work[k]
        panels = [after(own[k], *made), outer[k], mate[k], far[k]]
        last = hidden if m else gate
        made = products(
            m, start, width, slots, mine, theirs, panels, gate, grown, last, columns, sending, keeping
        )
        if sending:
            out[k] = made[0]
            with jax.named_scope(f"sums{k}"):
                received[k] = lax.ppermute(out[k], "dp", TO_OUTER)
        if keeping:
            grown = made[-2]
            if m:
                hidden = made[-1]
            else:
                gate = made[-1]

    def conclude(k, made=None):
        nonlocal grown, gate, hidden
        m, start, width = work[k]
        grown, last = finish(m, start, width, slots, mine, own[k], received[k], gate, grown, hidden, columns, made)
        if m:
            hidden = last
        else:
            gate = last

    panel([0], fetched[1], token_share)
    token_growth = joined(token_share, after(token_rest, own[0]), 4)
    token_half, = fetch_half(token_growth, 1)
    mine = (width_growth, token_growth)
    rows_half = jnp.concatenate(fetched[:2] + [after(fetched[2], own[0])], axis=0)
    send(0)
    panel([1], own[0], token_growth, rows_half)
    forward(0, mate[0], own[1])
    token_half = after(token_half, own[1])
    theirs = (rows_half, swap(rows_half, 1), token_half, swap(token_half, 1))
    send(1, outer[0])
    panel([2], outer[0])
    multiply(0, far[0], own[2])
    forward(1, out[0])
    send(2, outer[1])
    panel([3], outer[1], out[0], mate[1])
    send(3)
    forward(2, own[3])
    multiply(1, outer[2])
    forward(3, out[1], mate[2])
    panel([4, 5], outer[3], received[0])
    send(4)
    conclude(0)
    multiply(2, own[4], mate[3])
    forward(4, out[2], far[3])
    send(5, outer[4])
    conclude(1)
    multiply(3, outer[4])
    forward(5, out[3], mate[4])
    conclude(2)
    multiply(4, outer[5])
    conclude(3)
    multiply(5, out[4], keeping=False)
    multiply(5, out[5], sending=False)
    last_product = own_product(slots, mine, after(own[5], out[5]))
    conclude(4)
    conclude(5, last_product)
    return jnp.swapaxes(grown, 1, 2), hidden.T


def solution(mesh):
    placed = (P("dp", "tensor"), P(None, ("dp", "tensor"), None), P("tensor", None), P("dp", None))
    return jax.shard_map(
        line_form if mesh.shape["dp"] == 4 else gathered_form,
        mesh=mesh,
        in_specs=placed,
        out_specs=(P(None, "dp", "tensor"), P("dp", "tensor")),
        check_vma=False,
    )
```

```python
import functools

import jax
import jax.numpy as jnp
from jax import lax
from jax.experimental import pallas as pl
from jax.experimental.pallas import tpu as pltpu
from jax.sharding import PartitionSpec as P

BF16, F32 = jnp.bfloat16, jnp.float32
WIDTH = 512
VMEM_LIMIT = 56 * 1024 * 1024
ANY = pl.BlockSpec(memory_space=pl.ANY)


def pieces(extent, width):
    starts = list(range(0, extent, width))
    return [(start, min(width, extent - start)) for start in starts]


def after(array, *made):
    return lax.optimization_barrier((array,) + made)[0]


def token_rows(tokens, width_growth, *fetched):
    nd = lax.axis_size("dp")
    by_rows = lax.all_to_all(tokens, "tensor", 0, 1, tiled=True)
    by_features = lax.all_to_all(by_rows, "dp", 1, 0, tiled=True)
    by_features = after(by_features, *fetched[:1])
    part = jnp.dot(by_features, width_growth, preferred_element_type=F32).astype(BF16)
    parts = lax.all_to_all(part, "dp", 0, 0, tiled=True)
    return jnp.sum(parts.reshape(nd, -1, parts.shape[1]).astype(F32), axis=0).astype(BF16)


def swap(rows, bit):
    return lax.ppermute(rows, "tensor", [(j, j ^ bit) for j in range(lax.axis_size("tensor"))])


def joined(rows, got, bit):
    low = (lax.axis_index("tensor") // bit) % 2 == 0
    return jnp.concatenate([jnp.where(low, rows, got), jnp.where(low, got, rows)], axis=0)


def gathered_form(tokens, small_weights, ffn_growth, width_growth):
    columns = ffn_growth.shape[0]
    small = [lax.all_gather(small_weights[m], "tensor", axis=0, tiled=True) for m in range(2)]
    token_growth = lax.all_gather(token_rows(tokens, width_growth), "tensor", axis=0, tiled=True)
    grown, pre = [], []
    for m in range(2):
        grown_parts, pre_parts = [], []
        for start, width in pieces(columns, WIDTH):
            panel = jnp.einsum(
                "sf,cf->sc", small[m], ffn_growth[start:start + width], preferred_element_type=F32
            ).astype(BF16)
            panels = lax.all_gather(panel, "dp", axis=0, tiled=True)
            grown_parts.append(jnp.dot(width_growth, panels, preferred_element_type=F32).astype(BF16))
            pre_parts.append(jnp.dot(token_growth, panels, preferred_element_type=F32))
        grown.append(jnp.concatenate(grown_parts, axis=1))
        pre.append(jnp.concatenate(pre_parts, axis=1))
    hidden = (jax.nn.silu(pre[0]) * pre[1]).astype(BF16)
    return (jnp.stack(grown), hidden)


SWAP_INNER = [(1, 2), (2, 1)]
TO_INNER = [(0, 1), (3, 2)]
TO_OUTER = [(1, 0), (2, 3)]
SLOTS = [[0, 1, 2, 3], [1, 0, 2, 3], [2, 3, 1, 0], [3, 0, 1, 2]]


def panel_kernel(steps, splits, small_ref, growth_ref, *refs):
    out_refs, acc_ref = refs[:-1], refs[-1]
    step = pl.program_id(0)
    part = lax.dot_general(
        small_ref[...], growth_ref[...], (((1,), (1,)), ((), ())), preferred_element_type=F32
    )

    @pl.when(step == 0)
    def _():
        acc_ref[...] = part

    @pl.when((step > 0) & (step < steps - 1))
    def _():
        acc_ref[...] += part

    @pl.when(step == steps - 1)
    def _():
        total = acc_ref[...] + part
        for (start, width), out_ref in zip(splits, out_refs):
            wide = out_ref.shape[1]
            piece = total[:, start - splits[0][0]:start - splits[0][0] + wide]
            if width < wide:
                column = lax.broadcasted_iota(jnp.int32, piece.shape, 1)
                piece = jnp.where(column < width, piece, 0.0)
            out_ref[...] = piece.astype(BF16)


def tiled(width):
    return -(-width // 128) * 128


def panel_of(small, growth, splits, weight):
    rows, depth = small.shape
    first = splits[0][0]
    wide = tiled(splits[-1][0] + splits[-1][1] - first)
    steps = 7
    deep = depth // steps
    return pl.pallas_call(
        functools.partial(panel_kernel, steps, splits),
        out_shape=[jax.ShapeDtypeStruct((rows, tiled(width)), BF16) for _, width in splits],
        grid=(steps,),
        in_specs=[
            pl.BlockSpec((rows, deep), lambda k: (0, k)),
            pl.BlockSpec((pl.Element(wide, (0, max(0, first + wide - growth.shape[0]))), pl.Element(deep)), lambda k: (first, k * deep)),
        ],
        out_specs=[pl.BlockSpec((rows, tiled(width)), lambda k: (0, 0)) for _, width in splits],
        scratch_shapes=[pltpu.VMEM((rows, wide), F32)],
        compiler_params=pltpu.CompilerParams(vmem_limit_bytes=VMEM_LIMIT),
        cost_estimate=pl.CostEstimate(flops=weight * rows * depth * wide, bytes_accessed=0, transcendentals=0),
        name="panel",
    )(small, growth)


def gated(gate, up):
    return (gate / (1.0 + jnp.exp(-gate)) * up).astype(BF16)


def products_kernel(m, start, width, sending, keeping, slots_ref, *refs):
    refs = list(refs)
    theirs, their_tokens = (refs.pop(0), refs.pop(0)), (refs.pop(0), refs.pop(0))
    rows_ref, tokens_ref = refs.pop(0), refs.pop(0)
    sources = [refs.pop(0) for _ in range(4)]
    if keeping:
        if m:
            gate_ref = refs.pop(0)
        if m or start:
            refs.pop(0)
        if start:
            refs.pop(0)
    if sending:
        out_ref = refs.pop(0)
    if keeping:
        grown_ref, last_ref = refs.pop(0), refs.pop(0)
    panels_ref, factors_ref, stage_ref, slab_ref, extra_ref, gate_buf, sems, factor_sems, end_sems = refs
    block = sources[0].shape[0]
    count = rows_ref.shape[0]
    extra = tokens_ref.shape[0]
    half, few = count // 2, extra // 2
    depth, used = panels_ref.shape[0], their_tokens[0].shape[1]

    def placed(s):
        row = pl.multiple_of(slots_ref[s] * block, 16)
        return pltpu.make_async_copy(sources[s], panels_ref.at[pl.ds(row, block), :], sems.at[s])

    def from_either(pair, i, buffer, offset, sem):
        size = pair[0].shape[0]
        copies = [
            pltpu.make_async_copy(ref, factors_ref.at[buffer, pl.ds(offset, size), pl.ds(0, used)], sem) for ref in pair
        ]
        mine = slots_ref[6] == i

        @pl.when(mine)
        def _():
            copies[0].start()

        @pl.when(jnp.logical_not(mine))
        def _():
            copies[1].start()

        return copies[0]

    def plain(ref, first, size, buffer, offset, sem):
        copy = pltpu.make_async_copy(
            ref.at[pl.ds(first, size), :], factors_ref.at[buffer, pl.ds(offset, size), :], sem
        )
        copy.start()
        return copy

    work = ["sent", "sent", "tokens", "kept", "kept"][0 if sending else 2:5 if keeping else 3]
    place = {"sent": 0, "kept": 0}

    def fetch(i):
        buffer = i % 3
        sem = [factor_sems.at[buffer, j] for j in range(3)]
        if work[i] == "sent":
            place["sent"] += 1
            return [from_either(theirs, place["sent"] - 1, buffer, 0, sem[0])]
        if work[i] == "kept":
            place["kept"] += 1
            return [plain(rows_ref, (place["kept"] - 1) * half, half, buffer, 0, sem[0])]
        copies = []
        if sending:
            copies.append(from_either(their_tokens, 0, buffer, 0, sem[0]))
            copies.append(from_either(their_tokens, 1, buffer, few, sem[1]))
        if keeping:
            copies.append(plain(tokens_ref, 0, extra, buffer, extra, sem[2]))
        return copies

    def product(buffer, first, size):
        return jnp.dot(factors_ref[buffer, first:first + size, :], panels_ref[...], preferred_element_type=F32)

    def product_out(buffer, size):
        row = pl.multiple_of(jnp.where(slots_ref[0] == 1, depth - used, 0), 128)
        return jnp.dot(
            factors_ref[buffer, :size, :used], panels_ref[pl.ds(row, used), :], preferred_element_type=F32
        )

    @pl.when(slots_ref[4] == 1)
    def _():
        first = [placed(s) for s in range(4)]
        for copy in first:
            copy.start()
        coming = [fetch(0), fetch(1)]
        if m and keeping:
            gate_copy = pltpu.make_async_copy(
                gate_ref.at[:, pl.ds(start, tiled(width))], gate_buf, end_sems.at[4])
            gate_copy.start()
        for copy in first:
            copy.wait()
        ends = []

        def finished(source, target):
            copy = pltpu.make_async_copy(source, target, end_sems.at[len(ends)])
            copy.start()
            ends.append(copy)

        done = {"sent": 0, "kept": 0}
        for i, kind in enumerate(work):
            if i + 2 < len(work):
                coming.append(fetch(i + 2))
            for copy in coming[i]:
                copy.wait()
            if kind == "sent":
                stage_ref[done[kind] * half:(done[kind] + 1) * half, :] = product_out(i % 3, half).astype(BF16)
                done[kind] += 1
            elif kind == "kept":
                part = slice(done[kind] * half, (done[kind] + 1) * half)
                slab_ref[:, part] = product(i % 3, 0, half).astype(BF16).T
                done[kind] += 1
            else:
                if sending:
                    stage_ref[count:, :] = product_out(i % 3, extra).astype(BF16)
                    finished(stage_ref, out_ref)
                if keeping:
                    pre = product(i % 3, extra, extra)
                    if m:
                        gate_copy.wait()
                        extra_ref[...] = gated(gate_buf[...], pre).T
                        finished(extra_ref.at[:width, :], last_ref.at[pl.ds(start, width), :])
                    else:
                        extra_ref[...] = pre
                        finished(extra_ref, last_ref.at[:, pl.ds(start, tiled(width))])
        if keeping:
            finished(slab_ref.at[:width, :], grown_ref.at[m, pl.ds(start, width), :])
        for copy in ends:
            copy.wait()


def products(m, start, width, slots, mine, theirs, panels, gate, grown, last, columns, sending, keeping):
    rows, token_growth = mine
    count, depth = rows.shape
    extra = token_growth.shape[0]
    block, wide = panels[0].shape
    args = [*theirs, rows, token_growth, *panels]
    aliases = {}
    if keeping and m:
        args.append(gate)
    if keeping and grown is not None:
        aliases[len(args) + 1] = int(sending)
        args.append(grown)
    if keeping and last is not None:
        aliases[len(args) + 1] = int(sending) + 1
        args.append(last)
    out_shape = []
    if sending:
        out_shape.append(jax.ShapeDtypeStruct((count + extra, wide), BF16))
    if keeping:
        out_shape.append(jax.ShapeDtypeStruct((2, columns, count), BF16))
        out_shape.append(
            jax.ShapeDtypeStruct((columns, extra), BF16) if m else jax.ShapeDtypeStruct((extra, tiled(columns)), F32)
        )
    return pl.pallas_call(
        functools.partial(products_kernel, m, start, width, sending, keeping),
        out_shape=out_shape,
        grid_spec=pltpu.PrefetchScalarGridSpec(
            num_scalar_prefetch=1,
            grid=(1,),
            in_specs=[ANY] * len(args),
            out_specs=[ANY] * len(out_shape),
            scratch_shapes=[
                pltpu.VMEM((depth, wide), BF16),
                pltpu.VMEM((3, count // 2, depth), BF16),
                pltpu.VMEM((count + extra, wide), BF16),
                pltpu.VMEM((wide, count), BF16),
                pltpu.VMEM((wide, extra), BF16) if m else pltpu.VMEM((extra, wide), F32),
                pltpu.VMEM((extra, wide), F32),
                pltpu.SemaphoreType.DMA((4,)),
                pltpu.SemaphoreType.DMA((3, 3)),
                pltpu.SemaphoreType.DMA((5,)),
            ],
        ),
        input_output_aliases=aliases,
        compiler_params=pltpu.CompilerParams(vmem_limit_bytes=VMEM_LIMIT),
        cost_estimate=pl.CostEstimate(flops=3 * (sending + keeping) * (count + extra) * depth * wide, bytes_accessed=0, transcendentals=0),
        name="products",
    )(slots, *args)


def own_kernel(slots_ref, rows_ref, tokens_ref, own_ref, sums_ref, factors_ref, panels_ref, sums_buf, sems):
    block = own_ref.shape[0]

    @pl.when(slots_ref[4] == 0)
    def _():
        copies = own_copies(slots_ref, rows_ref, tokens_ref, own_ref, factors_ref, panels_ref, sems)
        for copy in copies:
            copy.start()
        other = pl.multiple_of((1 - slots_ref[5]) * block, 16)
        panels_ref[pl.ds(other, block), :] = jnp.zeros((block, panels_ref.shape[1]), BF16)
        for copy in copies:
            copy.wait()
        sums_buf[...] = jnp.dot(factors_ref[...], panels_ref[...], preferred_element_type=F32)
        end = pltpu.make_async_copy(sums_buf, sums_ref, sems.at[0])
        end.start()
        end.wait()


def own_copies(slots_ref, rows_ref, tokens_ref, own_ref, factors_ref, panels_ref, sems):
    block, count, depth = own_ref.shape[0], rows_ref.shape[0], factors_ref.shape[1]
    side = pl.multiple_of(slots_ref[5] * depth, 128)
    place = pl.multiple_of(slots_ref[5] * block, 16)
    return [
        pltpu.make_async_copy(own_ref, panels_ref.at[pl.ds(place, block), :], sems.at[0]),
        pltpu.make_async_copy(
            tokens_ref.at[:, pl.ds(side, depth)], factors_ref.at[pl.ds(count, tokens_ref.shape[0]), :], sems.at[1]),
        pltpu.make_async_copy(rows_ref.at[:, pl.ds(side, depth)], factors_ref.at[pl.ds(0, count), :], sems.at[2]),
    ]


def own_product(slots, mine, own):
    rows, token_growth = mine
    total, (block, wide) = rows.shape[0] + token_growth.shape[0], own.shape
    return pl.pallas_call(
        own_kernel,
        out_shape=jax.ShapeDtypeStruct((total, wide), F32),
        grid_spec=pltpu.PrefetchScalarGridSpec(
            num_scalar_prefetch=1,
            grid=(1,),
            in_specs=[ANY] * 3,
            out_specs=ANY,
            scratch_shapes=[
                pltpu.VMEM((total, 2 * block), BF16),
                pltpu.VMEM((2 * block, wide), BF16),
                pltpu.VMEM((total, wide), F32),
                pltpu.SemaphoreType.DMA((3,)),
            ],
        ),
        compiler_params=pltpu.CompilerParams(vmem_limit_bytes=VMEM_LIMIT),
        cost_estimate=pl.CostEstimate(flops=0, bytes_accessed=0, transcendentals=0),
        name="own_product",
    )(slots, rows, token_growth, own)


def finish_kernel(m, start, width, made, slots_ref, *refs):
    refs = list(refs)
    sources = [refs.pop(0) for _ in range(1 if made else 3)]
    got_ref, gate_ref = refs.pop(0), refs.pop(0)
    del refs[:2 if m else 1]
    grown_ref, last_ref = refs.pop(0), refs.pop(0)
    bufs = [refs.pop(0) for _ in range(1 if made else 2)]
    got_buf, gate_buf, slab_ref, extra_ref, sems = refs
    wide = got_ref.shape[1]
    count, extra = slab_ref.shape[1], gate_buf.shape[0]
    half = count // 2

    @pl.when(slots_ref[4] == 0)
    def _():
        if made:
            copies = [pltpu.make_async_copy(sources[0], bufs[0], sems.at[0])]
        else:
            copies = own_copies(slots_ref, *sources, *bufs, sems)
        copies.append(pltpu.make_async_copy(got_ref, got_buf, sems.at[3]))
        if m:
            copies.append(pltpu.make_async_copy(gate_ref.at[:, pl.ds(start, tiled(width))], gate_buf, sems.at[4]))
        for copy in copies:
            copy.start()
        if not made:
            block = sources[2].shape[0]
            other = pl.multiple_of((1 - slots_ref[5]) * block, 16)
            bufs[1][pl.ds(other, block), :] = jnp.zeros((block, wide), BF16)
        for copy in copies:
            copy.wait()

        def product(first, size):
            if made:
                sums = bufs[0][first:first + size, :]
            else:
                sums = jnp.dot(bufs[0][first:first + size, :], bufs[1][...], preferred_element_type=F32)
            return sums + got_buf[first:first + size, :].astype(F32)

        pre = product(count, extra)
        if m:
            extra_ref[...] = gated(gate_buf[...], pre).T
            end = pltpu.make_async_copy(
                extra_ref.at[:width, :], last_ref.at[pl.ds(start, width), :], sems.at[0])
        else:
            extra_ref[...] = pre
            end = pltpu.make_async_copy(extra_ref, last_ref.at[:, pl.ds(start, tiled(width))], sems.at[0])
        end.start()
        for i in range(2):
            slab_ref[:, i * half:(i + 1) * half] = product(i * half, half).astype(BF16).T
        slab = pltpu.make_async_copy(
            slab_ref.at[:width, :], grown_ref.at[m, pl.ds(start, width), :], sems.at[1])
        slab.start()
        end.wait()
        slab.wait()


def finish(m, start, width, slots, mine, own, got, gate, grown, hidden, columns, made=None):
    rows, token_growth = mine
    count, depth = rows.shape
    extra = token_growth.shape[0]
    block, wide = own.shape
    args = [rows, token_growth, own] if made is None else [made]
    args += [got, gate, grown] + ([hidden] if m else [])
    last = len(args)
    if made is None:
        scratch = [pltpu.VMEM((count + extra, 2 * block), BF16), pltpu.VMEM((2 * block, wide), BF16)]
    else:
        scratch = [pltpu.VMEM((count + extra, wide), F32)]
    return pl.pallas_call(
        functools.partial(finish_kernel, m, start, width, made is not None),
        out_shape=(
            jax.ShapeDtypeStruct((2, columns, count), BF16),
            jax.ShapeDtypeStruct((columns, extra), BF16) if m else jax.ShapeDtypeStruct((extra, tiled(columns)), F32),
        ),
        grid_spec=pltpu.PrefetchScalarGridSpec(
            num_scalar_prefetch=1,
            grid=(1,),
            in_specs=[ANY] * len(args),
            out_specs=(ANY, ANY),
            scratch_shapes=scratch + [
                pltpu.VMEM((count + extra, wide), BF16),
                pltpu.VMEM((extra, wide), F32),
                pltpu.VMEM((wide, count), BF16),
                pltpu.VMEM((wide, extra), BF16) if m else pltpu.VMEM((extra, wide), F32),
                pltpu.SemaphoreType.DMA((5,)),
            ],
        ),
        input_output_aliases={last - 1: 0, last: 1} if m else {last: 0, last - 1: 1},
        compiler_params=pltpu.CompilerParams(vmem_limit_bytes=VMEM_LIMIT),
        cost_estimate=pl.CostEstimate(flops=0, bytes_accessed=0, transcendentals=0),
        name="finish",
    )(slots, *args)


def used_depth(depth):
    return tiled(3 * depth // 4)


def fetch_half(rows, parts):
    half, depth = rows.shape[0] // 2, rows.shape[1]
    core = lax.rem(lax.axis_index("tensor"), 2)
    first = jnp.where(lax.axis_index("dp") == 0, depth - used_depth(depth), 0)
    size = -(-half // parts // 16) * 16
    fetched = []
    for start in range(0, half, size):
        part = lax.dynamic_slice(rows, (core * half + start, first), (min(size, half - start), used_depth(depth)))
        column = first + lax.broadcasted_iota(jnp.int32, part.shape, 1)
        part = jnp.where(column // (depth // 4) == lax.axis_index("dp"), jnp.zeros_like(part), part)
        fetched.append(lax.ppermute(after(part, *fetched[-1:]), "dp", TO_INNER))
    return fetched


def line_form(tokens, small_weights, ffn_growth, width_growth):
    columns = ffn_growth.shape[0]
    index = lax.axis_index("dp")
    is_inner = ((index == 1) | (index == 2)).astype(jnp.int32)
    core = lax.rem(lax.axis_index("tensor"), 2)
    slots = jnp.concatenate(
        [jnp.array(SLOTS, jnp.int32)[index], jnp.stack([is_inner, (index == 3).astype(jnp.int32), core])]
    )
    small = [lax.all_gather(small_weights[m], "tensor", axis=0, tiled=True) for m in range(2)]
    fetched = fetch_half(width_growth, 3)
    token_share = token_rows(tokens, width_growth, fetched[0])
    token_share = joined(token_share, swap(token_share, 1), 1)
    token_share = joined(token_share, swap(token_share, 2), 2)
    token_rest = swap(token_share, 4)

    work = [(m, start, width) for m in range(2) for start, width in pieces(columns, WIDTH)]
    own, outer, mate, far, out, received = ({} for _ in range(6))
    grown = gate = hidden = theirs = None

    def panel(chosen, *made, weight=3):
        m = work[chosen[0]][0]
        source = after(small[m], *made) if made else small[m]
        for k, part in zip(chosen, panel_of(source, ffn_growth, [work[k][1:] for k in chosen], weight)):
            own[k] = part

    def send(k, *made):
        sent = after(own[k], *made) if made else own[k]
        with jax.named_scope(f"outer{k}"):
            outer[k] = lax.ppermute(sent, "dp", TO_INNER)
        with jax.named_scope(f"mate{k}"):
            mate[k] = lax.ppermute(sent, "dp", SWAP_INNER)

    def forward(k, *made):
        outer[k] = after(outer[k], *made)
        with jax.named_scope(f"far{k}"):
            far[k] = lax.ppermute(outer[k], "dp", SWAP_INNER)

    def multiply(k, *made, sending=True, keeping=True):
        nonlocal grown, gate, hidden
        m, start, width = work[k]
        panels = [after(own[k], *made), outer[k], mate[k], far[k]]
        last = hidden if m else gate
        made = products(
            m, start, width, slots, mine, theirs, panels, gate, grown, last, columns, sending, keeping
        )
        if sending:
            out[k] = made[0]
            with jax.named_scope(f"sums{k}"):
                received[k] = lax.ppermute(out[k], "dp", TO_OUTER)
        if keeping:
            grown = made[-2]
            if m:
                hidden = made[-1]
            else:
                gate = made[-1]

    def conclude(k, made=None):
        nonlocal grown, gate, hidden
        m, start, width = work[k]
        grown, last = finish(m, start, width, slots, mine, own[k], received[k], gate, grown, hidden, columns, made)
        if m:
            hidden = last
        else:
            gate = last

    panel([0], fetched[1], token_share)
    token_growth = joined(token_share, after(token_rest, own[0]), 4)
    token_half, = fetch_half(token_growth, 1)
    mine = (width_growth, token_growth)
    rows_half = jnp.concatenate(fetched[:2] + [after(fetched[2], own[0])], axis=0)
    send(0)
    panel([1], own[0], token_growth, rows_half)
    forward(0, mate[0], own[1])
    send(1, outer[0])
    panel([2], outer[0], weight=3)
    token_half = after(token_half, own[2])
    theirs = (rows_half, swap(rows_half, 1), token_half, swap(token_half, 1))
    multiply(0, far[0], own[2], outer[1])
    forward(1, out[0])
    send(2, outer[1])
    panel([3], outer[1], out[0], mate[1])
    send(3)
    forward(2, own[3])
    multiply(1, outer[2])
    forward(3, out[1], mate[2])
    panel([4, 5], outer[3], received[0])
    send(4)
    conclude(0)
    multiply(2, own[4], mate[3])
    forward(4, out[2], far[3])
    send(5, outer[4])
    conclude(1)
    multiply(3, outer[4])
    forward(5, out[3], mate[4])
    conclude(2)
    multiply(4, outer[5])
    conclude(3)
    multiply(5, out[4], keeping=False)
    multiply(5, out[5], sending=False)
    last_product = own_product(slots, mine, after(own[5], out[5]))
    conclude(4)
    conclude(5, last_product)
    return jnp.swapaxes(grown, 1, 2), hidden.T


def solution(mesh):
    placed = (P("dp", "tensor"), P(None, ("dp", "tensor"), None), P("tensor", None), P("dp", None))
    return jax.shard_map(
        line_form if mesh.shape["dp"] == 4 else gathered_form,
        mesh=mesh,
        in_specs=placed,
        out_specs=(P(None, "dp", "tensor"), P("dp", "tensor")),
        check_vma=False,
    )
```

```python
import functools

import jax
import jax.numpy as jnp
from jax import lax
from jax.experimental import pallas as pl
from jax.experimental.pallas import tpu as pltpu
from jax.sharding import PartitionSpec as P

BF16, F32 = jnp.bfloat16, jnp.float32
WIDTH = 512
VMEM_LIMIT = 56 * 1024 * 1024
ANY = pl.BlockSpec(memory_space=pl.ANY)


def pieces(extent, width):
    starts = list(range(0, extent, width))
    return [(start, min(width, extent - start)) for start in starts]


def after(array, *made):
    return lax.optimization_barrier((array,) + made)[0]


def token_rows(tokens, width_growth, *fetched):
    nd = lax.axis_size("dp")
    by_rows = lax.all_to_all(tokens, "tensor", 0, 1, tiled=True)
    by_features = lax.all_to_all(by_rows, "dp", 1, 0, tiled=True)
    by_features = after(by_features, *fetched[:1])
    part = jnp.dot(by_features, width_growth, preferred_element_type=F32).astype(BF16)
    parts = lax.all_to_all(part, "dp", 0, 0, tiled=True)
    return jnp.sum(parts.reshape(nd, -1, parts.shape[1]).astype(F32), axis=0).astype(BF16)


def swap(rows, bit):
    return lax.ppermute(rows, "tensor", [(j, j ^ bit) for j in range(lax.axis_size("tensor"))])


def joined(rows, got, bit):
    low = (lax.axis_index("tensor") // bit) % 2 == 0
    return jnp.concatenate([jnp.where(low, rows, got), jnp.where(low, got, rows)], axis=0)


def gathered_form(tokens, small_weights, ffn_growth, width_growth):
    columns = ffn_growth.shape[0]
    small = [lax.all_gather(small_weights[m], "tensor", axis=0, tiled=True) for m in range(2)]
    token_growth = lax.all_gather(token_rows(tokens, width_growth), "tensor", axis=0, tiled=True)
    grown, pre = [], []
    for m in range(2):
        grown_parts, pre_parts = [], []
        for start, width in pieces(columns, WIDTH):
            panel = jnp.einsum(
                "sf,cf->sc", small[m], ffn_growth[start:start + width], preferred_element_type=F32
            ).astype(BF16)
            panels = lax.all_gather(panel, "dp", axis=0, tiled=True)
            grown_parts.append(jnp.dot(width_growth, panels, preferred_element_type=F32).astype(BF16))
            pre_parts.append(jnp.dot(token_growth, panels, preferred_element_type=F32))
        grown.append(jnp.concatenate(grown_parts, axis=1))
        pre.append(jnp.concatenate(pre_parts, axis=1))
    hidden = (jax.nn.silu(pre[0]) * pre[1]).astype(BF16)
    return (jnp.stack(grown), hidden)


SWAP_INNER = [(1, 2), (2, 1)]
TO_INNER = [(0, 1), (3, 2)]
TO_OUTER = [(1, 0), (2, 3)]
SLOTS = [[0, 1, 2, 3], [1, 0, 2, 3], [2, 3, 1, 0], [3, 0, 1, 2]]


def panel_kernel(steps, splits, small_ref, growth_ref, *refs):
    out_refs, acc_ref = refs[:-1], refs[-1]
    step = pl.program_id(0)
    part = lax.dot_general(
        small_ref[...], growth_ref[...], (((1,), (1,)), ((), ())), preferred_element_type=F32
    )

    @pl.when(step == 0)
    def _():
        acc_ref[...] = part

    @pl.when((step > 0) & (step < steps - 1))
    def _():
        acc_ref[...] += part

    @pl.when(step == steps - 1)
    def _():
        total = acc_ref[...] + part
        for (start, width), out_ref in zip(splits, out_refs):
            wide = out_ref.shape[1]
            piece = total[:, start - splits[0][0]:start - splits[0][0] + wide]
            if width < wide:
                column = lax.broadcasted_iota(jnp.int32, piece.shape, 1)
                piece = jnp.where(column < width, piece, 0.0)
            out_ref[...] = piece.astype(BF16)


def tiled(width):
    return -(-width // 128) * 128


def panel_of(small, growth, splits, weight):
    rows, depth = small.shape
    first = splits[0][0]
    wide = tiled(splits[-1][0] + splits[-1][1] - first)
    steps = 7
    deep = depth // steps
    return pl.pallas_call(
        functools.partial(panel_kernel, steps, splits),
        out_shape=[jax.ShapeDtypeStruct((rows, tiled(width)), BF16) for _, width in splits],
        grid=(steps,),
        in_specs=[
            pl.BlockSpec((rows, deep), lambda k: (0, k)),
            pl.BlockSpec((pl.Element(wide, (0, max(0, first + wide - growth.shape[0]))), pl.Element(deep)), lambda k: (first, k * deep)),
        ],
        out_specs=[pl.BlockSpec((rows, tiled(width)), lambda k: (0, 0)) for _, width in splits],
        scratch_shapes=[pltpu.VMEM((rows, wide), F32)],
        compiler_params=pltpu.CompilerParams(vmem_limit_bytes=VMEM_LIMIT),
        cost_estimate=pl.CostEstimate(flops=weight * rows * depth * wide, bytes_accessed=0, transcendentals=0),
        name="panel",
    )(small, growth)


def gated(gate, up):
    return (gate / (1.0 + jnp.exp(-gate)) * up).astype(BF16)


def products_kernel(m, start, width, sending, keeping, slots_ref, *refs):
    refs = list(refs)
    theirs, their_tokens = (refs.pop(0), refs.pop(0)), (refs.pop(0), refs.pop(0))
    rows_ref, tokens_ref = refs.pop(0), refs.pop(0)
    sources = [refs.pop(0) for _ in range(4)]
    if keeping:
        if m:
            gate_ref = refs.pop(0)
        if m or start:
            refs.pop(0)
        if start:
            refs.pop(0)
    if sending:
        out_ref = refs.pop(0)
    if keeping:
        grown_ref, last_ref = refs.pop(0), refs.pop(0)
    panels_ref, factors_ref, stage_ref, slab_ref, extra_ref, gate_buf, sems, factor_sems, end_sems = refs
    block = sources[0].shape[0]
    count = rows_ref.shape[0]
    extra = tokens_ref.shape[0]
    half, few = count // 2, extra // 2
    depth, used = panels_ref.shape[0], their_tokens[0].shape[1]

    def placed(s):
        row = pl.multiple_of(slots_ref[s] * block, 16)
        return pltpu.make_async_copy(sources[s], panels_ref.at[pl.ds(row, block), :], sems.at[s])

    def from_either(pair, i, buffer, offset, sem):
        size = pair[0].shape[0]
        copies = [
            pltpu.make_async_copy(ref, factors_ref.at[buffer, pl.ds(offset, size), pl.ds(0, used)], sem) for ref in pair
        ]
        mine = slots_ref[6] == i

        @pl.when(mine)
        def _():
            copies[0].start()

        @pl.when(jnp.logical_not(mine))
        def _():
            copies[1].start()

        return copies[0]

    def plain(ref, first, size, buffer, offset, sem):
        copy = pltpu.make_async_copy(
            ref.at[pl.ds(first, size), :], factors_ref.at[buffer, pl.ds(offset, size), :], sem
        )
        copy.start()
        return copy

    work = ["sent", "sent", "tokens", "kept", "kept"][0 if sending else 2:5 if keeping else 3]
    place = {"sent": 0, "kept": 0}

    def fetch(i):
        buffer = i % 3
        sem = [factor_sems.at[buffer, j] for j in range(3)]
        if work[i] == "sent":
            place["sent"] += 1
            return [from_either(theirs, place["sent"] - 1, buffer, 0, sem[0])]
        if work[i] == "kept":
            place["kept"] += 1
            return [plain(rows_ref, (place["kept"] - 1) * half, half, buffer, 0, sem[0])]
        copies = []
        if sending:
            copies.append(from_either(their_tokens, 0, buffer, 0, sem[0]))
            copies.append(from_either(their_tokens, 1, buffer, few, sem[1]))
        if keeping:
            copies.append(plain(tokens_ref, 0, extra, buffer, extra, sem[2]))
        return copies

    def product(buffer, first, size):
        return jnp.dot(factors_ref[buffer, first:first + size, :], panels_ref[...], preferred_element_type=F32)

    def product_out(buffer, size):
        row = pl.multiple_of(jnp.where(slots_ref[0] == 1, depth - used, 0), 128)
        return jnp.dot(
            factors_ref[buffer, :size, :used], panels_ref[pl.ds(row, used), :], preferred_element_type=F32
        )

    @pl.when(slots_ref[4] == 1)
    def _():
        first = [placed(s) for s in range(4)]
        for copy in first:
            copy.start()
        coming = [fetch(0), fetch(1)]
        if m and keeping:
            gate_copy = pltpu.make_async_copy(
                gate_ref.at[:, pl.ds(start, tiled(width))], gate_buf, end_sems.at[4])
            gate_copy.start()
        for copy in first:
            copy.wait()
        ends = []

        def finished(source, target):
            copy = pltpu.make_async_copy(source, target, end_sems.at[len(ends)])
            copy.start()
            ends.append(copy)

        done = {"sent": 0, "kept": 0}
        for i, kind in enumerate(work):
            if i + 2 < len(work):
                coming.append(fetch(i + 2))
            for copy in coming[i]:
                copy.wait()
            if kind == "sent":
                stage_ref[done[kind] * half:(done[kind] + 1) * half, :] = product_out(i % 3, half).astype(BF16)
                done[kind] += 1
            elif kind == "kept":
                part = slice(done[kind] * half, (done[kind] + 1) * half)
                slab_ref[:, part] = product(i % 3, 0, half).astype(BF16).T
                done[kind] += 1
            else:
                if sending:
                    stage_ref[count:, :] = product_out(i % 3, extra).astype(BF16)
                    finished(stage_ref, out_ref)
                if keeping:
                    pre = product(i % 3, extra, extra)
                    if m:
                        gate_copy.wait()
                        extra_ref[...] = gated(gate_buf[...], pre).T
                        finished(extra_ref.at[:width, :], last_ref.at[pl.ds(start, width), :])
                    else:
                        extra_ref[...] = pre
                        finished(extra_ref, last_ref.at[:, pl.ds(start, tiled(width))])
        if keeping:
            finished(slab_ref.at[:width, :], grown_ref.at[m, pl.ds(start, width), :])
        for copy in ends:
            copy.wait()


def products(m, start, width, slots, mine, theirs, panels, gate, grown, last, columns, sending, keeping):
    rows, token_growth = mine
    count, depth = rows.shape
    extra = token_growth.shape[0]
    block, wide = panels[0].shape
    args = [*theirs, rows, token_growth, *panels]
    aliases = {}
    if keeping and m:
        args.append(gate)
    if keeping and grown is not None:
        aliases[len(args) + 1] = int(sending)
        args.append(grown)
    if keeping and last is not None:
        aliases[len(args) + 1] = int(sending) + 1
        args.append(last)
    out_shape = []
    if sending:
        out_shape.append(jax.ShapeDtypeStruct((count + extra, wide), BF16))
    if keeping:
        out_shape.append(jax.ShapeDtypeStruct((2, columns, count), BF16))
        out_shape.append(
            jax.ShapeDtypeStruct((columns, extra), BF16) if m else jax.ShapeDtypeStruct((extra, tiled(columns)), F32)
        )
    return pl.pallas_call(
        functools.partial(products_kernel, m, start, width, sending, keeping),
        out_shape=out_shape,
        grid_spec=pltpu.PrefetchScalarGridSpec(
            num_scalar_prefetch=1,
            grid=(1,),
            in_specs=[ANY] * len(args),
            out_specs=[ANY] * len(out_shape),
            scratch_shapes=[
                pltpu.VMEM((depth, wide), BF16),
                pltpu.VMEM((3, count // 2, depth), BF16),
                pltpu.VMEM((count + extra, wide), BF16),
                pltpu.VMEM((wide, count), BF16),
                pltpu.VMEM((wide, extra), BF16) if m else pltpu.VMEM((extra, wide), F32),
                pltpu.VMEM((extra, wide), F32),
                pltpu.SemaphoreType.DMA((4,)),
                pltpu.SemaphoreType.DMA((3, 3)),
                pltpu.SemaphoreType.DMA((5,)),
            ],
        ),
        input_output_aliases=aliases,
        compiler_params=pltpu.CompilerParams(vmem_limit_bytes=VMEM_LIMIT),
        cost_estimate=pl.CostEstimate(flops=(6 if sending and keeping else 6) * (count + extra) * depth * wide, bytes_accessed=0, transcendentals=0),
        name="products",
    )(slots, *args)


def own_kernel(slots_ref, rows_ref, tokens_ref, own_ref, sums_ref, factors_ref, panels_ref, sums_buf, sems):
    block = own_ref.shape[0]

    @pl.when(slots_ref[4] == 0)
    def _():
        copies = own_copies(slots_ref, rows_ref, tokens_ref, own_ref, factors_ref, panels_ref, sems)
        for copy in copies:
            copy.start()
        other = pl.multiple_of((1 - slots_ref[5]) * block, 16)
        panels_ref[pl.ds(other, block), :] = jnp.zeros((block, panels_ref.shape[1]), BF16)
        for copy in copies:
            copy.wait()
        sums_buf[...] = jnp.dot(factors_ref[...], panels_ref[...], preferred_element_type=F32)
        end = pltpu.make_async_copy(sums_buf, sums_ref, sems.at[0])
        end.start()
        end.wait()


def own_copies(slots_ref, rows_ref, tokens_ref, own_ref, factors_ref, panels_ref, sems):
    block, count, depth = own_ref.shape[0], rows_ref.shape[0], factors_ref.shape[1]
    side = pl.multiple_of(slots_ref[5] * depth, 128)
    place = pl.multiple_of(slots_ref[5] * block, 16)
    return [
        pltpu.make_async_copy(own_ref, panels_ref.at[pl.ds(place, block), :], sems.at[0]),
        pltpu.make_async_copy(
            tokens_ref.at[:, pl.ds(side, depth)], factors_ref.at[pl.ds(count, tokens_ref.shape[0]), :], sems.at[1]),
        pltpu.make_async_copy(rows_ref.at[:, pl.ds(side, depth)], factors_ref.at[pl.ds(0, count), :], sems.at[2]),
    ]


def own_product(slots, mine, own):
    rows, token_growth = mine
    total, (block, wide) = rows.shape[0] + token_growth.shape[0], own.shape
    return pl.pallas_call(
        own_kernel,
        out_shape=jax.ShapeDtypeStruct((total, wide), F32),
        grid_spec=pltpu.PrefetchScalarGridSpec(
            num_scalar_prefetch=1,
            grid=(1,),
            in_specs=[ANY] * 3,
            out_specs=ANY,
            scratch_shapes=[
                pltpu.VMEM((total, 2 * block), BF16),
                pltpu.VMEM((2 * block, wide), BF16),
                pltpu.VMEM((total, wide), F32),
                pltpu.SemaphoreType.DMA((3,)),
            ],
        ),
        compiler_params=pltpu.CompilerParams(vmem_limit_bytes=VMEM_LIMIT),
        cost_estimate=pl.CostEstimate(flops=0, bytes_accessed=0, transcendentals=0),
        name="own_product",
    )(slots, rows, token_growth, own)


def finish_kernel(m, start, width, made, slots_ref, *refs):
    refs = list(refs)
    sources = [refs.pop(0) for _ in range(1 if made else 3)]
    got_ref, gate_ref = refs.pop(0), refs.pop(0)
    del refs[:2 if m else 1]
    grown_ref, last_ref = refs.pop(0), refs.pop(0)
    bufs = [refs.pop(0) for _ in range(1 if made else 2)]
    got_buf, gate_buf, slab_ref, extra_ref, sems = refs
    wide = got_ref.shape[1]
    count, extra = slab_ref.shape[1], gate_buf.shape[0]
    half = count // 2

    @pl.when(slots_ref[4] == 0)
    def _():
        if made:
            copies = [pltpu.make_async_copy(sources[0], bufs[0], sems.at[0])]
        else:
            copies = own_copies(slots_ref, *sources, *bufs, sems)
        copies.append(pltpu.make_async_copy(got_ref, got_buf, sems.at[3]))
        if m:
            copies.append(pltpu.make_async_copy(gate_ref.at[:, pl.ds(start, tiled(width))], gate_buf, sems.at[4]))
        for copy in copies:
            copy.start()
        if not made:
            block = sources[2].shape[0]
            other = pl.multiple_of((1 - slots_ref[5]) * block, 16)
            bufs[1][pl.ds(other, block), :] = jnp.zeros((block, wide), BF16)
        for copy in copies:
            copy.wait()

        def product(first, size):
            if made:
                sums = bufs[0][first:first + size, :]
            else:
                sums = jnp.dot(bufs[0][first:first + size, :], bufs[1][...], preferred_element_type=F32)
            return sums + got_buf[first:first + size, :].astype(F32)

        pre = product(count, extra)
        if m:
            extra_ref[...] = gated(gate_buf[...], pre).T
            end = pltpu.make_async_copy(
                extra_ref.at[:width, :], last_ref.at[pl.ds(start, width), :], sems.at[0])
        else:
            extra_ref[...] = pre
            end = pltpu.make_async_copy(extra_ref, last_ref.at[:, pl.ds(start, tiled(width))], sems.at[0])
        end.start()
        for i in range(2):
            slab_ref[:, i * half:(i + 1) * half] = product(i * half, half).astype(BF16).T
        slab = pltpu.make_async_copy(
            slab_ref.at[:width, :], grown_ref.at[m, pl.ds(start, width), :], sems.at[1])
        slab.start()
        end.wait()
        slab.wait()


def finish(m, start, width, slots, mine, own, got, gate, grown, hidden, columns, made=None):
    rows, token_growth = mine
    count, depth = rows.shape
    extra = token_growth.shape[0]
    block, wide = own.shape
    args = [rows, token_growth, own] if made is None else [made]
    args += [got, gate, grown] + ([hidden] if m else [])
    last = len(args)
    if made is None:
        scratch = [pltpu.VMEM((count + extra, 2 * block), BF16), pltpu.VMEM((2 * block, wide), BF16)]
    else:
        scratch = [pltpu.VMEM((count + extra, wide), F32)]
    return pl.pallas_call(
        functools.partial(finish_kernel, m, start, width, made is not None),
        out_shape=(
            jax.ShapeDtypeStruct((2, columns, count), BF16),
            jax.ShapeDtypeStruct((columns, extra), BF16) if m else jax.ShapeDtypeStruct((extra, tiled(columns)), F32),
        ),
        grid_spec=pltpu.PrefetchScalarGridSpec(
            num_scalar_prefetch=1,
            grid=(1,),
            in_specs=[ANY] * len(args),
            out_specs=(ANY, ANY),
            scratch_shapes=scratch + [
                pltpu.VMEM((count + extra, wide), BF16),
                pltpu.VMEM((extra, wide), F32),
                pltpu.VMEM((wide, count), BF16),
                pltpu.VMEM((wide, extra), BF16) if m else pltpu.VMEM((extra, wide), F32),
                pltpu.SemaphoreType.DMA((5,)),
            ],
        ),
        input_output_aliases={last - 1: 0, last: 1} if m else {last: 0, last - 1: 1},
        compiler_params=pltpu.CompilerParams(vmem_limit_bytes=VMEM_LIMIT),
        cost_estimate=pl.CostEstimate(flops=0, bytes_accessed=0, transcendentals=0),
        name="finish",
    )(slots, *args)


def used_depth(depth):
    return tiled(3 * depth // 4)


def fetch_half(rows, parts):
    half, depth = rows.shape[0] // 2, rows.shape[1]
    core = lax.rem(lax.axis_index("tensor"), 2)
    first = jnp.where(lax.axis_index("dp") == 0, depth - used_depth(depth), 0)
    size = -(-half // parts // 16) * 16
    fetched = []
    for start in range(0, half, size):
        part = lax.dynamic_slice(rows, (core * half + start, first), (min(size, half - start), used_depth(depth)))
        column = first + lax.broadcasted_iota(jnp.int32, part.shape, 1)
        part = jnp.where(column // (depth // 4) == lax.axis_index("dp"), jnp.zeros_like(part), part)
        fetched.append(lax.ppermute(after(part, *fetched[-1:]), "dp", TO_INNER))
    return fetched


def line_form(tokens, small_weights, ffn_growth, width_growth):
    columns = ffn_growth.shape[0]
    index = lax.axis_index("dp")
    is_inner = ((index == 1) | (index == 2)).astype(jnp.int32)
    core = lax.rem(lax.axis_index("tensor"), 2)
    slots = jnp.concatenate(
        [jnp.array(SLOTS, jnp.int32)[index], jnp.stack([is_inner, (index == 3).astype(jnp.int32), core])]
    )
    small = [lax.all_gather(small_weights[m], "tensor", axis=0, tiled=True) for m in range(2)]
    fetched = fetch_half(width_growth, 3)
    token_share = token_rows(tokens, width_growth, fetched[0])
    token_share = joined(token_share, swap(token_share, 1), 1)
    token_share = joined(token_share, swap(token_share, 2), 2)
    token_rest = swap(token_share, 4)

    work = [(m, start, width) for m in range(2) for start, width in pieces(columns, WIDTH)]
    own, outer, mate, far, out, received = ({} for _ in range(6))
    grown = gate = hidden = theirs = None

    def panel(chosen, *made, weight=3):
        m = work[chosen[0]][0]
        source = after(small[m], *made) if made else small[m]
        for k, part in zip(chosen, panel_of(source, ffn_growth, [work[k][1:] for k in chosen], weight)):
            own[k] = part

    def send(k, *made):
        sent = after(own[k], *made) if made else own[k]
        with jax.named_scope(f"outer{k}"):
            outer[k] = lax.ppermute(sent, "dp", TO_INNER)
        with jax.named_scope(f"mate{k}"):
            mate[k] = lax.ppermute(sent, "dp", SWAP_INNER)

    def forward(k, *made):
        outer[k] = after(outer[k], *made)
        with jax.named_scope(f"far{k}"):
            far[k] = lax.ppermute(outer[k], "dp", SWAP_INNER)

    def multiply(k, *made, sending=True, keeping=True):
        nonlocal grown, gate, hidden
        m, start, width = work[k]
        panels = [after(own[k], *made), outer[k], mate[k], far[k]]
        last = hidden if m else gate
        made = products(
            m, start, width, slots, mine, theirs, panels, gate, grown, last, columns, sending, keeping
        )
        if sending:
            out[k] = made[0]
            with jax.named_scope(f"sums{k}"):
                received[k] = lax.ppermute(out[k], "dp", TO_OUTER)
        if keeping:
            grown = made[-2]
            if m:
                hidden = made[-1]
            else:
                gate = made[-1]

    def conclude(k, made=None):
        nonlocal grown, gate, hidden
        m, start, width = work[k]
        grown, last = finish(m, start, width, slots, mine, own[k], received[k], gate, grown, hidden, columns, made)
        if m:
            hidden = last
        else:
            gate = last

    panel([0], fetched[1], token_share)
    token_growth = joined(token_share, after(token_rest, own[0]), 4)
    token_half, = fetch_half(token_growth, 1)
    mine = (width_growth, token_growth)
    rows_half = jnp.concatenate(fetched[:2] + [after(fetched[2], own[0])], axis=0)
    send(0)
    panel([1], own[0], token_growth, rows_half)
    forward(0, mate[0], own[1])
    send(1, outer[0])
    panel([2], outer[0], weight=3)
    token_half = after(token_half, own[2])
    theirs = (rows_half, swap(rows_half, 1), token_half, swap(token_half, 1))
    multiply(0, far[0], own[2], outer[1])
    forward(1, out[0])
    send(2, outer[1])
    panel([3], outer[1], out[0], mate[1])
    send(3)
    forward(2, own[3])
    multiply(1, outer[2])
    forward(3, out[1], mate[2])
    panel([4, 5], outer[3], received[0])
    send(4)
    conclude(0)
    multiply(2, own[4], mate[3])
    forward(4, out[2], far[3])
    send(5, outer[4])
    conclude(1)
    multiply(3, outer[4], keeping=False)
    forward(5, out[3], mate[4])
    conclude(2)
    multiply(4, outer[5], keeping=False)
    multiply(3, out[4], sending=False)
    multiply(5, own[3], received[3], keeping=False)
    last_product = own_product(slots, mine, after(own[5], out[5]))
    conclude(3)
    multiply(4, out[5], sending=False)
    multiply(5, out[5], sending=False)
    conclude(4)
    conclude(5, last_product)
    return jnp.swapaxes(grown, 1, 2), hidden.T


def solution(mesh):
    placed = (P("dp", "tensor"), P(None, ("dp", "tensor"), None), P("tensor", None), P("dp", None))
    return jax.shard_map(
        line_form if mesh.shape["dp"] == 4 else gathered_form,
        mesh=mesh,
        in_specs=placed,
        out_specs=(P(None, "dp", "tensor"), P("dp", "tensor")),
        check_vma=False,
    )
```
